128 devices in a mesh: grp: 8 (over z_hi, y), dev: 16 (over x, z_lo, core).
Axes of the slice: x: 4, y: 4, z: 4 (z_hi: 2, z_lo: 2; z = z_hi * 2 + z_lo), core: 2. Of those that a mesh axis runs over, the one named last changes fastest.
Arguments:
- gas_velocity: float32 [8, 3, 128, 128, 128], P('grp', None, 'dev'), may hold values from -6 to 6
- parcel_velocity: float32 [8, 3, 64, 16384], P('grp', None, None, 'dev'), may hold values from -6 to 6
- parcel_cell: int32 [8, 64, 16384], P('grp', None, 'dev'), may hold values from 0 to 127
- block_fill: int32 [8, 16384], P('grp', 'dev'), may hold values from 0 to 64
- relax_rate: float32 [8, 64, 16384], P('grp', None, 'dev'), may hold values from 0.1 to 10
- parcel_mass: float32 [8, 64, 16384], P('grp', None, 'dev'), may hold values from 0.1 to 1
- sample_blocks: bfloat16 [5632, 16, 256], P(('grp', 'dev')), may hold values from -6 to 6
- learner_ids: int32 [5632], P(('grp', 'dev')), may hold values from 0 to 47, as said below
- master_weights: float32 [10240, 128], P('dev'), may hold values from -2 to 2
- first_moment: float32 [10240, 128], P('dev'), may hold values from -6 to 6
- second_moment: float32 [10240, 128], P('dev'), may hold values from 1 to 30
Outputs:
- gas_out: float32 [8, 3, 128, 128, 128], P('grp', None, 'dev')
- parcel_out: float32 [8, 3, 64, 16384], P('grp', None, None, 'dev')
- master_out: float32 [10240, 128], P('dev')
- first_out: float32 [10240, 128], P('dev')
- second_out: float32 [10240, 128], P('dev')
The draws below stay inside these ranges and needn't reach their ends.
Inputs may be any that keep to these rules, and one draw needn't show every extreme that they name: `learner_ids`: each device's 44 blocks go to 44 different learners; every learner receives at least one block and at most 128, and some learner receives exactly 128.
All inputs are finite; a program needn't handle non-finite values.
Results may differ from the reference program's by a relative error of at most 0.0004.
The reference program's roundings to bfloat16 on the way count: a program that leaves them out, or rounds other values in their place, can miss the bound.
Values may be sent and summed in bfloat16 or wider, within the bound.
A program may use at most 128 MiB of HBM per device.

```python
import math
import jax
import jax.numpy as jnp
from jax import lax

CY = 128
CZ = 128
CB = 128
PB = 64
SUB = 2
S = 16
F_IN = 128
HID = 1024
F_OUT = 128
SIMG = 5
LEARN = 48
NB = 44
SENDERS = 128
BLOCKS = 5632
MOST = 128
NX = 128
GBLK = 16384
PROWS = 10240
N_GRP = 8


def draw_learner_ids(key, part):
    key = jax.random.fold_in(key, 11)
    rest_count = LEARN - 1
    rest_blocks = BLOCKS - MOST
    base_load = rest_blocks // rest_count
    extra_blocks = rest_blocks % rest_count
    order = jnp.arange(rest_count, dtype=jnp.int32)
    loads = base_load + (order < extra_blocks).astype(jnp.int32)
    pair_key, perm_key = jax.random.split(key)
    pair_shift = jax.random.randint(pair_key, (rest_count // 2 + 1,), 0, base_load // 16 + 1, dtype=jnp.int32)
    partner = order // 2
    shifted = pair_shift[partner] * jnp.where(order % 2 == 0, 1, -1).astype(jnp.int32)
    shifted = jnp.where(2 * partner + 1 < rest_count, shifted, 0)
    loads = loads + shifted
    all_loads = jnp.concatenate([jnp.full((1,), MOST, jnp.int32), loads])
    placed = jax.random.permutation(perm_key, LEARN)
    learner_loads = jnp.zeros((LEARN,), jnp.int32).at[placed].set(all_loads)
    bounds = jnp.cumsum(learner_loads)
    entries = jnp.arange(BLOCKS, dtype=jnp.int32)
    owner = jnp.searchsorted(bounds, entries, side='right').astype(jnp.int32)
    return owner.reshape(NB, SENDERS).T.reshape(BLOCKS)


def draw_master_weights(key, part):
    key = jax.random.fold_in(key, 23)
    position = jnp.arange(PROWS * CB, dtype=jnp.int32).reshape(PROWS, CB)
    scale_table = jnp.where(position < F_IN * HID, F_IN ** (-0.5), HID ** (-0.5)).astype(jnp.float32)
    base_values = jnp.clip(jax.random.normal(key, (PROWS, CB), jnp.float32), -6.0, 6.0)
    return base_values * scale_table


def touch_ends(drawn, stream_key, low, top_value):
    extent = drawn.shape
    spot = [jax.random.randint(jax.random.fold_in(stream_key, axis), (), 0, extent[axis]) for axis in range(len(extent))]
    drawn = drawn.at[tuple(spot)].set(low)
    longest = extent.index(max(extent))
    spot[longest] = (spot[longest] + 1) % extent[longest]
    return drawn.at[tuple(spot)].set(top_value)


def level_of(rng, shape, cuts, low, largest):
    factor_of = 1.0
    for axis_at, shards_of in cuts:
        steps = jax.random.uniform(jax.random.fold_in(jax.random.fold_in(rng, 6), axis_at), (shards_of,), jnp.float32, low / len(cuts), largest / len(cuts))
        factor_of = factor_of * jnp.repeat(jnp.exp(steps), shape[axis_at] // shards_of).reshape((-1,) + (1,) * (len(shape) - 1 - axis_at))
    return factor_of


def scatter_about(rng, shape, spread, reach, cuts=(), held_as=jnp.bfloat16):
    loudness = level_of(rng, shape, cuts, -0.22, 0.18) if cuts else 1.0
    values = jax.random.normal(rng, shape, jnp.float32) * spread * loudness
    return jnp.minimum(jnp.maximum(values, -reach), reach).astype(held_as)


def setup_inputs(seed: int = 0) -> dict:
    arg_keys = jax.random.split(jax.random.key(seed), 12)
    gas_velocity = scatter_about(arg_keys[0], (N_GRP, 3, NX, CY, CZ), 1.0, 6.0, ((0, 8), (2, 16)), jnp.float32)
    parcel_velocity = scatter_about(arg_keys[1], (N_GRP, 3, PB, GBLK), 1.0, 6.0, ((0, 8), (3, 16)), jnp.float32)
    parcel_cell = touch_ends(jax.random.randint(arg_keys[2], (N_GRP, PB, GBLK), 0, CB), jax.random.fold_in(arg_keys[2], 1), 0, CB - 1).astype(jnp.int32)
    block_fill = touch_ends(jax.random.randint(arg_keys[3], (N_GRP, GBLK), 0, PB + 1), jax.random.fold_in(arg_keys[3], 1), 0, PB).astype(jnp.int32)
    relax_rate = jnp.clip(jnp.exp(math.log(10.0) - 4.6051702 * jax.random.uniform(arg_keys[4], (N_GRP, PB, GBLK), jnp.float32) ** level_of(arg_keys[4], (N_GRP, PB, GBLK), ((0, 8), (2, 16)), -0.2, 0.2)), 0.1, 10.0)
    parcel_mass = jnp.clip(jnp.exp(math.log(1.0) - 2.3025851 * jax.random.uniform(arg_keys[5], (N_GRP, PB, GBLK), jnp.float32) ** level_of(arg_keys[5], (N_GRP, PB, GBLK), ((0, 8), (2, 16)), -0.2, 0.2)), 0.1, 1.0)
    sample_blocks = scatter_about(arg_keys[6], (BLOCKS, S, F_IN + F_OUT), 1.0, 6.0, ((0, 128),))
    learner_ids = draw_learner_ids(jax.random.fold_in(arg_keys[11], 71), 0)
    master_weights = draw_master_weights(jax.random.fold_in(arg_keys[11], 71), 0)
    first_moment = scatter_about(arg_keys[9], (PROWS, CB), 1.0, 6.0, ((0, 16),), jnp.float32)
    second_moment = jnp.clip(jnp.exp(math.log(30.0) - 3.4011974 * jax.random.uniform(arg_keys[10], (PROWS, CB), jnp.float32) ** level_of(arg_keys[10], (PROWS, CB), ((0, 16),), -0.2, 0.2)), 1.0, 30.0)
    return {"gas_velocity": gas_velocity, "parcel_velocity": parcel_velocity, "parcel_cell": parcel_cell, "block_fill": block_fill, "relax_rate": relax_rate, "parcel_mass": parcel_mass, "sample_blocks": sample_blocks, "learner_ids": learner_ids, "master_weights": master_weights, "first_moment": first_moment, "second_moment": second_moment}


KAPPA = 0.15
BETA_ONE = 0.9
BETA_TWO = 0.95
ADAM_EPS = 1e-08
LEARN_RATE = 0.001
ADAM_STEP = 10

def learner_group_flags(group_numbers, group_total, learner_groups):
    half_mark = group_numbers == group_total // 2
    quarter_mark = (group_numbers == group_total // 4) & (learner_groups >= 3)
    return (group_numbers == 0) | half_mark | quarter_mark

def walls_sum(gas_field):
    padded = jnp.pad(gas_field, [(0, 0), (0, 0), (0, 0), (1, 1), (1, 1)])
    return padded[:, :, :, 2:, 1:-1] + padded[:, :, :, :-2, 1:-1] + padded[:, :, :, 1:-1, 2:] + padded[:, :, :, 1:-1, :-2]

def diffuse(gas_field, lower_side, upper_side):
    return gas_field + KAPPA * (lower_side + upper_side + walls_sum(gas_field) - 6.0 * gas_field)

def silu_slope(argument):
    sigmoid_value = jax.nn.sigmoid(argument)
    return sigmoid_value * (1.0 + argument * (1.0 - sigmoid_value))

def contract_rows(left_side, right_side):
    return lax.dot_general(left_side, right_side, (((0,), (0,)), ((), ())), preferred_element_type=jnp.float32)

def contract_columns(left_side, right_side):
    return lax.dot_general(left_side, right_side, (((1,), (1,)), ((), ())), preferred_element_type=jnp.float32)

def model_grads(full_weights, features, targets, row_scale):
    flattened = full_weights.reshape(-1)
    first_end = F_IN * HID
    second_end = first_end + HID * HID
    w_first = flattened[:first_end].reshape(F_IN, HID)
    w_second = flattened[first_end:second_end].reshape(HID, HID)
    w_third = flattened[second_end:].reshape(HID, F_OUT)
    pre_first = jnp.dot(features, w_first, preferred_element_type=jnp.float32)
    act_first = jax.nn.silu(pre_first).astype(jnp.bfloat16)
    pre_second = jnp.dot(act_first, w_second, preferred_element_type=jnp.float32)
    act_second = jax.nn.silu(pre_second).astype(jnp.bfloat16)
    predicted = jnp.dot(act_second, w_third, preferred_element_type=jnp.float32)
    error_scaled = ((predicted - targets.astype(jnp.float32)) * row_scale[:, None]).astype(jnp.bfloat16)
    grad_third = contract_rows(act_second, error_scaled)
    back_second = (contract_columns(error_scaled, w_third) * silu_slope(pre_second)).astype(jnp.bfloat16)
    grad_second = contract_rows(act_first, back_second)
    back_first = (contract_columns(back_second, w_second) * silu_slope(pre_first)).astype(jnp.bfloat16)
    grad_first = contract_rows(features, back_first)
    joined = jnp.concatenate([grad_first.reshape(-1), grad_second.reshape(-1), grad_third.reshape(-1)])
    return joined.reshape(full_weights.shape[0], full_weights.shape[1])

def adam_update(weights, moment_one, moment_two, gradient):
    first_new = BETA_ONE * moment_one + (1.0 - BETA_ONE) * gradient
    second_new = BETA_TWO * moment_two + (1.0 - BETA_TWO) * gradient * gradient
    first_hat = first_new / (1.0 - BETA_ONE ** ADAM_STEP)
    second_hat = second_new / (1.0 - BETA_TWO ** ADAM_STEP)
    updated = weights - LEARN_RATE * first_hat / (jnp.sqrt(second_hat) + ADAM_EPS)
    return (updated, first_new, second_new)

def reference(gas_velocity, parcel_velocity, parcel_cell, block_fill, relax_rate, parcel_mass, sample_blocks, learner_ids, master_weights, first_moment, second_moment):
    cell_count = NX * CY * CZ
    block_count = cell_count // CB
    lower_side = jnp.roll(gas_velocity, 1, axis=2)
    upper_side = jnp.roll(gas_velocity, -1, axis=2)
    smoothed = (0.5 * gas_velocity + 0.25 * (lower_side + upper_side)).reshape(N_GRP, 3, cell_count)
    offsets = jnp.arange(block_count, dtype=jnp.int32) * CB
    cell_index = (offsets[None, None, :] + parcel_cell.astype(jnp.int32)).reshape(N_GRP, 1, PB * block_count)
    wide_index = jnp.broadcast_to(cell_index, (N_GRP, 3, PB * block_count))
    gas_at = jnp.take_along_axis(smoothed, wide_index, axis=2).reshape(N_GRP, 3, PB, block_count)
    live_slots = jnp.arange(PB, dtype=jnp.int32)[None, :, None] < block_fill[:, None, :]
    rate_column = relax_rate[:, None]
    relaxed = (parcel_velocity + rate_column * gas_at) / (1.0 + rate_column)
    moved_velocity = jnp.where(live_slots[:, None], relaxed, parcel_velocity)
    handed = jnp.where(live_slots[:, None], parcel_mass[:, None] * (parcel_velocity - relaxed), 0.0)

    def deposit_group(index_row, values):
        return jnp.zeros((3, cell_count), jnp.float32).at[:, index_row].add(values)
    deposited = jax.vmap(deposit_group)(cell_index.reshape(N_GRP, PB * block_count), handed.reshape(N_GRP, 3, PB * block_count))
    deposited = deposited.reshape(gas_velocity.shape)
    source = 0.5 * deposited + 0.25 * (jnp.roll(deposited, 1, axis=2) + jnp.roll(deposited, -1, axis=2))
    gas_field = gas_velocity
    for substep in range(SUB):
        if substep > 0:
            lower_side = jnp.roll(gas_field, 1, axis=2)
            upper_side = jnp.roll(gas_field, -1, axis=2)
        gas_field = diffuse(gas_field, lower_side, upper_side)
        if substep == 0:
            gas_field = gas_field + source
    group_numbers = jnp.arange(N_GRP, dtype=jnp.int32)
    in_evolution = jnp.logical_not(learner_group_flags(group_numbers, N_GRP, N_GRP - SIMG))
    gas_out = jnp.where(in_evolution[:, None, None, None, None], gas_field, gas_velocity)
    parcel_out = jnp.where(in_evolution[:, None, None, None], moved_velocity, parcel_velocity)
    learners = jnp.arange(LEARN, dtype=jnp.int32)
    member = (learner_ids[:, None] == learners[None, :]).astype(jnp.float32)
    counts = member.sum(axis=0)
    block_scale = (member / counts[None, :]).sum(axis=1)
    row_scale = jnp.repeat(block_scale, S)
    features = sample_blocks[:, :, :F_IN].reshape(BLOCKS * S, F_IN)
    targets = sample_blocks[:, :, F_IN:].reshape(BLOCKS * S, F_OUT)
    full_weights = master_weights.astype(jnp.bfloat16)
    gradient = model_grads(full_weights, features, targets, row_scale)
    master_out, first_out, second_out = adam_update(master_weights, first_moment, second_moment, gradient)
    return (gas_out, parcel_out, master_out, first_out, second_out)
```

```python
import functools

import jax
import jax.numpy as jnp
from jax import lax
from jax.experimental import pallas as pl
from jax.experimental.pallas import tpu as pltpu
from jax.sharding import PartitionSpec as P

MESH = pl.DeviceIdType.MESH
F32 = jnp.float32
BF16 = jnp.bfloat16

KAPPA = 0.15
BETA_ONE = 0.9
BETA_TWO = 0.95
ADAM_EPS = 1e-08
LEARN_RATE = 0.001
ADAM_STEP = 10

BLK = 44
ROWS = 704
PIECE = 80
PARTS = (("x", 0, 24), ("y", 24, 32), ("z", 56, 24))
VMEM_LIMIT = 56 * 1024 * 1024


def coords():
    g = lax.axis_index("grp")
    d = lax.axis_index("dev")
    z = (g // 4) * 2 + (d // 2) % 2
    return d // 4, g % 4, z, d % 2


def device(x, y, z, core):
    return ((z // 2) * 4 + y, x * 4 + (z % 2) * 2 + core)


def on_axis(axis, x, y, z, k):
    return (
        (x + k) % 4 if axis == "x" else x,
        (y + k) % 4 if axis == "y" else y,
        (z + k) % 4 if axis == "z" else z,
    )


def evolves():
    g = lax.axis_index("grp")
    return jnp.logical_not((g == 0) | (g == 4) | (g == 2))


class Copies:
    def __init__(self, send_sem, recv_sem):
        self.send_sem, self.recv_sem = send_sem, recv_sem
        self.count = 0

    def make(self, src, dst, where):
        n = self.count
        self.count += 1
        return pltpu.make_async_remote_copy(
            src_ref=src,
            dst_ref=dst,
            send_sem=self.send_sem.at[n],
            recv_sem=self.recv_sem.at[n],
            device_id=where,
            device_id_type=MESH,
        )

    def start(self, src, dst, where):
        copy = self.make(src, dst, where)
        copy.start()
        return copy


def greet(partners):
    barrier = pltpu.get_barrier_semaphore()
    for partner in partners:
        pl.semaphore_signal(barrier, inc=1, device_id=partner, device_id_type=MESH)
    pl.semaphore_wait(barrier, len(partners))


def slab_device(step):
    d = lax.axis_index("dev")
    return (lax.axis_index("grp"), (d + step + 16) % 16)


def axis_partners():
    x, y, z, core = coords()
    found = [device(x, y, z, 1 - core)]
    for axis in ("x", "y", "z"):
        for k in (1, 2, 3):
            found.append(device(*on_axis(axis, x, y, z, k), core))
    g, d = lax.axis_index("grp"), lax.axis_index("dev")
    found.append((g, (d + 15 + 2 * core) % 16))
    return found


def gather_kernel(
    w_ref, ids_ref, gas_ref, wall_ref, total_ref, halo_ref, cnt, cnt_in, send_sem, recv_sem
):
    x, y, z, core = coords()
    d = lax.axis_index("dev")
    sibling = device(x, y, z, 1 - core)
    for j in range(8):
        wall_ref[j, d] = w_ref[pl.ds(j, PIECE, stride=8), :].astype(BF16)
    lanes = lax.broadcasted_iota(jnp.int32, (BLK, 128), 1)
    mine = (ids_ref[...] == lanes).astype(F32)
    cnt[0] = jnp.broadcast_to(jnp.sum(mine, axis=0, keepdims=True), (8, 128))
    greet(axis_partners())
    net = Copies(send_sem, recv_sem)
    sent = []

    def shard(px, pz, pc):
        return wall_ref.at[:, px * 4 + (pz % 2) * 2 + pc]

    def give(px, pz, pc, where):
        copy = net.start(shard(px, pz, pc), shard(px, pz, pc), where)
        sent.append(copy)
        return copy

    zm = z + 1 - 2 * (z % 2)
    count_copy = net.start(cnt.at[0], cnt_in.at[0], sibling)
    sent.append(count_copy)
    from_z = give(x, z, core, device(x, y, zm, core))
    own_x = [give(x, z, core, device((x + k) % 4, y, z, core)) for k in (1, 2, 3)]
    own_d2d = give(x, z, core, sibling)
    low = net.make(gas_ref.at[:, pl.ds(6, 2)], halo_ref.at[:, pl.ds(0, 2)], slab_device(1))
    high = net.make(gas_ref.at[:, pl.ds(0, 2)], halo_ref.at[:, pl.ds(2, 2)], slab_device(-1))

    @pl.when(evolves())
    def _():
        low.start()
        high.start()

    from_z.wait_recv()
    far_x = [give(x, zm, core, device((x + k) % 4, y, z, core)) for k in (1, 2, 3)]
    d2d = [own_d2d, give(x, zm, core, sibling)]
    count_copy.wait_recv()
    cnt[1] = cnt[0] + cnt_in[0]
    at, slot = 1, 1
    for axis in ("x", "y", "z"):
        copies = []
        for k in (1, 2, 3):
            copies.append(
                net.start(cnt.at[at], cnt_in.at[slot], device(*on_axis(axis, x, y, z, k), core))
            )
            slot += 1
        sent.extend(copies)
        for copy in copies:
            copy.wait_recv()
        cnt[at + 1] = cnt[at] + cnt_in[slot - 3] + cnt_in[slot - 2] + cnt_in[slot - 1]
        at += 1
    total_ref[...] = cnt[at]
    for k, copy in zip((1, 2, 3), own_x):
        copy.wait_recv()
        d2d.append(give((x + 4 - k) % 4, z, core, sibling))
    for k, copy in zip((1, 2, 3), far_x):
        copy.wait_recv()
        d2d.append(give((x + 4 - k) % 4, zm, core, sibling))
    for copy in d2d:
        copy.wait_recv()
    for copy in sent:
        copy.wait_send()

    @pl.when(evolves())
    def _():
        low.wait()
        high.wait()


def gas_first_kernel(
    gas_ref, halo_ref, pv_ref, cell_ref, fill_ref, rate_ref, mass_ref,
    pout_ref, dep_ref, sm, cpair, hs, ob,
):
    @pl.when(jnp.logical_not(evolves()))
    def _():
        pout_ref[...] = pv_ref[...]

    @pl.when(evolves())
    def _():
        for k in range(3):
            for i in range(8):
                lower = halo_ref[k, 1] if i == 0 else gas_ref[k, i - 1]
                upper = halo_ref[k, 2] if i == 7 else gas_ref[k, i + 1]
                sm[k, pl.ds(i * 128, 128), :] = 0.5 * gas_ref[k, i] + 0.25 * (lower + upper)
        lane = lax.broadcasted_iota(jnp.int32, (128, 128), 1)
        slots = lax.broadcasted_iota(jnp.int32, (64, 128), 0)
        left_lanes = lane < 64

        def tile(t, carry):
            l0 = pl.multiple_of(t * 128, 128)
            r0 = pl.multiple_of(t * 128 + 512, 128)
            cols = (pl.ds(l0, 128), pl.ds(r0, 128))
            index = jnp.concatenate([cell_ref[:, c] for c in cols], axis=0).T
            cpair[cols[0], :] = index
            for k in range(3):
                found = [
                    jnp.take_along_axis(sm[k, c, :], index, axis=1, mode="promise_in_bounds")
                    for c in cols
                ]
                gas_at = jnp.where(left_lanes, found[0], found[1]).T
                hands = []
                for side, c in enumerate(cols):
                    velocity, rate = pv_ref[k, :, c], rate_ref[:, c]
                    live = slots < fill_ref[:, c]
                    relaxed = (velocity + rate * gas_at[64 * side : 64 * side + 64]) / (1.0 + rate)
                    pout_ref[k, :, c] = jnp.where(live, relaxed, velocity)
                    hands.append(jnp.where(live, mass_ref[:, c] * (velocity - relaxed), 0.0))
                handed = jnp.concatenate(hands, axis=0).T
                coarse = handed.astype(BF16).astype(F32)
                fine = handed - coarse
                base = t * 2048
                for first, part in ((0, coarse), (8, fine)):
                    hs[pl.ds(base + first + k, 128, stride=16), :] = jnp.where(left_lanes, part, 0.0)
                    hs[pl.ds(base + first + 3 + k, 128, stride=16), :] = jnp.where(
                        left_lanes, 0.0, part
                    )
            zero = jnp.zeros((128, 128), F32)
            for row in (6, 7, 14, 15):
                hs[pl.ds(t * 2048 + row, 128, stride=16), :] = zero
            return carry

        lax.fori_loop(0, 4, tile, 0)
        cells = lax.broadcasted_iota(jnp.int32, (128, 128), 0)
        upper_rows = lax.broadcasted_iota(jnp.int32, (32, 128), 0) < 16

        def deposit(step, carry):
            for u in range(4):
                b = step * 4 + u
                values = hs[pl.ds(pl.multiple_of(b * 32, 32), 32), :]
                left = jnp.concatenate(
                    [jnp.where(upper_rows, values, 0.0), jnp.where(upper_rows, 0.0, values)], axis=1
                ).astype(BF16)
                hot = jnp.concatenate(
                    [
                        (cells == cpair[pl.ds(2 * b + i, 1), :]).astype(F32).astype(BF16)
                        for i in range(2)
                    ],
                    axis=1,
                )
                out = lax.dot_general(
                    left, hot, (((1,), (1,)), ((), ())), preferred_element_type=F32
                )
                ob[pl.ds(pl.multiple_of(b * 16, 16), 16), :] = jnp.concatenate(
                    [out[0:8] + out[8:16], out[16:24] + out[24:32]], axis=0
                )
            return carry

        lax.fori_loop(0, 64, deposit, 0)
        for k in range(3):
            for side in range(2):
                dep_ref[k, pl.ds(512 * side, 512), :] = ob[
                    pl.ds(3 * side + k, 512, stride=8), :
                ]


def dot(left, right, dims=((1,), (0,))):
    return lax.dot_general(left, right, (dims, ((), ())), preferred_element_type=F32)


def train_kernel(
    xy_ref, ids_ref, total_ref, wall_ref, grad_ref,
    a1, s1, a2, s2, b2, b1, err, w3f, w3, scale,
):
    for j in range(8):
        w3f[pl.ds(j, 128, stride=8), :] = wall_ref[j, pl.ds(1152, 128), :].astype(F32)
    for i in range(4):
        w3[i] = w3f[pl.ds(256 * i, 256), :].astype(BF16)
    lanes = lax.broadcasted_iota(jnp.int32, (BLK, 128), 1)
    inverse = 1.0 / jnp.maximum(total_ref[0:1, :], 1.0)
    picked = jnp.where(ids_ref[...] == lanes, inverse, 0.0)
    per_block = jnp.broadcast_to(jnp.sum(picked, axis=1, keepdims=True), (BLK, 128))
    for n in range(BLK):
        scale[pl.ds(16 * n, 16), :] = jnp.broadcast_to(per_block[n : n + 1], (16, 128))

    def columns(j, first, rows):
        return jnp.concatenate(
            [wall_ref[2 * j + i, pl.ds(first, rows), :] for i in range(2)], axis=1
        )

    def activate(pre, act, slope, j):
        s = 1.0 / (1.0 + jnp.exp(-pre))
        value = pre * s
        act[j] = value.astype(BF16)
        slope[j] = s * (1.0 + pre * (1.0 - s))

    def first(j, c):
        activate(dot(xy_ref[:, 0:128], columns(j, 0, 128)), a1, s1, j)
        return c

    lax.fori_loop(0, 4, first, 0)

    def second(j, c):
        acts = jnp.concatenate([a1[i] for i in range(4)], axis=1)
        activate(dot(acts, columns(j, 128, 1024)), a2, s2, j)
        return c

    lax.fori_loop(0, 4, second, 0)
    acts = jnp.concatenate([a2[i] for i in range(4)], axis=1)
    predicted = dot(acts, jnp.concatenate([w3[i] for i in range(4)], axis=0))
    err[...] = ((predicted - xy_ref[:, 128:256].astype(F32)) * scale[...]).astype(BF16)

    def third_back(j, c):
        w3f[pl.ds(pl.multiple_of(j * 256, 256), 256), :] = dot(a2[j], err[...], ((0,), (0,)))
        b2[j] = (dot(err[...], w3[j], ((1,), (1,))) * s2[j]).astype(BF16)
        return c

    lax.fori_loop(0, 4, third_back, 0)
    for j in range(8):
        grad_ref[j, pl.ds(1152, 128), :] = w3f[pl.ds(j, 128, stride=8), :]

    def second_back(i, c):
        h0 = pl.multiple_of(128 + i * 256, 128)
        for j in range(4):
            piece = dot(a1[i], b2[j], ((0,), (0,)))
            grad_ref[2 * j, pl.ds(h0, 256), :] = piece[:, :128]
            grad_ref[2 * j + 1, pl.ds(h0, 256), :] = piece[:, 128:]
        backs = jnp.concatenate([b2[j] for j in range(4)], axis=1)
        rows = jnp.concatenate([wall_ref[j, pl.ds(h0, 256), :] for j in range(8)], axis=1)
        b1[i] = (dot(backs, rows, ((1,), (1,))) * s1[i]).astype(BF16)
        return c

    lax.fori_loop(0, 4, second_back, 0)

    def first_back(j, c):
        piece = dot(xy_ref[:, 0:128], b1[j], ((0,), (0,)))
        grad_ref[2 * j, pl.ds(0, 128), :] = piece[:, :128]
        grad_ref[2 * j + 1, pl.ds(0, 128), :] = piece[:, 128:]
        return c

    lax.fori_loop(0, 4, first_back, 0)


def gas_second(gas_ref, halo_ref, dep_ref, dep_halo, gout_ref, mid):
    row = lax.broadcasted_iota(jnp.int32, (128, 128), 0)
    col = lax.broadcasted_iota(jnp.int32, (128, 128), 1)

    def walls(f):
        return (
            jnp.where(row == 0, 0.0, pltpu.roll(f, 1, 0))
            + jnp.where(row == 127, 0.0, pltpu.roll(f, 127, 0))
            + jnp.where(col == 0, 0.0, pltpu.roll(f, 1, 1))
            + jnp.where(col == 127, 0.0, pltpu.roll(f, 127, 1))
        )

    def component(k, c):
        def gas(i):
            if i < 0:
                return halo_ref[k, i + 2]
            return gas_ref[k, i] if i < 8 else halo_ref[k, i - 6]

        def dep(i):
            if i < 0:
                return dep_halo[0, k, i + 2].astype(F32)
            if i < 8:
                return dep_ref[k, pl.ds(i * 128, 128), :]
            return dep_halo[1, k, i - 8].astype(F32)

        for i in range(-1, 9):
            f = gas(i)
            step = f + KAPPA * (gas(i - 1) + gas(i + 1) + walls(f) - 6.0 * f)
            mid[i + 1] = step + 0.5 * dep(i) + 0.25 * (dep(i - 1) + dep(i + 1))
        for i in range(8):
            f = mid[i + 1]
            gout_ref[k, i] = f + KAPPA * (mid[i] + mid[i + 2] + walls(f) - 6.0 * f)
        return c

    lax.fori_loop(0, 3, component, 0)


def reduce_kernel(
    grad_ref, w_ref, m_ref, v_ref, gas_ref, halo_ref, dep_ref,
    wout_ref, mout_ref, vout_ref, gout_ref,
    sum_x, sum_y, sum_z, in1_x, in1_y, in1_z, in2_x, in2_y, in2_z, in3_x, in3_y, in3_z,
    fin, flat, dep_out, dep_halo, mid, send_sem, recv_sem,
):
    x, y, z, core = coords()
    zh, zl = z // 2, z % 2
    g = lax.axis_index("grp")
    d = lax.axis_index("dev")
    sibling = device(x, y, z, 1 - core)

    @pl.when(evolves())
    def _():
        for k in range(3):
            for i in range(2):
                dep_out[0, k, i] = dep_ref[k, pl.ds(128 * (6 + i), 128), :].astype(BF16)
                dep_out[1, k, i] = dep_ref[k, pl.ds(128 * i, 128), :].astype(BF16)

    partners = axis_partners()
    partners += [device(x, (y + k) % 4, (z + 2) % 4, core) for k in (1, 2, 3)]
    greet(partners)
    net = Copies(send_sem, recv_sem)
    sent = []
    sums = (sum_x, sum_y, sum_z)
    inputs = ((in1_x, in1_y, in1_z), (in2_x, in2_y, in2_z), (in3_x, in3_y, in3_z))
    order = (("x", "y", "z"), ("y", "z", "x"), ("z", "x", "y"))

    low = net.make(dep_out.at[0], dep_halo.at[0], slab_device(1))
    high = net.make(dep_out.at[1], dep_halo.at[1], slab_device(-1))

    @pl.when(evolves())
    def _():
        low.start()
        high.start()

    pair = []
    for part, (_, r0, n) in enumerate(PARTS):
        pair.append(
            net.start(
                grad_ref.at[:, :, :, :, 1 - core, pl.ds(r0, n)], sums[part].at[...], sibling
            )
        )
    sent += pair

    def view(ref, part, done, phase, k):
        axis = order[part][phase]
        nx, ny, nz = on_axis(axis, x, y, z, k)
        full = slice(None)
        index = [full, full, full, full]
        for a in done + (axis,):
            if a == "x":
                index[2] = nx
            elif a == "y":
                index[1] = ny
            else:
                index[0], index[3] = nz // 2, nz % 2
        return tuple(index)

    waiting = [None, None, None]

    def send(part, phase):
        done = order[part][:phase]
        waiting[part] = []
        for k in (1, 2, 3):
            nx, ny, nz = on_axis(order[part][phase], x, y, z, k)
            waiting[part].append(
                net.start(
                    sums[part].at[view(sums[part], part, done, phase, k)],
                    inputs[phase][part].at[k - 1],
                    device(nx, ny, nz, core),
                )
            )
        sent.extend(waiting[part])

    for part, (_, r0, n) in enumerate(PARTS):
        pair[part].wait_recv()
        sums[part][...] = sums[part][...] + grad_ref[:, :, :, :, core, pl.ds(r0, n), :]
        send(part, 0)

    @pl.when(evolves())
    def _():
        low.wait()
        high.wait()
        gas_second(gas_ref, halo_ref, dep_ref, dep_halo, gout_ref, mid)

    @pl.when(jnp.logical_not(evolves()))
    def _():
        gout_ref[...] = gas_ref[...]

    for phase in range(3):
        for part, (_, r0, n) in enumerate(PARTS):
            for copy in waiting[part]:
                copy.wait_recv()
            here = view(sums[part], part, order[part][:phase], phase, 0)
            come = inputs[phase][part]
            total = sums[part][here] + come[0] + come[1] + come[2]
            if phase < 2:
                sums[part][here] = total
                send(part, phase + 1)
            else:
                fin[g, pl.ds(r0, n), :] = total
    across = []
    for k in range(1, 8):
        across.append(net.start(fin.at[g], fin.at[g], ((g + k) % 8, d)))
    sent += across
    for copy in across:
        copy.wait_recv()
    for j in range(8):
        flat[pl.ds(j, PIECE, stride=8), :] = fin[j]
    gradient = flat[...]
    first_new = BETA_ONE * m_ref[...] + (1.0 - BETA_ONE) * gradient
    second_new = BETA_TWO * v_ref[...] + (1.0 - BETA_TWO) * gradient * gradient
    mout_ref[...] = first_new
    vout_ref[...] = second_new
    first_hat = first_new / (1.0 - BETA_ONE**ADAM_STEP)
    second_hat = second_new / (1.0 - BETA_TWO**ADAM_STEP)
    wout_ref[...] = w_ref[...] - LEARN_RATE * first_hat / (jnp.sqrt(second_hat) + ADAM_EPS)
    for copy in sent:
        copy.wait_send()


def in_vmem(count):
    return [pl.BlockSpec(memory_space=pltpu.VMEM)] * count


def shards(
    gas_velocity, parcel_velocity, parcel_cell, block_fill, relax_rate, parcel_mass,
    sample_blocks, learner_ids, master_weights, first_moment, second_moment,
):
    shape = jax.ShapeDtypeStruct
    ids = jnp.broadcast_to(learner_ids[:, None], (BLK, 128))
    gas = gas_velocity[0]
    wall, total, halo = pl.pallas_call(
        gather_kernel,
        name="weights_counts_halo",
        out_shape=(
            shape((8, 16, PIECE, 128), BF16),
            shape((8, 128), F32),
            shape((3, 4, 128, 128), F32),
        ),
        in_specs=in_vmem(3),
        out_specs=tuple(in_vmem(3)),
        scratch_shapes=[
            pltpu.VMEM((5, 8, 128), F32),
            pltpu.VMEM((10, 8, 128), F32),
            pltpu.SemaphoreType.DMA((32,)),
            pltpu.SemaphoreType.DMA((32,)),
        ],
        compiler_params=pltpu.CompilerParams(
            collective_id=0, has_side_effects=True, vmem_limit_bytes=VMEM_LIMIT
        ),
    )(master_weights, ids, gas)
    parcels, deposit = pl.pallas_call(
        gas_first_kernel,
        name="parcels",
        out_shape=(shape((3, 64, 1024), F32), shape((3, 1024, 128), F32)),
        in_specs=in_vmem(7),
        out_specs=tuple(in_vmem(2)),
        scratch_shapes=[
            pltpu.VMEM((3, 1024, 128), F32),
            pltpu.VMEM((512, 128), jnp.int32),
            pltpu.VMEM((8192, 128), F32),
            pltpu.VMEM((4096, 128), F32),
        ],
        compiler_params=pltpu.CompilerParams(vmem_limit_bytes=VMEM_LIMIT),
    )(gas, halo, parcel_velocity[0], parcel_cell[0], block_fill, relax_rate[0], parcel_mass[0])
    grads = pl.pallas_call(
        train_kernel,
        name="train",
        out_shape=shape((8, 1280, 128), F32),
        in_specs=in_vmem(4),
        out_specs=in_vmem(1)[0],
        scratch_shapes=[
            pltpu.VMEM((4, ROWS, 256), BF16),
            pltpu.VMEM((4, ROWS, 256), F32),
            pltpu.VMEM((4, ROWS, 256), BF16),
            pltpu.VMEM((4, ROWS, 256), F32),
            pltpu.VMEM((4, ROWS, 256), BF16),
            pltpu.VMEM((4, ROWS, 256), BF16),
            pltpu.VMEM((ROWS, 128), BF16),
            pltpu.VMEM((1024, 128), F32),
            pltpu.VMEM((4, 256, 128), BF16),
            pltpu.VMEM((ROWS, 128), F32),
        ],
        compiler_params=pltpu.CompilerParams(vmem_limit_bytes=VMEM_LIMIT),
    )(sample_blocks.reshape(ROWS, 256), ids, total, wall.reshape(8, 1280, 128))
    sizes = [n for _, _, n in PARTS]
    first_in = [
        pltpu.VMEM((3, 2, 4, 2, sizes[0], 128), F32),
        pltpu.VMEM((3, 2, 4, 2, sizes[1], 128), F32),
        pltpu.VMEM((3, 4, 4, sizes[2], 128), F32),
    ]
    second_in = [
        pltpu.VMEM((3, 2, 2, sizes[0], 128), F32),
        pltpu.VMEM((3, 4, sizes[1], 128), F32),
        pltpu.VMEM((3, 4, sizes[2], 128), F32),
    ]
    third_in = [pltpu.VMEM((3, n, 128), F32) for n in sizes]
    master_out, first_out, second_out, gas_out = pl.pallas_call(
        reduce_kernel,
        name="reduce_update_diffuse",
        out_shape=(
            shape((640, 128), F32),
            shape((640, 128), F32),
            shape((640, 128), F32),
            shape((3, 8, 128, 128), F32),
        ),
        in_specs=in_vmem(7),
        out_specs=tuple(in_vmem(4)),
        scratch_shapes=[pltpu.VMEM((2, 4, 4, 2, n, 128), F32) for n in sizes]
        + first_in
        + second_in
        + third_in
        + [
            pltpu.VMEM((8, PIECE, 128), F32),
            pltpu.VMEM((640, 128), F32),
            pltpu.VMEM((2, 3, 2, 128, 128), BF16),
            pltpu.VMEM((2, 3, 2, 128, 128), BF16),
            pltpu.VMEM((10, 128, 128), F32),
            pltpu.SemaphoreType.DMA((48,)),
            pltpu.SemaphoreType.DMA((48,)),
        ],
        compiler_params=pltpu.CompilerParams(
            collective_id=1, has_side_effects=True, vmem_limit_bytes=VMEM_LIMIT
        ),
    )(
        grads.reshape(2, 4, 4, 2, 2, PIECE, 128),
        master_weights, first_moment, second_moment, gas, halo, deposit,
    )
    return gas_out[None], parcels[None], master_out, first_out, second_out


def solution(mesh):
    placed = (
        P("grp", None, "dev", None, None),
        P("grp", None, None, "dev"),
        P("grp", None, "dev"),
        P("grp", "dev"),
        P("grp", None, "dev"),
        P("grp", None, "dev"),
        P(("grp", "dev"), None, None),
        P(("grp", "dev")),
        P("dev", None),
        P("dev", None),
        P("dev", None),
    )
    return jax.shard_map(
        shards,
        mesh=mesh,
        in_specs=placed,
        out_specs=(
            P("grp", None, "dev", None, None),
            P("grp", None, None, "dev"),
            P("dev", None),
            P("dev", None),
            P("dev", None),
        ),
        check_vma=False,
    )
```

```python
import functools

import jax
import jax.numpy as jnp
from jax import lax
from jax.experimental import pallas as pl
from jax.experimental.pallas import tpu as pltpu
from jax.sharding import PartitionSpec as P

MESH = pl.DeviceIdType.MESH
F32 = jnp.float32
BF16 = jnp.bfloat16

KAPPA = 0.15
BETA_ONE = 0.9
BETA_TWO = 0.95
ADAM_EPS = 1e-08
LEARN_RATE = 0.001
ADAM_STEP = 10

BLK = 44
ROWS = 704
PIECE = 80
PARTS = (("x", 0, 24), ("y", 24, 32), ("z", 56, 24))
VMEM_LIMIT = 60 * 1024 * 1024
RECV_X = 140


def coords():
    g = lax.axis_index("grp")
    d = lax.axis_index("dev")
    z = (g // 4) * 2 + (d // 2) % 2
    return d // 4, g % 4, z, d % 2


def device(x, y, z, core):
    return ((z // 2) * 4 + y, x * 4 + (z % 2) * 2 + core)


def on_axis(axis, x, y, z, k):
    return (
        (x + k) % 4 if axis == "x" else x,
        (y + k) % 4 if axis == "y" else y,
        (z + k) % 4 if axis == "z" else z,
    )


def evolves():
    g = lax.axis_index("grp")
    return jnp.logical_not((g == 0) | (g == 4) | (g == 2))


class Copies:
    def __init__(self, send_sem, recv_sem):
        self.send_sem, self.recv_sem = send_sem, recv_sem
        self.count = 0

    def make(self, src, dst, where):
        n = self.count
        self.count += 1
        return pltpu.make_async_remote_copy(
            src_ref=src,
            dst_ref=dst,
            send_sem=self.send_sem.at[n],
            recv_sem=self.recv_sem.at[n],
            device_id=where,
            device_id_type=MESH,
        )

    def start(self, src, dst, where):
        copy = self.make(src, dst, where)
        copy.start()
        return copy


def greet(partners):
    barrier = pltpu.get_barrier_semaphore()
    for partner in partners:
        pl.semaphore_signal(barrier, inc=1, device_id=partner, device_id_type=MESH)
    pl.semaphore_wait(barrier, len(partners))


def slab_device(step):
    d = lax.axis_index("dev")
    return (lax.axis_index("grp"), (d + step + 16) % 16)


def all_partners():
    x, y, z, core = coords()
    found = [device(x, y, z, 1 - core)]
    for axis in ("x", "y", "z"):
        for k in (1, 2, 3):
            found.append(device(*on_axis(axis, x, y, z, k), core))
    g, d = lax.axis_index("grp"), lax.axis_index("dev")
    found.append((g, (d + 15 + 2 * core) % 16))
    found += [device(x, (y + k) % 4, (z + 2) % 4, core) for k in (1, 2, 3)]
    return found


def dot(left, right, dims=((1,), (0,))):
    return lax.dot_general(left, right, (dims, ((), ())), preferred_element_type=F32)


def smooth(gas_ref, halo_ref, sm, layers):
    for k in range(3):
        for i in layers:
            lower = halo_ref[k, 1] if i == 0 else gas_ref[k, i - 1]
            upper = halo_ref[k, 2] if i == 7 else gas_ref[k, i + 1]
            sm[k, pl.ds(i * 128, 128), :] = 0.5 * gas_ref[k, i] + 0.25 * (lower + upper)


def drag(t, pv_ref, cell_ref, fill_ref, rate_ref, mass_ref, pout_ref, sm, cpair, hs):
    lane = lax.broadcasted_iota(jnp.int32, (128, 128), 1)
    slots = lax.broadcasted_iota(jnp.int32, (64, 128), 0)
    left_lanes = lane < 64
    cols = (pl.ds(t * 128, 128), pl.ds(t * 128 + 512, 128))
    index = jnp.concatenate([cell_ref[:, c] for c in cols], axis=0).T
    cpair[cols[0], :] = index
    for k in range(3):
        found = [
            jnp.take_along_axis(sm[k, c, :], index, axis=1, mode="promise_in_bounds") for c in cols
        ]
        gas_at = jnp.where(left_lanes, found[0], found[1]).T
        hands = []
        for side, c in enumerate(cols):
            velocity, rate = pv_ref[k, :, c], rate_ref[:, c]
            live = slots < fill_ref[:, c]
            relaxed = (velocity + rate * gas_at[64 * side : 64 * side + 64]) / (1.0 + rate)
            pout_ref[k, :, c] = jnp.where(live, relaxed, velocity)
            hands.append(jnp.where(live, mass_ref[:, c] * (velocity - relaxed), 0.0))
        handed = jnp.concatenate(hands, axis=0).T
        coarse = handed.astype(BF16).astype(F32)
        fine = handed - coarse
        base = t * 2048
        for first, part in ((0, coarse), (8, fine)):
            hs[pl.ds(base + first + k, 128, stride=16), :] = jnp.where(left_lanes, part, 0.0)
            hs[pl.ds(base + first + 3 + k, 128, stride=16), :] = jnp.where(left_lanes, 0.0, part)
    zero = jnp.zeros((128, 128), F32)
    for row in (6, 7, 14, 15):
        hs[pl.ds(t * 2048 + row, 128, stride=16), :] = zero


def deposit(t, cpair, hs, ob, dep):
    cells = lax.broadcasted_iota(jnp.int32, (128, 128), 0)
    upper_rows = lax.broadcasted_iota(jnp.int32, (32, 128), 0) < 16

    def several(step, carry):
        for u in range(8):
            b = t * 64 + step * 8 + u
            values = hs[pl.ds(pl.multiple_of(b * 32, 32), 32), :]
            left = jnp.concatenate(
                [jnp.where(upper_rows, values, 0.0), jnp.where(upper_rows, 0.0, values)], axis=1
            ).astype(BF16)
            hot = jnp.concatenate(
                [
                    (cells == cpair[pl.ds(2 * b + i, 1), :]).astype(F32).astype(BF16)
                    for i in range(2)
                ],
                axis=1,
            )
            out = dot(left, hot, ((1,), (1,)))
            ob[pl.ds(pl.multiple_of(b * 16, 16), 16), :] = jnp.concatenate(
                [out[0:8] + out[8:16], out[16:24] + out[24:32]], axis=0
            )
        return carry

    lax.fori_loop(0, 8, several, 0)
    for k in range(3):
        for side in range(2):
            dep[k, pl.ds(512 * side + 128 * t, 128), :] = ob[
                pl.ds(1024 * t + 3 * side + k, 128, stride=8), :
            ]


def gas_second(gas_ref, halo_ref, dep_ref, dep_halo, gout_ref, mid):
    row = lax.broadcasted_iota(jnp.int32, (128, 128), 0)
    col = lax.broadcasted_iota(jnp.int32, (128, 128), 1)

    def walls(f):
        return (
            jnp.where(row == 0, 0.0, pltpu.roll(f, 1, 0))
            + jnp.where(row == 127, 0.0, pltpu.roll(f, 127, 0))
            + jnp.where(col == 0, 0.0, pltpu.roll(f, 1, 1))
            + jnp.where(col == 127, 0.0, pltpu.roll(f, 127, 1))
        )

    def component(k, c):
        def gas(i):
            if i < 0:
                return halo_ref[k, i + 2]
            return gas_ref[k, i] if i < 8 else halo_ref[k, i - 6]

        def dep(i):
            if i < 0:
                return dep_halo[0, k, i + 2].astype(F32)
            if i < 8:
                return dep_ref[k, pl.ds(i * 128, 128), :]
            return dep_halo[1, k, i - 8].astype(F32)

        for i in range(-1, 9):
            f = gas(i)
            step = f + KAPPA * (gas(i - 1) + gas(i + 1) + walls(f) - 6.0 * f)
            mid[i + 1] = step + 0.5 * dep(i) + 0.25 * (dep(i - 1) + dep(i + 1))
        for i in range(8):
            f = mid[i + 1]
            gout_ref[k, i] = f + KAPPA * (mid[i] + mid[i + 2] + walls(f) - 6.0 * f)
        return c

    lax.fori_loop(0, 3, component, 0)


def step_kernel(
    w_ref, m_ref, v_ref, ids_ref, xy_ref, gas_ref, pv_ref, cell_ref, fill_ref, rate_ref, mass_ref,
    wout_ref, mout_ref, vout_ref, gout_ref, pout_ref,
    wall, halo, cnt, cnt_in, sm, cpair, hs, ob, dep, dep_out, dep_halo, mid,
    a1, s1, a2, s2, b2, b1, err, w3f, w3, scale,
    grad, pair_sum, in1_x, in1_y, in1_z, sum1_x, sum1_y, sum1_z, in2_x, in2_y, in2_z,
    sum2_x, sum2_y, sum2_z, in3_x, in3_y, in3_z, fin, flat, send_sem, recv_sem,
):
    x, y, z, core = coords()
    zh, zl = z // 2, z % 2
    g, d = lax.axis_index("grp"), lax.axis_index("dev")
    sibling = device(x, y, z, 1 - core)
    evo = evolves()
    net = Copies(send_sem, recv_sem)
    sent = []

    def push(src, dst, where):
        copy = net.start(src, dst, where)
        sent.append(copy)
        return copy

    def when_evolving(*steps):
        @pl.when(evo)
        def _():
            for step in steps:
                step()

    for j in range(8):
        wall[j, pl.ds(pl.multiple_of(d * PIECE, 16), PIECE), :] = w_ref[
            pl.ds(j, PIECE, stride=8), :
        ].astype(BF16)
    lanes = lax.broadcasted_iota(jnp.int32, (BLK, 128), 1)
    mine = (ids_ref[...] == lanes).astype(F32)
    cnt[0] = jnp.broadcast_to(jnp.sum(mine, axis=0, keepdims=True), (8, 128))
    greet(all_partners())

    def shard(px, pz, pc, j0, jn):
        first = pl.multiple_of((px * 4 + (pz % 2) * 2 + pc) * PIECE, 16)
        return wall.at[pl.ds(j0, jn), pl.ds(first, PIECE)]

    def give(px, pz, j0, jn, where):
        piece = shard(px, pz, core, j0, jn)
        return push(piece, piece, where)

    half = (y % 2) * 4
    zm = z + 1 - 2 * zl
    from_z = [
        give(x, z, 0, 4, device(x, y, (z + 1) % 4, core)),
        give(x, z, 4, 4, device(x, y, (z + 3) % 4, core)),
    ]
    near_x = [give(x, z, half, 4, device((x + k) % 4, y, z, core)) for k in (1, 2, 3)]
    over = [give(x, z, 0, 8, sibling)]
    count_copy = push(cnt.at[0], cnt_in.at[0], sibling)
    low = net.make(gas_ref.at[:, pl.ds(6, 2)], halo.at[:, pl.ds(0, 2)], slab_device(1))
    high = net.make(gas_ref.at[:, pl.ds(0, 2)], halo.at[:, pl.ds(2, 2)], slab_device(-1))

    def parcels(t):
        drag(t, pv_ref, cell_ref, fill_ref, rate_ref, mass_ref, pout_ref, sm, cpair, hs)

    when_evolving(
        low.start,
        high.start,
        lambda: smooth(gas_ref, halo, sm, range(1, 7)),
        lambda: parcels(1),
        lambda: parcels(2),
    )
    for copy in from_z:
        copy.wait_recv()
    far_x = [give(x, zm, half, 4, device((x + k) % 4, y, z, core)) for k in (1, 2, 3)]
    over.append(give(x, zm, 0, 8, sibling))
    when_evolving(lambda: deposit(1, cpair, hs, ob, dep))

    up, down = device(x, (y + 1) % 4, z, core), device(x, (y + 3) % 4, z, core)
    from_y = []
    for pz, copies in ((z, near_x), (zm, far_x)):
        for k, copy in zip((1, 2, 3), copies):
            copy.wait_recv()
            px = (x + 4 - k) % 4
            from_y.append((px, pz, 0, give(px, pz, half, 2, up)))
            from_y.append((px, pz, 2, give(px, pz, half + 2, 2, down)))
            over.append(give(px, pz, half, 4, sibling))
        if pz is z:
            when_evolving(lambda: deposit(2, cpair, hs, ob, dep))
    other = 4 - half
    for px, pz, q, copy in from_y:
        copy.wait_recv()
        over.append(give(px, pz, other + q, 2, sibling))
    count_copy.wait_recv()
    cnt[1] = cnt[0] + cnt_in[0]

    def count_send(axis, at, slot):
        return [
            push(cnt.at[at], cnt_in.at[slot + k], device(*on_axis(axis, x, y, z, k + 1), core))
            for k in range(3)
        ]

    def count_add(copies, at, slot):
        for copy in copies:
            copy.wait_recv()
        cnt[at + 1] = cnt[at] + cnt_in[slot] + cnt_in[slot + 1] + cnt_in[slot + 2]

    counting = count_send("x", 1, 1)
    for copy in over:
        copy.wait_recv()

    for j in range(8):
        w3f[pl.ds(j, 128, stride=8), :] = wall[j, pl.ds(1152, 128), :].astype(F32)
    for i in range(4):
        w3[i] = w3f[pl.ds(256 * i, 256), :].astype(BF16)

    def columns(j, first, rows):
        return jnp.concatenate([wall[2 * j + i, pl.ds(first, rows), :] for i in range(2)], axis=1)

    def activate(pre, act, slope, j):
        s = 0.5 * jnp.tanh(0.5 * pre) + 0.5
        value = pre * s
        act[j] = value.astype(BF16)
        slope[j] = s + value * (1.0 - s)

    def first(j, c):
        activate(dot(xy_ref[:, 0:128], columns(j, 0, 128)), a1, s1, j)
        return c

    def second(j, c):
        acts = jnp.concatenate([a1[i] for i in range(4)], axis=1)
        activate(dot(acts, columns(j, 128, 1024)), a2, s2, j)
        return c

    lax.fori_loop(0, 4, first, 0)
    count_add(counting, 1, 1)
    counting = count_send("y", 2, 4)
    lax.fori_loop(0, 2, second, 0)
    count_add(counting, 2, 4)
    counting = count_send("z", 3, 7)
    lax.fori_loop(2, 4, second, 0)
    count_add(counting, 3, 7)
    inverse = 1.0 / jnp.maximum(cnt[4, 0:1, :], 1.0)
    picked = jnp.where(ids_ref[...] == lanes, inverse, 0.0)
    per_block = jnp.broadcast_to(jnp.sum(picked, axis=1, keepdims=True), (BLK, 128))
    for n in range(BLK):
        scale[pl.ds(16 * n, 16), :] = jnp.broadcast_to(per_block[n : n + 1], (16, 128))
    acts = jnp.concatenate([a2[i] for i in range(4)], axis=1)
    predicted = dot(acts, jnp.concatenate([w3[i] for i in range(4)], axis=0))
    err[...] = ((predicted - xy_ref[:, 128:256].astype(F32)) * scale[...]).astype(BF16)

    def third_back(j, c):
        w3f[pl.ds(pl.multiple_of(j * 256, 256), 256), :] = dot(a2[j], err[...], ((0,), (0,)))
        b2[j] = (dot(err[...], w3[j], ((1,), (1,))) * s2[j]).astype(BF16)
        return c

    lax.fori_loop(0, 4, third_back, 0)
    for j in range(8):
        grad[j // 4, j % 4, pl.ds(1152, 128), :] = w3f[pl.ds(j, 128, stride=8), :]

    def grad_second(i):
        for j in range(4):
            piece = dot(a1[i], b2[j], ((0,), (0,)))
            for e in range(2):
                n = 2 * j + e
                grad[n // 4, n % 4, pl.ds(128 + 256 * i, 256), :] = piece[:, 128 * e : 128 * e + 128]

    def back_first(i, c):
        h0 = pl.multiple_of(128 + i * 256, 128)
        backs = jnp.concatenate([b2[j] for j in range(4)], axis=1)
        rows = jnp.concatenate([wall[j, pl.ds(h0, 256), :] for j in range(8)], axis=1)
        b1[i] = (dot(backs, rows, ((1,), (1,))) * s1[i]).astype(BF16)
        return c

    (_, x0, xn), (_, y0, yn), (_, z0, zn) = PARTS
    pairs = {}

    def pair_start(px):
        pairs[px] = [
            push(
                grad.at[:, :, pl.ds(pl.multiple_of((px * 4 + q * 2 + 1 - core) * PIECE, 8), PIECE)],
                pair_sum.at[px, q],
                sibling,
            )
            for q in range(2)
        ]

    first_x = {}
    first_y, first_z = [], []

    def pair_done(px):
        for q, copy in enumerate(pairs[px]):
            copy.wait_recv()
            own = pl.ds(pl.multiple_of((px * 4 + q * 2 + core) * PIECE, 8), PIECE)
            pair_sum[px, q] = pair_sum[px, q] + grad[:, :, own, :]
        k = (px - x + 4) % 4
        slot = jnp.maximum(k - 1, 0)
        n = net.count
        net.count += 1
        copy = pltpu.make_async_remote_copy(
            src_ref=pair_sum.at[px, :, :, :, pl.ds(x0, xn)],
            dst_ref=in1_x.at[slot],
            send_sem=send_sem.at[n],
            recv_sem=recv_x.at[slot],
            device_id=device(px, y, z, core),
            device_id_type=MESH,
        )
        first_x[px] = copy

        @pl.when(k > 0)
        def _():
            copy.start()

        for k in (1, 2, 3):
            ny = (y + k) % 4
            first_y.append(
                push(
                    pair_sum.at[px, :, :, ny, pl.ds(y0, yn)],
                    in1_y.at[k - 1, px],
                    device(x, ny, z, core),
                )
            )
        for k in (1, 2, 3):
            nz = (z + k) % 4
            first_z.append(
                push(
                    pair_sum.at[px, nz % 2, nz // 2, :, pl.ds(z0, zn)],
                    in1_z.at[k - 1, px],
                    device(x, y, nz, core),
                )
            )

    recv_x = recv_sem.at[pl.ds(RECV_X, 3)]
    grad_second(3)
    pair_start(3)
    grad_second(2)
    pair_start(2)
    pair_done(3)
    grad_second(1)
    pair_done(2)
    grad_second(0)
    pair_start(1)
    lax.fori_loop(0, 4, back_first, 0)
    pair_done(1)
    for j in range(4):
        piece = dot(xy_ref[:, 0:128], b1[j], ((0,), (0,)))
        for e in range(2):
            n = 2 * j + e
            grad[n // 4, n % 4, pl.ds(0, 128), :] = piece[:, 128 * e : 128 * e + 128]
    pair_start(0)
    pair_done(0)

    def send_deposit():
        for k in range(3):
            for i in range(2):
                dep_out[0, k, i] = dep[k, pl.ds(128 * (6 + i), 128), :].astype(BF16)
                dep_out[1, k, i] = dep[k, pl.ds(128 * i, 128), :].astype(BF16)
        dep_low.start()
        dep_high.start()

    dep_low = net.make(dep_out.at[0], dep_halo.at[0], slab_device(1))
    dep_high = net.make(dep_out.at[1], dep_halo.at[1], slab_device(-1))
    when_evolving(
        low.wait,
        high.wait,
        lambda: smooth(gas_ref, halo, sm, (0, 7)),
        lambda: parcels(0),
        lambda: parcels(3),
        lambda: deposit(0, cpair, hs, ob, dep),
        lambda: deposit(3, cpair, hs, ob, dep),
        send_deposit,
    )

    for k in (1, 2, 3):
        pltpu.make_async_remote_copy(
            src_ref=in1_x.at[k - 1],
            dst_ref=in1_x.at[k - 1],
            send_sem=send_sem.at[0],
            recv_sem=recv_x.at[k - 1],
            device_id=sibling,
            device_id_type=MESH,
        ).wait_recv()
    sum1_x[...] = pair_sum[x, :, :, :, pl.ds(x0, xn), :] + in1_x[0] + in1_x[1] + in1_x[2]
    second_x = [
        push(sum1_x.at[:, :, (y + k) % 4], in2_x.at[k - 1], device(x, (y + k) % 4, z, core))
        for k in (1, 2, 3)
    ]
    for copy in first_z:
        copy.wait_recv()
    sum1_z[...] = pair_sum[:, zl, zh, :, pl.ds(z0, zn), :] + in1_z[0] + in1_z[1] + in1_z[2]
    second_z = [
        push(sum1_z.at[(x + k) % 4], in2_z.at[k - 1], device((x + k) % 4, y, z, core))
        for k in (1, 2, 3)
    ]
    for copy in first_y:
        copy.wait_recv()
    sum1_y[...] = pair_sum[:, :, :, y, pl.ds(y0, yn), :] + in1_y[0] + in1_y[1] + in1_y[2]
    second_y = []
    for k in (1, 2, 3):
        nz = (z + k) % 4
        second_y.append(
            push(sum1_y.at[:, nz % 2, nz // 2], in2_y.at[k - 1], device(x, y, nz, core))
        )
    for copy in second_x:
        copy.wait_recv()
    sum2_x[...] = sum1_x[:, :, y] + in2_x[0] + in2_x[1] + in2_x[2]
    third_x = []
    for k in (1, 2, 3):
        nz = (z + k) % 4
        third_x.append(push(sum2_x.at[nz % 2, nz // 2], in3_x.at[k - 1], device(x, y, nz, core)))
    for copy in second_z:
        copy.wait_recv()
    sum2_z[...] = sum1_z[x] + in2_z[0] + in2_z[1] + in2_z[2]
    third_z = [
        push(sum2_z.at[(y + k) % 4], in3_z.at[k - 1], device(x, (y + k) % 4, z, core))
        for k in (1, 2, 3)
    ]
    for copy in second_y:
        copy.wait_recv()
    sum2_y[...] = sum1_y[:, zl, zh] + in2_y[0] + in2_y[1] + in2_y[2]
    third_y = [
        push(sum2_y.at[(x + k) % 4], in3_y.at[k - 1], device((x + k) % 4, y, z, core))
        for k in (1, 2, 3)
    ]
    for copy in third_x + third_z + third_y:
        copy.wait_recv()
    fin[g, pl.ds(x0, xn), :] = sum2_x[zl, zh] + in3_x[0] + in3_x[1] + in3_x[2]
    fin[g, pl.ds(y0, yn), :] = sum2_y[x] + in3_y[0] + in3_y[1] + in3_y[2]
    fin[g, pl.ds(z0, zn), :] = sum2_z[y] + in3_z[0] + in3_z[1] + in3_z[2]
    across = [push(fin.at[g], fin.at[g], ((g + k) % 8, d)) for k in range(1, 8)]

    when_evolving(
        dep_low.wait,
        dep_high.wait,
        lambda: gas_second(gas_ref, halo, dep, dep_halo, gout_ref, mid),
    )

    @pl.when(jnp.logical_not(evo))
    def _():
        gout_ref[...] = gas_ref[...]
        pout_ref[...] = pv_ref[...]

    for copy in across:
        copy.wait_recv()
    for j in range(8):
        flat[pl.ds(j, PIECE, stride=8), :] = fin[j]
    gradient = flat[...]
    first_new = BETA_ONE * m_ref[...] + (1.0 - BETA_ONE) * gradient
    second_new = BETA_TWO * v_ref[...] + (1.0 - BETA_TWO) * gradient * gradient
    mout_ref[...] = first_new
    vout_ref[...] = second_new
    first_hat = first_new / (1.0 - BETA_ONE**ADAM_STEP)
    second_hat = second_new / (1.0 - BETA_TWO**ADAM_STEP)
    wout_ref[...] = w_ref[...] - LEARN_RATE * first_hat / (jnp.sqrt(second_hat) + ADAM_EPS)
    for copy in sent:
        copy.wait_send()
    for px in range(4):

        @pl.when(px != x)
        def _():
            first_x[px].wait_send()


def in_vmem(count):
    return [pl.BlockSpec(memory_space=pltpu.VMEM)] * count


def shards(
    gas_velocity, parcel_velocity, parcel_cell, block_fill, relax_rate, parcel_mass,
    sample_blocks, learner_ids, master_weights, first_moment, second_moment,
):
    shape = jax.ShapeDtypeStruct
    ids = jnp.broadcast_to(learner_ids[:, None], (BLK, 128))
    (_, _, xn), (_, _, yn), (_, _, zn) = PARTS

    def buf(*dims, dtype=F32):
        return pltpu.VMEM(dims, dtype)

    scratch = [
        buf(8, 1280, 128, dtype=BF16),
        buf(3, 4, 128, 128),
        buf(5, 8, 128),
        buf(10, 8, 128),
        buf(3, 1024, 128),
        buf(512, 128, dtype=jnp.int32),
        buf(8192, 128),
        buf(4096, 128),
        buf(3, 1024, 128),
        buf(2, 3, 2, 128, 128, dtype=BF16),
        buf(2, 3, 2, 128, 128, dtype=BF16),
        buf(10, 128, 128),
        buf(4, ROWS, 256, dtype=BF16),
        buf(4, ROWS, 256),
        buf(4, ROWS, 256, dtype=BF16),
        buf(4, ROWS, 256),
        buf(4, ROWS, 256, dtype=BF16),
        buf(4, ROWS, 256, dtype=BF16),
        buf(ROWS, 128, dtype=BF16),
        buf(1024, 128),
        buf(4, 256, 128, dtype=BF16),
        buf(ROWS, 128),
        buf(2, 4, 1280, 128),
        buf(4, 2, 2, 4, PIECE, 128),
        buf(3, 2, 2, 4, xn, 128),
        buf(3, 4, 2, 2, yn, 128),
        buf(3, 4, 4, zn, 128),
        buf(2, 2, 4, xn, 128),
        buf(4, 2, 2, yn, 128),
        buf(4, 4, zn, 128),
        buf(3, 2, 2, xn, 128),
        buf(3, 4, yn, 128),
        buf(3, 4, zn, 128),
        buf(2, 2, xn, 128),
        buf(4, yn, 128),
        buf(4, zn, 128),
        buf(3, xn, 128),
        buf(3, yn, 128),
        buf(3, zn, 128),
        buf(8, PIECE, 128),
        buf(640, 128),
        pltpu.SemaphoreType.DMA((RECV_X,)),
        pltpu.SemaphoreType.DMA((RECV_X + 3,)),
    ]
    master_out, first_out, second_out, gas_out, parcels = pl.pallas_call(
        step_kernel,
        name="step",
        out_shape=(
            shape((640, 128), F32),
            shape((640, 128), F32),
            shape((640, 128), F32),
            shape((3, 8, 128, 128), F32),
            shape((3, 64, 1024), F32),
        ),
        in_specs=in_vmem(11),
        out_specs=tuple(in_vmem(5)),
        scratch_shapes=scratch,
        compiler_params=pltpu.CompilerParams(
            collective_id=0, has_side_effects=True, vmem_limit_bytes=VMEM_LIMIT
        ),
    )(
        master_weights, first_moment, second_moment, ids, sample_blocks.reshape(ROWS, 256),
        gas_velocity[0], parcel_velocity[0], parcel_cell[0], block_fill, relax_rate[0],
        parcel_mass[0],
    )
    return gas_out[None], parcels[None], master_out, first_out, second_out


def solution(mesh):
    placed = (
        P("grp", None, "dev", None, None),
        P("grp", None, None, "dev"),
        P("grp", None, "dev"),
        P("grp", "dev"),
        P("grp", None, "dev"),
        P("grp", None, "dev"),
        P(("grp", "dev"), None, None),
        P(("grp", "dev")),
        P("dev", None),
        P("dev", None),
        P("dev", None),
    )
    return jax.shard_map(
        shards,
        mesh=mesh,
        in_specs=placed,
        out_specs=(
            P("grp", None, "dev", None, None),
            P("grp", None, None, "dev"),
            P("dev", None),
            P("dev", None),
            P("dev", None),
        ),
        check_vma=False,
    )
```

```python
import jax
import jax.numpy as jnp
from jax import lax
from jax.experimental import pallas as pl
from jax.experimental.pallas import tpu as pltpu
from jax.sharding import PartitionSpec as P

MESH = pl.DeviceIdType.MESH
F32 = jnp.float32
BF16 = jnp.bfloat16

KAPPA = 0.15
BETA_ONE = 0.9
BETA_TWO = 0.95
ADAM_EPS = 1e-08
LEARN_RATE = 0.001
ADAM_STEP = 10

BLK = 44
ROWS = 704
PIECE = 80
PARTS = (("x", 0, 24), ("y", 24, 32), ("z", 56, 24))
VMEM_LIMIT = 60 * 1024 * 1024
RECV_X = 150


def coords():
    g = lax.axis_index("grp")
    d = lax.axis_index("dev")
    z = (g // 4) * 2 + (d // 2) % 2
    return d // 4, g % 4, z, d % 2


def device(x, y, z, core):
    return ((z // 2) * 4 + y, x * 4 + (z % 2) * 2 + core)


def on_axis(axis, x, y, z, k):
    return (
        (x + k) % 4 if axis == "x" else x,
        (y + k) % 4 if axis == "y" else y,
        (z + k) % 4 if axis == "z" else z,
    )


def evolves():
    g = lax.axis_index("grp")
    return jnp.logical_not((g == 0) | (g == 4) | (g == 2))


class Copies:
    def __init__(self, send_sem, recv_sem):
        self.send_sem, self.recv_sem = send_sem, recv_sem
        self.count = 0

    def make(self, src, dst, where):
        n = self.count
        self.count += 1
        return pltpu.make_async_remote_copy(
            src_ref=src,
            dst_ref=dst,
            send_sem=self.send_sem.at[n],
            recv_sem=self.recv_sem.at[n],
            device_id=where,
            device_id_type=MESH,
        )

    def start(self, src, dst, where):
        copy = self.make(src, dst, where)
        copy.start()
        return copy


def slab_device(step):
    d = lax.axis_index("dev")
    return (lax.axis_index("grp"), (d + step + 16) % 16)


def all_partners():
    x, y, z, core = coords()
    found = [device(x, y, z, 1 - core)]
    for axis in ("x", "y", "z"):
        for k in (1, 2, 3):
            found.append(device(*on_axis(axis, x, y, z, k), core))
    g, d = lax.axis_index("grp"), lax.axis_index("dev")
    found.append((g, (d + 15 + 2 * core) % 16))
    found += [device(x, (y + k) % 4, (z + 2) % 4, core) for k in (1, 2, 3)]
    return found


def dot(left, right, dims=((1,), (0,))):
    return lax.dot_general(left, right, (dims, ((), ())), preferred_element_type=F32)


def smooth(gas_ref, halo_ref, sm, layers):
    for k in range(3):
        for i in layers:
            lower = halo_ref[k, 1] if i == 0 else gas_ref[k, i - 1]
            upper = halo_ref[k, 2] if i == 7 else gas_ref[k, i + 1]
            sm[k, pl.ds(i * 128, 128), :] = 0.5 * gas_ref[k, i] + 0.25 * (lower + upper)


def drag(t, pv_ref, cell_ref, fill_ref, rate_ref, mass_ref, pout_ref, sm, cpair, hs):
    lane = lax.broadcasted_iota(jnp.int32, (128, 128), 1)
    slots = lax.broadcasted_iota(jnp.int32, (64, 128), 0)
    left_lanes = lane < 64
    cols = (pl.ds(t * 128, 128), pl.ds(t * 128 + 512, 128))
    index = jnp.concatenate([cell_ref[:, c] for c in cols], axis=0).T
    cpair[cols[0], :] = index
    for k in range(3):
        found = [
            jnp.take_along_axis(sm[k, c, :], index, axis=1, mode="promise_in_bounds") for c in cols
        ]
        gas_at = jnp.where(left_lanes, found[0], found[1]).T
        hands = []
        for side, c in enumerate(cols):
            velocity, rate = pv_ref[k, :, c], rate_ref[:, c]
            live = slots < fill_ref[:, c]
            relaxed = (velocity + rate * gas_at[64 * side : 64 * side + 64]) / (1.0 + rate)
            pout_ref[k, :, c] = jnp.where(live, relaxed, velocity)
            hands.append(jnp.where(live, mass_ref[:, c] * (velocity - relaxed), 0.0))
        handed = jnp.concatenate(hands, axis=0).T
        coarse = handed.astype(BF16).astype(F32)
        fine = handed - coarse
        base = t * 2048
        for first, part in ((0, coarse), (8, fine)):
            hs[pl.ds(base + first + k, 128, stride=16), :] = jnp.where(left_lanes, part, 0.0)
            hs[pl.ds(base + first + 3 + k, 128, stride=16), :] = jnp.where(left_lanes, 0.0, part)
    zero = jnp.zeros((128, 128), F32)
    for row in (6, 7, 14, 15):
        hs[pl.ds(t * 2048 + row, 128, stride=16), :] = zero


def deposit(t, cpair, hs, ob, dep):
    cells = lax.broadcasted_iota(jnp.int32, (128, 128), 0)
    upper_rows = lax.broadcasted_iota(jnp.int32, (32, 128), 0) < 16

    def several(step, carry):
        for u in range(32):
            b = t * 64 + step * 32 + u
            values = hs[pl.ds(pl.multiple_of(b * 32, 32), 32), :]
            left = jnp.concatenate(
                [jnp.where(upper_rows, values, 0.0), jnp.where(upper_rows, 0.0, values)], axis=1
            ).astype(BF16)
            hot = jnp.concatenate(
                [
                    (cells == cpair[pl.ds(2 * b + i, 1), :]).astype(F32).astype(BF16)
                    for i in range(2)
                ],
                axis=1,
            )
            out = dot(left, hot, ((1,), (1,)))
            ob[pl.ds(pl.multiple_of(b * 16, 16), 16), :] = jnp.concatenate(
                [out[0:8] + out[8:16], out[16:24] + out[24:32]], axis=0
            )
        return carry

    lax.fori_loop(0, 2, several, 0)
    for k in range(3):
        for side in range(2):
            dep[k, pl.ds(512 * side + 128 * t, 128), :] = ob[
                pl.ds(1024 * t + 3 * side + k, 128, stride=8), :
            ]


def gas_second(gas_ref, halo_ref, dep_ref, dep_halo, gout_ref, mid):
    row = lax.broadcasted_iota(jnp.int32, (128, 128), 0)
    col = lax.broadcasted_iota(jnp.int32, (128, 128), 1)

    def walls(f):
        return (
            jnp.where(row == 0, 0.0, pltpu.roll(f, 1, 0))
            + jnp.where(row == 127, 0.0, pltpu.roll(f, 127, 0))
            + jnp.where(col == 0, 0.0, pltpu.roll(f, 1, 1))
            + jnp.where(col == 127, 0.0, pltpu.roll(f, 127, 1))
        )

    def component(k, c):
        def gas(i):
            if i < 0:
                return halo_ref[k, i + 2]
            return gas_ref[k, i] if i < 8 else halo_ref[k, i - 6]

        def dep(i):
            if i < 0:
                return dep_halo[0, k, i + 2].astype(F32)
            if i < 8:
                return dep_ref[k, pl.ds(i * 128, 128), :]
            return dep_halo[1, k, i - 8].astype(F32)

        for i in range(-1, 9):
            f = gas(i)
            step = f + KAPPA * (gas(i - 1) + gas(i + 1) + walls(f) - 6.0 * f)
            mid[i + 1] = step + 0.5 * dep(i) + 0.25 * (dep(i - 1) + dep(i + 1))
        for i in range(8):
            f = mid[i + 1]
            gout_ref[k, i] = f + KAPPA * (mid[i] + mid[i + 2] + walls(f) - 6.0 * f)
        return c

    lax.fori_loop(0, 3, component, 0)


def step_kernel(
    ids_ref, w_in, xy_in, gas_in, pv_in, cell_in, fill_in, rate_in, mass_in,
    grad_out, gas_out, parcel_out,
    ids, w_ref, xy_ref, gas_ref, pv_ref, cell_ref, fill_ref, rate_ref, mass_ref, gout_ref, pout_ref,
    in_sem, out_sem,
    wall, halo, cnt, cnt_in, sm, cpair, hs, ob, dep, dep_out, dep_halo, mid,
    a1, s1, a2, s2, b2, b1, err, w3f, w3, scale,
    grad, pair_sum, in1_x, in1_y, in1_z, sum1_x, sum1_y, sum1_z, in2_x, in2_y, in2_z,
    sum2_x, sum2_y, sum2_z, in3_x, in3_y, in3_z, fin, flat, send_sem, recv_sem,
):
    x, y, z, core = coords()
    zh, zl = z // 2, z % 2
    g, d = lax.axis_index("grp"), lax.axis_index("dev")
    sibling = device(x, y, z, 1 - core)
    evo = evolves()
    net = Copies(send_sem, recv_sem)
    sent = []

    def push(src, dst, where):
        copy = net.start(src, dst, where)
        sent.append(copy)
        return copy

    def when_evolving(*steps):
        @pl.when(evo)
        def _():
            for step in steps:
                step()

    partners = all_partners()
    barrier = pltpu.get_barrier_semaphore()
    for partner in partners:
        pl.semaphore_signal(barrier, inc=1, device_id=partner, device_id_type=MESH)
    pairs_in = (
        (w_in, w_ref), (gas_in, gas_ref), (cell_in, cell_ref), (pv_in, pv_ref), (rate_in, rate_ref),
        (mass_in, mass_ref), (fill_in, fill_ref), (xy_in, xy_ref),
    )
    loads = [
        pltpu.make_async_copy(src, dst, in_sem.at[i]) for i, (src, dst) in enumerate(pairs_in)
    ]
    for load in loads:
        load.start()
    for n in range(BLK):
        ids[pl.ds(n, 1), :] = jnp.full((1, 128), ids_ref[n], jnp.int32)
    gas_store = pltpu.make_async_copy(gout_ref, gas_out, out_sem.at[0])
    parcel_store = pltpu.make_async_copy(pout_ref, parcel_out, out_sem.at[1])
    gas_same = pltpu.make_async_copy(gas_ref, gas_out, out_sem.at[0])
    parcel_same = pltpu.make_async_copy(pv_ref, parcel_out, out_sem.at[1])

    loads[0].wait()
    for j in range(8):
        wall[j, pl.ds(pl.multiple_of(d * PIECE, 16), PIECE), :] = w_ref[
            pl.ds(j, PIECE, stride=8), :
        ].astype(BF16)
    lanes = lax.broadcasted_iota(jnp.int32, (BLK, 128), 1)
    mine = (ids[...] == lanes).astype(F32)
    cnt[0] = jnp.broadcast_to(jnp.sum(mine, axis=0, keepdims=True), (8, 128))
    pl.semaphore_wait(barrier, len(partners))

    def shard(px, pz, pc, j0, jn):
        first = pl.multiple_of((px * 4 + (pz % 2) * 2 + pc) * PIECE, 16)
        return wall.at[pl.ds(j0, jn), pl.ds(first, PIECE)]

    def give(px, pz, j0, jn, where):
        piece = shard(px, pz, core, j0, jn)
        return push(piece, piece, where)

    half = (y % 2) * 4
    zm = z + 1 - 2 * zl
    count_copy = push(cnt.at[0], cnt_in.at[0], sibling)
    from_z = [
        give(x, z, 0, 4, device(x, y, (z + 1) % 4, core)),
        give(x, z, 4, 4, device(x, y, (z + 3) % 4, core)),
    ]
    near_x = [give(x, z, half, 4, device((x + k) % 4, y, z, core)) for k in (1, 2, 3)]
    over = [give(x, z, 0, 8, sibling)]
    low = net.make(gas_ref.at[:, pl.ds(6, 2)], halo.at[:, pl.ds(0, 2)], slab_device(1))
    high = net.make(gas_ref.at[:, pl.ds(0, 2)], halo.at[:, pl.ds(2, 2)], slab_device(-1))

    def parcels(t):
        drag(t, pv_ref, cell_ref, fill_ref, rate_ref, mass_ref, pout_ref, sm, cpair, hs)

    for load in loads[1:]:
        load.wait()

    @pl.when(jnp.logical_not(evo))
    def _():
        gas_same.start()
        parcel_same.start()

    when_evolving(
        lambda: smooth(gas_ref, halo, sm, range(1, 7)),
        lambda: parcels(1),
        lambda: parcels(2),
    )
    count_copy.wait_recv()
    cnt[1] = cnt[0] + cnt_in[0]

    def count_send(axis, at, slot):
        return [
            push(cnt.at[at], cnt_in.at[slot + k], device(*on_axis(axis, x, y, z, k + 1), core))
            for k in range(3)
        ]

    def count_add(copies, at, slot):
        for copy in copies:
            copy.wait_recv()
        cnt[at + 1] = cnt[at] + cnt_in[slot] + cnt_in[slot + 1] + cnt_in[slot + 2]

    counting = count_send("y", 1, 1)
    for copy in from_z:
        copy.wait_recv()
    far_x = [give(x, zm, half, 4, device((x + k) % 4, y, z, core)) for k in (1, 2, 3)]
    over.append(give(x, zm, 0, 8, sibling))
    when_evolving(lambda: deposit(1, cpair, hs, ob, dep))

    up, down = device(x, (y + 1) % 4, z, core), device(x, (y + 3) % 4, z, core)
    from_y = []
    for pz, copies in ((z, near_x), (zm, far_x)):
        for k, copy in zip((1, 2, 3), copies):
            copy.wait_recv()
            px = (x + 4 - k) % 4
            from_y.append((px, pz, 0, give(px, pz, half, 2, up)))
            from_y.append((px, pz, 2, give(px, pz, half + 2, 2, down)))
            over.append(give(px, pz, half, 4, sibling))
        if pz is z:
            count_add(counting, 1, 1)
            counting = count_send("z", 2, 4)
            when_evolving(lambda: deposit(2, cpair, hs, ob, dep))
    count_add(counting, 2, 4)
    counting = count_send("x", 3, 7)
    other = 4 - half
    for px, pz, q, copy in from_y:
        copy.wait_recv()
        over.append(give(px, pz, other + q, 2, sibling))
    for copy in over:
        copy.wait_recv()

    when_evolving(low.start, high.start)

    for j in range(8):
        w3f[pl.ds(j, 128, stride=8), :] = wall[j, pl.ds(1152, 128), :].astype(F32)
    for i in range(4):
        w3[i] = w3f[pl.ds(256 * i, 256), :].astype(BF16)

    def columns(j, first, rows):
        return jnp.concatenate([wall[2 * j + i, pl.ds(first, rows), :] for i in range(2)], axis=1)

    def activate(pre, act, slope, j):
        s = 0.5 * jnp.tanh(0.5 * pre) + 0.5
        value = pre * s
        act[j] = value.astype(BF16)
        slope[j] = s + value * (1.0 - s)

    def first(j, c):
        activate(dot(xy_ref[:, 0:128], columns(j, 0, 128)), a1, s1, j)
        return c

    def second(j, c):
        acts = jnp.concatenate([a1[i] for i in range(4)], axis=1)
        activate(dot(acts, columns(j, 128, 1024)), a2, s2, j)
        return c

    lax.fori_loop(0, 4, first, 0)
    lax.fori_loop(0, 4, second, 0)
    count_add(counting, 3, 7)
    inverse = 1.0 / jnp.maximum(cnt[4, 0:1, :], 1.0)
    picked = jnp.where(ids[...] == lanes, inverse, 0.0)
    per_block = jnp.broadcast_to(jnp.sum(picked, axis=1, keepdims=True), (BLK, 128))
    for n in range(BLK):
        scale[pl.ds(16 * n, 16), :] = jnp.broadcast_to(per_block[n : n + 1], (16, 128))
    acts = jnp.concatenate([a2[i] for i in range(4)], axis=1)
    predicted = dot(acts, jnp.concatenate([w3[i] for i in range(4)], axis=0))
    err[...] = ((predicted - xy_ref[:, 128:256].astype(F32)) * scale[...]).astype(BF16)

    def third_back(j, c):
        w3f[pl.ds(pl.multiple_of(j * 256, 256), 256), :] = dot(a2[j], err[...], ((0,), (0,)))
        b2[j] = (dot(err[...], w3[j], ((1,), (1,))) * s2[j]).astype(BF16)
        return c

    lax.fori_loop(0, 4, third_back, 0)
    for j in range(8):
        grad[j // 4, j % 4, pl.ds(1152, 128), :] = w3f[pl.ds(j, 128, stride=8), :]

    def grad_second(i):
        for j in range(4):
            piece = dot(a1[i], b2[j], ((0,), (0,)))
            for e in range(2):
                n = 2 * j + e
                grad[n // 4, n % 4, pl.ds(128 + 256 * i, 256), :] = piece[:, 128 * e : 128 * e + 128]

    def back_first(i, c):
        h0 = pl.multiple_of(128 + i * 256, 128)
        backs = jnp.concatenate([b2[j] for j in range(4)], axis=1)
        rows = jnp.concatenate([wall[j, pl.ds(h0, 256), :] for j in range(8)], axis=1)
        b1[i] = (dot(backs, rows, ((1,), (1,))) * s1[i]).astype(BF16)
        return c

    (_, x0, xn), (_, y0, yn), (_, z0, zn) = PARTS
    pairs = {}

    def pair_start(px):
        pairs[px] = [
            push(
                grad.at[:, :, pl.ds(pl.multiple_of((px * 4 + q * 2 + 1 - core) * PIECE, 8), PIECE)],
                pair_sum.at[px, q],
                sibling,
            )
            for q in range(2)
        ]

    first_x = {}
    first_y, first_z = {}, {}

    def to_x(px, src, slots, sems):
        k = (px - x + 4) % 4
        slot = jnp.maximum(k - 1, 0)
        n = net.count
        net.count += 1
        copy = pltpu.make_async_remote_copy(
            src_ref=src,
            dst_ref=slots.at[slot],
            send_sem=send_sem.at[n],
            recv_sem=sems.at[slot],
            device_id=device(px, y, z, core),
            device_id_type=MESH,
        )

        @pl.when(k > 0)
        def _():
            copy.start()

        return copy

    def from_x(slots, sems):
        for k in range(3):
            pltpu.make_async_remote_copy(
                src_ref=slots.at[k],
                dst_ref=slots.at[k],
                send_sem=send_sem.at[0],
                recv_sem=sems.at[k],
                device_id=sibling,
                device_id_type=MESH,
            ).wait_recv()

    def pair_done(px):
        for q, copy in enumerate(pairs[px]):
            copy.wait_recv()
            own = pl.ds(pl.multiple_of((px * 4 + q * 2 + core) * PIECE, 8), PIECE)
            pair_sum[px, q] = pair_sum[px, q] + grad[:, :, own, :]
        first_x[px] = to_x(px, pair_sum.at[px, :, :, :, pl.ds(x0, xn)], in1_x, recv_x)

        for k in (1, 2, 3):
            ny = (y + k) % 4
            first_y.setdefault(px, []).append(
                push(
                    pair_sum.at[px, :, :, ny, pl.ds(y0, yn)],
                    in1_y.at[k - 1, px],
                    device(x, ny, z, core),
                )
            )
        for k in (1, 2, 3):
            nz = (z + k) % 4
            first_z.setdefault(px, []).append(
                push(
                    pair_sum.at[px, nz % 2, nz // 2, :, pl.ds(z0, zn)],
                    in1_z.at[k - 1, px],
                    device(x, y, nz, core),
                )
            )

    second_y, sent_z = [], {}

    def second_phase(px):
        for copy in first_z[px]:
            copy.wait_recv()
        sum1_z[px] = (
            pair_sum[px, zl, zh, :, pl.ds(z0, zn), :] + in1_z[0, px] + in1_z[1, px] + in1_z[2, px]
        )
        sent_z[px] = to_x(px, sum1_z.at[px], in2_z, recv_z)
        for copy in first_y[px]:
            copy.wait_recv()
        sum1_y[px] = (
            pair_sum[px, :, :, y, pl.ds(y0, yn), :] + in1_y[0, px] + in1_y[1, px] + in1_y[2, px]
        )
        for k in (1, 2, 3):
            nz = (z + k) % 4
            second_y.append(
                push(
                    sum1_y.at[px, nz % 2, nz // 2], in2_y.at[k - 1, px], device(x, y, nz, core)
                )
            )

    recv_x = recv_sem.at[pl.ds(RECV_X, 3)]
    recv_z = recv_sem.at[pl.ds(RECV_X + 3, 3)]
    grad_second(3)
    pair_start(3)
    grad_second(2)
    pair_start(2)
    pair_done(3)
    grad_second(1)
    pair_done(2)
    grad_second(0)
    pair_start(1)
    lax.fori_loop(0, 4, back_first, 0)
    pair_done(1)
    for j in range(4):
        piece = dot(xy_ref[:, 0:128], b1[j], ((0,), (0,)))
        for e in range(2):
            n = 2 * j + e
            grad[n // 4, n % 4, pl.ds(0, 128), :] = piece[:, 128 * e : 128 * e + 128]
    pair_start(0)
    pair_done(0)

    def send_deposit():
        for k in range(3):
            for i in range(2):
                dep_out[0, k, i] = dep[k, pl.ds(128 * (6 + i), 128), :].astype(BF16)
                dep_out[1, k, i] = dep[k, pl.ds(128 * i, 128), :].astype(BF16)
        dep_low.start()
        dep_high.start()

    dep_low = net.make(dep_out.at[0], dep_halo.at[0], slab_device(1))
    dep_high = net.make(dep_out.at[1], dep_halo.at[1], slab_device(-1))
    when_evolving(
        low.wait,
        high.wait,
        lambda: smooth(gas_ref, halo, sm, (0, 7)),
        lambda: parcels(0),
        lambda: parcels(3),
        parcel_store.start,
        lambda: deposit(0, cpair, hs, ob, dep),
    )
    second_phase(3)
    second_phase(2)
    when_evolving(lambda: deposit(3, cpair, hs, ob, dep), send_deposit)
    second_phase(1)


    from_x(in1_x, recv_x)
    sum1_x[...] = pair_sum[x, :, :, :, pl.ds(x0, xn), :] + in1_x[0] + in1_x[1] + in1_x[2]
    second_x = [
        push(sum1_x.at[:, :, (y + k) % 4], in2_x.at[k - 1], device(x, (y + k) % 4, z, core))
        for k in (1, 2, 3)
    ]
    second_phase(0)
    for copy in second_x:
        copy.wait_recv()
    sum2_x[...] = sum1_x[:, :, y] + in2_x[0] + in2_x[1] + in2_x[2]
    third_x = []
    for k in (1, 2, 3):
        nz = (z + k) % 4
        third_x.append(push(sum2_x.at[nz % 2, nz // 2], in3_x.at[k - 1], device(x, y, nz, core)))
    from_x(in2_z, recv_z)
    sum2_z[...] = sum1_z[x] + in2_z[0] + in2_z[1] + in2_z[2]
    third_z = [
        push(sum2_z.at[(y + k) % 4], in3_z.at[k - 1], device(x, (y + k) % 4, z, core))
        for k in (1, 2, 3)
    ]
    for copy in second_y:
        copy.wait_recv()
    sum2_y[...] = sum1_y[:, zl, zh] + in2_y[0] + in2_y[1] + in2_y[2]
    third_y = [
        push(sum2_y.at[(x + k) % 4], in3_y.at[k - 1], device((x + k) % 4, y, z, core))
        for k in (1, 2, 3)
    ]
    for copy in third_x + third_z + third_y:
        copy.wait_recv()
    fin[g, pl.ds(x0, xn), :] = sum2_x[zl, zh] + in3_x[0] + in3_x[1] + in3_x[2]
    fin[g, pl.ds(y0, yn), :] = sum2_y[x] + in3_y[0] + in3_y[1] + in3_y[2]
    fin[g, pl.ds(z0, zn), :] = sum2_z[y] + in3_z[0] + in3_z[1] + in3_z[2]
    across = [push(fin.at[g], fin.at[g], ((g + k) % 8, d)) for k in range(1, 8)]

    when_evolving(
        dep_low.wait,
        dep_high.wait,
        lambda: gas_second(gas_ref, halo, dep, dep_halo, gout_ref, mid),
        gas_store.start,
    )

    for copy in across:
        copy.wait_recv()
    for j in range(8):
        flat[pl.ds(j, PIECE, stride=8), :] = fin[j]
    grad_store = pltpu.make_async_copy(flat, grad_out, out_sem.at[2])
    grad_store.start()
    for store in (gas_store, parcel_store, grad_store):
        store.wait()
    for copy in sent:
        copy.wait_send()
    for px in range(4):

        @pl.when(px != x)
        def _():
            first_x[px].wait_send()
            sent_z[px].wait_send()


def finish_kernel(
    grad_in, w_in, m_in, v_in, gas_in, parcel_in,
    w_out, m_out, v_out, gas_out, parcel_out,
    grad, w, m, v, gas, parcels, in_sem, out_sem,
):
    staged = (
        (gas_in, gas), (parcel_in, parcels), (grad_in, grad), (m_in, m), (v_in, v), (w_in, w),
    )
    loads = [pltpu.make_async_copy(a, b, in_sem.at[i]) for i, (a, b) in enumerate(staged)]
    results = ((gas, gas_out), (parcels, parcel_out), (m, m_out), (v, v_out), (w, w_out))
    stores = [pltpu.make_async_copy(a, b, out_sem.at[i]) for i, (a, b) in enumerate(results)]
    for load in loads:
        load.start()
    for n in range(2):
        loads[n].wait()
        stores[n].start()
    for load in loads[2:]:
        load.wait()
    gradient = grad[...]
    first_new = BETA_ONE * m[...] + (1.0 - BETA_ONE) * gradient
    second_new = BETA_TWO * v[...] + (1.0 - BETA_TWO) * gradient * gradient
    m[...] = first_new
    v[...] = second_new
    first_hat = first_new / (1.0 - BETA_ONE**ADAM_STEP)
    second_hat = second_new / (1.0 - BETA_TWO**ADAM_STEP)
    w[...] = w[...] - LEARN_RATE * first_hat / (jnp.sqrt(second_hat) + ADAM_EPS)
    for store in stores[2:]:
        store.start()
    for store in stores:
        store.wait()


def anywhere(count):
    return [pl.BlockSpec(memory_space=pl.ANY)] * count


def shards(
    gas_velocity, parcel_velocity, parcel_cell, block_fill, relax_rate, parcel_mass,
    sample_blocks, learner_ids, master_weights, first_moment, second_moment,
):
    shape = jax.ShapeDtypeStruct
    (_, _, xn), (_, _, yn), (_, _, zn) = PARTS

    def buf(*dims, dtype=F32):
        return pltpu.VMEM(dims, dtype)

    scratch = [
        buf(BLK, 128, dtype=jnp.int32),
        buf(640, 128),
        buf(ROWS, 256, dtype=BF16),
        buf(3, 8, 128, 128),
        buf(3, 64, 1024),
        buf(64, 1024, dtype=jnp.int32),
        buf(1, 1024, dtype=jnp.int32),
        buf(64, 1024),
        buf(64, 1024),
        buf(3, 8, 128, 128),
        buf(3, 64, 1024),
        pltpu.SemaphoreType.DMA((8,)),
        pltpu.SemaphoreType.DMA((3,)),
        buf(8, 1280, 128, dtype=BF16),
        buf(3, 4, 128, 128),
        buf(5, 8, 128),
        buf(10, 8, 128),
        buf(3, 1024, 128),
        buf(512, 128, dtype=jnp.int32),
        buf(8192, 128),
        buf(4096, 128),
        buf(3, 1024, 128),
        buf(2, 3, 2, 128, 128, dtype=BF16),
        buf(2, 3, 2, 128, 128, dtype=BF16),
        buf(10, 128, 128),
        buf(4, ROWS, 256, dtype=BF16),
        buf(4, ROWS, 256),
        buf(4, ROWS, 256, dtype=BF16),
        buf(4, ROWS, 256),
        buf(4, ROWS, 256, dtype=BF16),
        buf(4, ROWS, 256, dtype=BF16),
        buf(ROWS, 128, dtype=BF16),
        buf(1024, 128),
        buf(4, 256, 128, dtype=BF16),
        buf(ROWS, 128),
        buf(2, 4, 1280, 128),
        buf(4, 2, 2, 4, PIECE, 128),
        buf(3, 2, 2, 4, xn, 128),
        buf(3, 4, 2, 2, yn, 128),
        buf(3, 4, 4, zn, 128),
        buf(2, 2, 4, xn, 128),
        buf(4, 2, 2, yn, 128),
        buf(4, 4, zn, 128),
        buf(3, 2, 2, xn, 128),
        buf(3, 4, yn, 128),
        buf(3, 4, zn, 128),
        buf(2, 2, xn, 128),
        buf(4, yn, 128),
        buf(4, zn, 128),
        buf(3, xn, 128),
        buf(3, yn, 128),
        buf(3, zn, 128),
        buf(8, PIECE, 128),
        buf(640, 128),
        pltpu.SemaphoreType.DMA((RECV_X,)),
        pltpu.SemaphoreType.DMA((RECV_X + 6,)),
    ]
    grads, gas_out, parcels = pl.pallas_call(
        step_kernel,
        name="step",
        out_shape=(
            shape((640, 128), F32),
            shape((3, 8, 128, 128), F32),
            shape((3, 64, 1024), F32),
        ),
        in_specs=[pl.BlockSpec(memory_space=pltpu.SMEM)] + anywhere(8),
        out_specs=tuple(anywhere(3)),
        scratch_shapes=scratch,
        compiler_params=pltpu.CompilerParams(
            collective_id=0, has_side_effects=True, vmem_limit_bytes=VMEM_LIMIT
        ),
    )(
        learner_ids, master_weights, sample_blocks.reshape(ROWS, 256), gas_velocity[0],
        parcel_velocity[0], parcel_cell[0], block_fill, relax_rate[0], parcel_mass[0],
    )
    state = shape((640, 128), F32)
    master_out, first_out, second_out, gas_out, parcels = pl.pallas_call(
        finish_kernel,
        name="finish",
        out_shape=(state, state, state, shape(gas_out.shape, F32), shape(parcels.shape, F32)),
        in_specs=anywhere(6),
        out_specs=tuple(anywhere(5)),
        scratch_shapes=[buf(640, 128) for _ in range(4)]
        + [
            buf(*gas_out.shape),
            buf(*parcels.shape),
            pltpu.SemaphoreType.DMA((6,)),
            pltpu.SemaphoreType.DMA((5,)),
        ],
        compiler_params=pltpu.CompilerParams(vmem_limit_bytes=VMEM_LIMIT),
    )(grads, master_weights, first_moment, second_moment, gas_out, parcels)
    return gas_out[None], parcels[None], master_out, first_out, second_out


def solution(mesh):
    placed = (
        P("grp", None, "dev", None, None),
        P("grp", None, None, "dev"),
        P("grp", None, "dev"),
        P("grp", "dev"),
        P("grp", None, "dev"),
        P("grp", None, "dev"),
        P(("grp", "dev"), None, None),
        P(("grp", "dev")),
        P("dev", None),
        P("dev", None),
        P("dev", None),
    )
    return jax.shard_map(
        shards,
        mesh=mesh,
        in_specs=placed,
        out_specs=(
            P("grp", None, "dev", None, None),
            P("grp", None, None, "dev"),
            P("dev", None),
            P("dev", None),
            P("dev", None),
        ),
        check_vma=False,
    )
```

```python
import jax
import jax.numpy as jnp
from jax import lax
from jax.experimental import pallas as pl
from jax.experimental.pallas import tpu as pltpu
from jax.sharding import PartitionSpec as P

MESH = pl.DeviceIdType.MESH
F32 = jnp.float32
BF16 = jnp.bfloat16

KAPPA = 0.15
BETA_ONE = 0.9
BETA_TWO = 0.95
ADAM_EPS = 1e-08
LEARN_RATE = 0.001
ADAM_STEP = 10

BLK = 44
ROWS = 704
PIECE = 80
VMEM_LIMIT = 46 * 1024 * 1024
RECV_X = 150


def coords():
    g = lax.axis_index("grp")
    d = lax.axis_index("dev")
    z = (g // 4) * 2 + (d // 2) % 2
    return d // 4, g % 4, z, d % 2


def device(x, y, z, core):
    return ((z // 2) * 4 + y, x * 4 + (z % 2) * 2 + core)


def on_axis(axis, x, y, z, k):
    return (
        (x + k) % 4 if axis == "x" else x,
        (y + k) % 4 if axis == "y" else y,
        (z + k) % 4 if axis == "z" else z,
    )


def evolves():
    g = lax.axis_index("grp")
    return jnp.logical_not((g == 0) | (g == 4) | (g == 2))


class Copies:
    def __init__(self, send_sem, recv_sem):
        self.send_sem, self.recv_sem = send_sem, recv_sem
        self.count = 0

    def make(self, src, dst, where):
        n = self.count
        self.count += 1
        return pltpu.make_async_remote_copy(
            src_ref=src,
            dst_ref=dst,
            send_sem=self.send_sem.at[n],
            recv_sem=self.recv_sem.at[n],
            device_id=where,
            device_id_type=MESH,
        )

    def start(self, src, dst, where):
        copy = self.make(src, dst, where)
        copy.start()
        return copy


def slab_device(step):
    d = lax.axis_index("dev")
    return (lax.axis_index("grp"), (d + step + 16) % 16)


def all_partners():
    x, y, z, core = coords()
    found = [device(x, y, z, 1 - core)]
    for axis in ("x", "y", "z"):
        for k in (1, 2, 3):
            found.append(device(*on_axis(axis, x, y, z, k), core))
    g, d = lax.axis_index("grp"), lax.axis_index("dev")
    found.append((g, (d + 15 + 2 * core) % 16))
    found += [device(x, (y + k) % 4, (z + 2) % 4, core) for k in (1, 2, 3)]
    return found


def dot(left, right, dims=((1,), (0,))):
    return lax.dot_general(left, right, (dims, ((), ())), preferred_element_type=F32)


def smooth(gas_ref, halo_ref, sm, layers):
    for k in range(3):
        for i in layers:
            lower = halo_ref[k, 1] if i == 0 else gas_ref[k, i - 1]
            upper = halo_ref[k, 2] if i == 7 else gas_ref[k, i + 1]
            sm[k, pl.ds(i * 128, 128), :] = 0.5 * gas_ref[k, i] + 0.25 * (lower + upper)


def drag(t, pv_ref, cell_ref, fill_ref, rate_ref, mass_ref, pout_ref, sm, cpair, hs):
    lane = lax.broadcasted_iota(jnp.int32, (128, 128), 1)
    slots = lax.broadcasted_iota(jnp.int32, (64, 128), 0)
    left_lanes = lane < 64
    cols = (pl.ds(t * 128, 128), pl.ds(t * 128 + 512, 128))
    index = jnp.concatenate([cell_ref[:, c] for c in cols], axis=0).T
    cpair[cols[0], :] = index
    for k in range(3):
        found = [
            jnp.take_along_axis(sm[k, c, :], index, axis=1, mode="promise_in_bounds") for c in cols
        ]
        gas_at = jnp.where(left_lanes, found[0], found[1]).T
        hands = []
        for side, c in enumerate(cols):
            velocity, rate = pv_ref[k, :, c], rate_ref[:, c]
            live = slots < fill_ref[:, c]
            relaxed = (velocity + rate * gas_at[64 * side : 64 * side + 64]) / (1.0 + rate)
            pout_ref[k, :, c] = jnp.where(live, relaxed, velocity)
            hands.append(jnp.where(live, mass_ref[:, c] * (velocity - relaxed), 0.0))
        handed = jnp.concatenate(hands, axis=0).T
        coarse = handed.astype(BF16).astype(F32)
        fine = handed - coarse
        base = t * 2048
        for first, part in ((0, coarse), (8, fine)):
            hs[pl.ds(base + first + k, 128, stride=16), :] = jnp.where(left_lanes, part, 0.0)
            hs[pl.ds(base + first + 3 + k, 128, stride=16), :] = jnp.where(left_lanes, 0.0, part)
    zero = jnp.zeros((128, 128), F32)
    for row in (6, 7, 14, 15):
        hs[pl.ds(t * 2048 + row, 128, stride=16), :] = zero


def deposit(t, cpair, hs, ob, dep):
    cells = lax.broadcasted_iota(jnp.int32, (128, 128), 0)
    upper_rows = lax.broadcasted_iota(jnp.int32, (32, 128), 0) < 16

    def several(step, carry):
        for u in range(32):
            b = t * 64 + step * 32 + u
            values = hs[pl.ds(pl.multiple_of(b * 32, 32), 32), :]
            left = jnp.concatenate(
                [jnp.where(upper_rows, values, 0.0), jnp.where(upper_rows, 0.0, values)], axis=1
            ).astype(BF16)
            hot = jnp.concatenate(
                [
                    (cells == cpair[pl.ds(2 * b + i, 1), :]).astype(F32).astype(BF16)
                    for i in range(2)
                ],
                axis=1,
            )
            out = dot(left, hot, ((1,), (1,)))
            ob[pl.ds(pl.multiple_of(b * 16, 16), 16), :] = jnp.concatenate(
                [out[0:8] + out[8:16], out[16:24] + out[24:32]], axis=0
            )
        return carry

    lax.fori_loop(0, 2, several, 0)
    for k in range(3):
        for side in range(2):
            dep[k, pl.ds(512 * side + 128 * t, 128), :] = ob[
                pl.ds(1024 * t + 3 * side + k, 128, stride=8), :
            ]


def gas_second(gas_ref, halo_ref, dep_ref, dep_halo, gout_ref, mid):
    row = lax.broadcasted_iota(jnp.int32, (128, 128), 0)
    col = lax.broadcasted_iota(jnp.int32, (128, 128), 1)

    def walls(f):
        return (
            jnp.where(row == 0, 0.0, pltpu.roll(f, 1, 0))
            + jnp.where(row == 127, 0.0, pltpu.roll(f, 127, 0))
            + jnp.where(col == 0, 0.0, pltpu.roll(f, 1, 1))
            + jnp.where(col == 127, 0.0, pltpu.roll(f, 127, 1))
        )

    def component(k, c):
        def gas(i):
            if i < 0:
                return halo_ref[k, i + 2]
            return gas_ref[k, i] if i < 8 else halo_ref[k, i - 6]

        def dep(i):
            if i < 0:
                return dep_halo[0, k, i + 2].astype(F32)
            if i < 8:
                return dep_ref[k, pl.ds(i * 128, 128), :]
            return dep_halo[1, k, i - 8].astype(F32)

        for i in range(-1, 9):
            f = gas(i)
            step = f + KAPPA * (gas(i - 1) + gas(i + 1) + walls(f) - 6.0 * f)
            mid[i + 1] = step + 0.5 * dep(i) + 0.25 * (dep(i - 1) + dep(i + 1))
        for i in range(8):
            f = mid[i + 1]
            gout_ref[k, i] = f + KAPPA * (mid[i] + mid[i + 2] + walls(f) - 6.0 * f)
        return c

    lax.fori_loop(0, 3, component, 0)


def step_kernel(
    ids_ref, w_in, xy_in, gas_in, pv_in, cell_in, fill_in, rate_in, mass_in,
    flat, gout_ref, pout_ref,
    ids, w_ref, xy_ref, gas_ref, pv_ref, cell_ref, fill_ref, rate_ref, mass_ref,
    in_sem, out_sem,
    wall, halo, cnt, cnt_in, sm, cpair, hs, ob, dep, dep_out, dep_halo, mid,
    a1, s1, a2, s2, b2, b1, err, w3f, w3, scale,
    grad, pair_sum, in1_x, in1_y, in1_z, sum1_x, sum1_y, sum1_z, in2_x, in2_y, in2_z,
    sum1_v, in2_v,
    sum2_x, sum2_y, sum2_z, in3_x, in3_y, in3_z, fin, send_sem, recv_sem,
):
    x, y, z, core = coords()
    zh, zl = z // 2, z % 2
    g, d = lax.axis_index("grp"), lax.axis_index("dev")
    sibling = device(x, y, z, 1 - core)
    evo = evolves()
    net = Copies(send_sem, recv_sem)
    sent = []

    def push(src, dst, where):
        copy = net.start(src, dst, where)
        sent.append(copy)
        return copy

    def when_evolving(*steps):
        @pl.when(evo)
        def _():
            for step in steps:
                step()

    partners = all_partners()
    barrier = pltpu.get_barrier_semaphore()
    for partner in partners:
        pl.semaphore_signal(barrier, inc=1, device_id=partner, device_id_type=MESH)
    pairs_in = (
        (w_in, w_ref), (gas_in, gas_ref), (cell_in, cell_ref), (pv_in, pv_ref), (rate_in, rate_ref),
        (mass_in, mass_ref), (fill_in, fill_ref), (xy_in, xy_ref),
    )
    loads = [
        pltpu.make_async_copy(src, dst, in_sem.at[i]) for i, (src, dst) in enumerate(pairs_in)
    ]
    for load in loads:
        load.start()
    for n in range(BLK):
        ids[pl.ds(n, 1), :] = jnp.full((1, 128), ids_ref[n], jnp.int32)
    gas_same = pltpu.make_async_copy(gas_ref, gout_ref, out_sem.at[0])
    parcel_same = pltpu.make_async_copy(pv_ref, pout_ref, out_sem.at[1])

    loads[0].wait()
    for j in range(8):
        spread = w_ref[pl.ds(j, PIECE, stride=8), :]
        mixed = jnp.concatenate([spread[:32], w_ref[pl.ds(256 + 48 * j, 48), :]], axis=0)
        last = w_ref[pl.ds(PIECE * j, PIECE), :]
        mine_j = jnp.where(d == 15, last, jnp.where(d == 14, mixed, spread))
        wall[j, pl.ds(pl.multiple_of(d * PIECE, 16), PIECE), :] = mine_j.astype(BF16)
    lanes = lax.broadcasted_iota(jnp.int32, (BLK, 128), 1)
    mine = (ids[...] == lanes).astype(F32)
    cnt[0] = jnp.broadcast_to(jnp.sum(mine, axis=0, keepdims=True), (8, 128))
    pl.semaphore_wait(barrier, len(partners))

    def shard(px, pz, pc, j0, jn):
        first = pl.multiple_of((px * 4 + (pz % 2) * 2 + pc) * PIECE, 16)
        return wall.at[pl.ds(j0, jn), pl.ds(first, PIECE)]

    def give(px, pz, j0, jn, where):
        piece = shard(px, pz, core, j0, jn)
        return push(piece, piece, where)

    half = (y % 2) * 4
    zm = z + 1 - 2 * zl
    count_copy = push(cnt.at[0], cnt_in.at[0], sibling)
    from_z = [
        give(x, z, 0, 4, device(x, y, (z + 1) % 4, core)),
        give(x, z, 4, 4, device(x, y, (z + 3) % 4, core)),
    ]
    near_x = [give(x, z, half, 4, device((x + k) % 4, y, z, core)) for k in (1, 2, 3)]
    over = [give(x, z, 0, 8, sibling)]
    low = net.make(gas_ref.at[:, pl.ds(6, 2)], halo.at[:, pl.ds(0, 2)], slab_device(1))
    high = net.make(gas_ref.at[:, pl.ds(0, 2)], halo.at[:, pl.ds(2, 2)], slab_device(-1))

    def parcels(t):
        drag(t, pv_ref, cell_ref, fill_ref, rate_ref, mass_ref, pout_ref, sm, cpair, hs)

    for load in loads[1:]:
        load.wait()

    @pl.when(jnp.logical_not(evo))
    def _():
        gas_same.start()
        parcel_same.start()

    when_evolving(
        lambda: smooth(gas_ref, halo, sm, range(1, 7)),
        lambda: parcels(1),
        lambda: parcels(2),
    )
    count_copy.wait_recv()
    cnt[1] = cnt[0] + cnt_in[0]

    def count_send(axis, at, slot):
        return [
            push(cnt.at[at], cnt_in.at[slot + k], device(*on_axis(axis, x, y, z, k + 1), core))
            for k in range(3)
        ]

    def count_add(copies, at, slot):
        for copy in copies:
            copy.wait_recv()
        cnt[at + 1] = cnt[at] + cnt_in[slot] + cnt_in[slot + 1] + cnt_in[slot + 2]

    counting = count_send("y", 1, 1)
    for copy in from_z:
        copy.wait_recv()
    far_x = [give(x, zm, half, 4, device((x + k) % 4, y, z, core)) for k in (1, 2, 3)]
    over.append(give(x, zm, 0, 8, sibling))
    when_evolving(lambda: deposit(1, cpair, hs, ob, dep))

    up, down = device(x, (y + 1) % 4, z, core), device(x, (y + 3) % 4, z, core)
    from_y = []
    for pz, copies in ((z, near_x), (zm, far_x)):
        for k, copy in zip((1, 2, 3), copies):
            copy.wait_recv()
            px = (x + 4 - k) % 4
            from_y.append((px, pz, 0, give(px, pz, half, 2, up)))
            from_y.append((px, pz, 2, give(px, pz, half + 2, 2, down)))
            over.append(give(px, pz, half, 4, sibling))
        if pz is z:
            count_add(counting, 1, 1)
            counting = count_send("z", 2, 4)
            when_evolving(lambda: deposit(2, cpair, hs, ob, dep))
    count_add(counting, 2, 4)
    counting = count_send("x", 3, 7)
    other = 4 - half
    for px, pz, q, copy in from_y:
        copy.wait_recv()
        over.append(give(px, pz, other + q, 2, sibling))
    for copy in over:
        copy.wait_recv()

    when_evolving(low.start, high.start)

    for j in range(8):
        w3[pl.ds(48 * j, 48), :] = wall[j, pl.ds(1152, 48), :]
        w3[pl.ds(384 + PIECE * j, PIECE), :] = wall[j, pl.ds(1200, PIECE), :]

    def columns(j, first, rows):
        return jnp.concatenate([wall[2 * j + i, pl.ds(first, rows), :] for i in range(2)], axis=1)

    def activate(pre, act, slope, j):
        s = 0.5 * jnp.tanh(0.5 * pre) + 0.5
        value = pre * s
        act[j] = value.astype(BF16)
        slope[j] = s + value * (1.0 - s)

    def first(j, c):
        activate(dot(xy_ref[:, 0:128], columns(j, 0, 128)), a1, s1, j)
        return c

    def second(j, c):
        acts = jnp.concatenate([a1[i] for i in range(4)], axis=1)
        activate(dot(acts, columns(j, 128, 1024)), a2, s2, j)
        return c

    lax.fori_loop(0, 4, first, 0)
    lax.fori_loop(0, 4, second, 0)
    count_add(counting, 3, 7)
    inverse = 1.0 / jnp.maximum(cnt[4, 0:1, :], 1.0)
    picked = jnp.where(ids[...] == lanes, inverse, 0.0)
    per_block = jnp.broadcast_to(jnp.sum(picked, axis=1, keepdims=True), (BLK, 128))
    for n in range(BLK):
        scale[pl.ds(16 * n, 16), :] = jnp.broadcast_to(per_block[n : n + 1], (16, 128))
    acts = jnp.concatenate([a2[i] for i in range(4)], axis=1)
    predicted = dot(acts, w3[...])
    err[...] = ((predicted - xy_ref[:, 128:256].astype(F32)) * scale[...]).astype(BF16)

    def third_back(j, c):
        part = pl.ds(pl.multiple_of(j * 256, 256), 256)
        w3f[part, :] = dot(a2[j], err[...], ((0,), (0,)))
        b2[j] = (dot(err[...], w3[part, :], ((1,), (1,))) * s2[j]).astype(BF16)
        return c

    lax.fori_loop(0, 4, third_back, 0)
    for j in range(8):
        grad[j // 4, j % 4, pl.ds(1152, 48), :] = w3f[pl.ds(48 * j, 48), :]
        grad[j // 4, j % 4, pl.ds(1200, PIECE), :] = w3f[pl.ds(384 + PIECE * j, PIECE), :]

    def grad_second(i):
        for j in range(4):
            piece = dot(a1[i], b2[j], ((0,), (0,)))
            for e in range(2):
                n = 2 * j + e
                grad[n // 4, n % 4, pl.ds(128 + 256 * i, 256), :] = piece[:, 128 * e : 128 * e + 128]

    def back_first(i, c):
        h0 = pl.multiple_of(128 + i * 256, 128)
        backs = jnp.concatenate([b2[j] for j in range(4)], axis=1)
        rows = jnp.concatenate([wall[j, pl.ds(h0, 256), :] for j in range(8)], axis=1)
        b1[i] = (dot(backs, rows, ((1,), (1,))) * s1[i]).astype(BF16)
        return c

    def y_rows(px):
        return pl.ds(24, 32 if px % 2 else 24)

    def z_rows(px):
        return pl.ds(56, 24) if px % 2 else pl.ds(48, 32)

    pairs = {}

    def pair_start(px):
        pairs[px] = [
            push(
                grad.at[:, :, pl.ds(pl.multiple_of((px * 4 + q * 2 + 1 - core) * PIECE, 8), PIECE)],
                pair_sum.at[px, q],
                sibling,
            )
            for q in range(2)
        ]

    first_x = {}
    first_y, first_z = {}, {}

    def to_x(px, src, slots, sems):
        k = (px - x + 4) % 4
        slot = jnp.maximum(k - 1, 0)
        n = net.count
        net.count += 1
        copy = pltpu.make_async_remote_copy(
            src_ref=src,
            dst_ref=slots.at[slot],
            send_sem=send_sem.at[n],
            recv_sem=sems.at[slot],
            device_id=device(px, y, z, core),
            device_id_type=MESH,
        )

        @pl.when(k > 0)
        def _():
            copy.start()

        return copy

    def from_x(slots, sems):
        for k in range(3):
            pltpu.make_async_remote_copy(
                src_ref=slots.at[k],
                dst_ref=slots.at[k],
                send_sem=send_sem.at[0],
                recv_sem=sems.at[k],
                device_id=sibling,
                device_id_type=MESH,
            ).wait_recv()

    def pair_done(px):
        for q, copy in enumerate(pairs[px]):
            copy.wait_recv()
            own = pl.ds(pl.multiple_of((px * 4 + q * 2 + core) * PIECE, 8), PIECE)
            pair_sum[px, q] = pair_sum[px, q] + grad[:, :, own, :]
        first_x[px] = to_x(px, pair_sum.at[px, :, :, :, pl.ds(0, 24)], in1_x, recv_x)

        for k in (1, 2, 3):
            ny = (y + k) % 4
            first_y.setdefault(px, []).append(
                push(
                    pair_sum.at[px, :, :, ny, y_rows(px)],
                    in1_y.at[k - 1, px, :, :, pl.ds(0, y_rows(px).size)],
                    device(x, ny, z, core),
                )
            )
        for k in (1, 2, 3):
            nz = (z + k) % 4
            first_z.setdefault(px, []).append(
                push(
                    pair_sum.at[px, nz % 2, nz // 2, :, z_rows(px)],
                    in1_z.at[k - 1, px, :, pl.ds(0, z_rows(px).size)],
                    device(x, y, nz, core),
                )
            )

    second_y, second_v, sent_z = {}, {}, {}

    def second_phase(px):
        for copy in first_z[px]:
            copy.wait_recv()
        zn = z_rows(px).size
        total = pair_sum[px, zl, zh, :, z_rows(px), :]
        for k in range(3):
            total = total + in1_z[k, px, :, pl.ds(0, zn), :]
        sum1_z[px] = total[:, zn - 24 :]
        sent_z[px] = to_x(px, sum1_z.at[px], in2_z, recv_z)
        if zn > 24:
            sum1_v[px // 2] = total[:, :8]
            second_v[px] = [
                push(
                    sum1_v.at[px // 2, (y + k) % 4],
                    in2_v.at[k - 1, px // 2],
                    device(x, (y + k) % 4, z, core),
                )
                for k in (1, 2, 3)
            ]
        for copy in first_y[px]:
            copy.wait_recv()
        yn = y_rows(px).size
        total = pair_sum[px, :, :, y, y_rows(px), :]
        for k in range(3):
            total = total + in1_y[k, px, :, :, pl.ds(0, yn), :]
        sum1_y[px, :, :, pl.ds(0, yn), :] = total
        second_y[px] = []
        for k in (1, 2, 3):
            nz = (z + k) % 4
            second_y[px].append(
                push(
                    sum1_y.at[px, nz % 2, nz // 2, pl.ds(0, yn)],
                    in2_y.at[k - 1, px, pl.ds(0, yn)],
                    device(x, y, nz, core),
                )
            )

    def third_phase(px):
        for copy in second_y[px] + second_v.get(px, []):
            copy.wait_recv()
        yn = y_rows(px).size
        rows = pl.ds(0, yn)
        sum2_y[px, rows, :] = (
            sum1_y[px, zl, zh, rows, :]
            + in2_y[0, px, rows, :] + in2_y[1, px, rows, :] + in2_y[2, px, rows, :]
        )
        if yn == 24:
            e = px // 2
            sum2_y[px, pl.ds(24, 8), :] = sum1_v[e, y] + in2_v[0, e] + in2_v[1, e] + in2_v[2, e]
        sent_y[px] = to_x(px, sum2_y.at[px], in3_y, recv_y)

    sent_y = {}
    recv_x = recv_sem.at[pl.ds(RECV_X, 3)]
    recv_z = recv_sem.at[pl.ds(RECV_X + 3, 3)]
    recv_y = recv_sem.at[pl.ds(RECV_X + 6, 3)]
    grad_second(3)
    pair_start(3)
    grad_second(2)
    pair_start(2)
    pair_done(3)
    grad_second(1)
    pair_done(2)
    grad_second(0)
    pair_start(1)
    lax.fori_loop(0, 4, back_first, 0)
    pair_done(1)
    for j in range(4):
        piece = dot(xy_ref[:, 0:128], b1[j], ((0,), (0,)))
        for e in range(2):
            n = 2 * j + e
            grad[n // 4, n % 4, pl.ds(0, 128), :] = piece[:, 128 * e : 128 * e + 128]
    pair_start(0)
    pair_done(0)

    def send_deposit():
        for k in range(3):
            for i in range(2):
                dep_out[0, k, i] = dep[k, pl.ds(128 * (6 + i), 128), :].astype(BF16)
                dep_out[1, k, i] = dep[k, pl.ds(128 * i, 128), :].astype(BF16)
        dep_low.start()
        dep_high.start()

    dep_low = net.make(dep_out.at[0], dep_halo.at[0], slab_device(1))
    dep_high = net.make(dep_out.at[1], dep_halo.at[1], slab_device(-1))
    when_evolving(
        low.wait,
        high.wait,
        lambda: smooth(gas_ref, halo, sm, (0, 7)),
        lambda: parcels(0),
        lambda: parcels(3),
        lambda: deposit(0, cpair, hs, ob, dep),
    )
    second_phase(3)
    second_phase(2)
    when_evolving(lambda: deposit(3, cpair, hs, ob, dep), send_deposit)
    second_phase(1)


    from_x(in1_x, recv_x)
    sum1_x[...] = pair_sum[x, :, :, :, pl.ds(0, 24), :] + in1_x[0] + in1_x[1] + in1_x[2]
    second_x = [
        push(sum1_x.at[:, :, (y + k) % 4], in2_x.at[k - 1], device(x, (y + k) % 4, z, core))
        for k in (1, 2, 3)
    ]
    second_phase(0)
    for copy in second_x:
        copy.wait_recv()
    sum2_x[...] = sum1_x[:, :, y] + in2_x[0] + in2_x[1] + in2_x[2]
    third_x = []
    for k in (1, 2, 3):
        nz = (z + k) % 4
        third_x.append(push(sum2_x.at[nz % 2, nz // 2], in3_x.at[k - 1], device(x, y, nz, core)))
    from_x(in2_z, recv_z)
    sum2_z[...] = sum1_z[x] + in2_z[0] + in2_z[1] + in2_z[2]
    third_z = [
        push(sum2_z.at[(y + k) % 4], in3_z.at[k - 1], device(x, (y + k) % 4, z, core))
        for k in (1, 2, 3)
    ]
    for px in (3, 2, 1, 0):
        third_phase(px)
    for copy in third_x + third_z:
        copy.wait_recv()
    fin[g, pl.ds(0, 24), :] = sum2_x[zl, zh] + in3_x[0] + in3_x[1] + in3_x[2]
    fin[g, pl.ds(56, 24), :] = sum2_z[y] + in3_z[0] + in3_z[1] + in3_z[2]
    from_x(in3_y, recv_y)
    fin[g, pl.ds(24, 32), :] = sum2_y[x] + in3_y[0] + in3_y[1] + in3_y[2]
    across = [push(fin.at[g], fin.at[g], ((g + k) % 8, d)) for k in range(1, 8)]

    when_evolving(
        dep_low.wait,
        dep_high.wait,
        lambda: gas_second(gas_ref, halo, dep, dep_halo, gout_ref, mid),
    )

    for copy in across:
        copy.wait_recv()

    @pl.when(d < 14)
    def _():
        for j in range(8):
            flat[pl.ds(j, PIECE, stride=8), :] = fin[j]

    @pl.when(d == 14)
    def _():
        for j in range(8):
            flat[pl.ds(j, 32, stride=8), :] = fin[j, :32]
            flat[pl.ds(256 + 48 * j, 48), :] = fin[j, 32:]

    @pl.when(d == 15)
    def _():
        for j in range(8):
            flat[pl.ds(PIECE * j, PIECE), :] = fin[j]

    @pl.when(jnp.logical_not(evo))
    def _():
        gas_same.wait()
        parcel_same.wait()

    for copy in sent:
        copy.wait_send()
    for px in range(4):

        @pl.when(px != x)
        def _():
            first_x[px].wait_send()
            sent_z[px].wait_send()
            sent_y[px].wait_send()


def finish_kernel(
    grad, w, m, v, gas, parcels,
    w_out, m_out, v_out, gas_out, parcel_out,
    w_new, m_new, v_new, out_sem,
):
    results = (
        (gas, gas_out), (parcels, parcel_out), (m_new, m_out), (v_new, v_out), (w_new, w_out),
    )
    stores = [pltpu.make_async_copy(a, b, out_sem.at[i]) for i, (a, b) in enumerate(results)]
    for store in stores[:2]:
        store.start()
    gradient = grad[...]
    first_new = BETA_ONE * m[...] + (1.0 - BETA_ONE) * gradient
    second_new = BETA_TWO * v[...] + (1.0 - BETA_TWO) * gradient * gradient
    m_new[...] = first_new
    v_new[...] = second_new
    first_hat = first_new / (1.0 - BETA_ONE**ADAM_STEP)
    second_hat = second_new / (1.0 - BETA_TWO**ADAM_STEP)
    w_new[...] = w[...] - LEARN_RATE * first_hat / (jnp.sqrt(second_hat) + ADAM_EPS)
    for store in stores[2:]:
        store.start()
    for store in stores:
        store.wait()


def anywhere(count):
    return [pl.BlockSpec(memory_space=pl.ANY)] * count


def shards(
    gas_velocity, parcel_velocity, parcel_cell, block_fill, relax_rate, parcel_mass,
    sample_blocks, learner_ids, master_weights, first_moment, second_moment,
):
    shape = jax.ShapeDtypeStruct

    def buf(*dims, dtype=F32):
        return pltpu.VMEM(dims, dtype)

    scratch = [
        buf(BLK, 128, dtype=jnp.int32),
        buf(640, 128),
        buf(ROWS, 256, dtype=BF16),
        buf(3, 8, 128, 128),
        buf(3, 64, 1024),
        buf(64, 1024, dtype=jnp.int32),
        buf(1, 1024, dtype=jnp.int32),
        buf(64, 1024),
        buf(64, 1024),
        pltpu.SemaphoreType.DMA((8,)),
        pltpu.SemaphoreType.DMA((2,)),
        buf(8, 1280, 128, dtype=BF16),
        buf(3, 4, 128, 128),
        buf(5, 8, 128),
        buf(10, 8, 128),
        buf(3, 1024, 128),
        buf(512, 128, dtype=jnp.int32),
        buf(8192, 128),
        buf(4096, 128),
        buf(3, 1024, 128),
        buf(2, 3, 2, 128, 128, dtype=BF16),
        buf(2, 3, 2, 128, 128, dtype=BF16),
        buf(10, 128, 128),
        buf(4, ROWS, 256, dtype=BF16),
        buf(4, ROWS, 256),
        buf(4, ROWS, 256, dtype=BF16),
        buf(4, ROWS, 256),
        buf(4, ROWS, 256, dtype=BF16),
        buf(4, ROWS, 256, dtype=BF16),
        buf(ROWS, 128, dtype=BF16),
        buf(1024, 128),
        buf(1024, 128, dtype=BF16),
        buf(ROWS, 128),
        buf(2, 4, 1280, 128),
        buf(4, 2, 2, 4, PIECE, 128),
        buf(3, 2, 2, 4, 24, 128),
        buf(3, 4, 2, 2, 32, 128),
        buf(3, 4, 4, 32, 128),
        buf(2, 2, 4, 24, 128),
        buf(4, 2, 2, 32, 128),
        buf(4, 4, 24, 128),
        buf(3, 2, 2, 24, 128),
        buf(3, 4, 32, 128),
        buf(3, 4, 24, 128),
        buf(2, 4, 8, 128),
        buf(3, 2, 8, 128),
        buf(2, 2, 24, 128),
        buf(4, 32, 128),
        buf(4, 24, 128),
        buf(3, 24, 128),
        buf(3, 32, 128),
        buf(3, 24, 128),
        buf(8, PIECE, 128),
        pltpu.SemaphoreType.DMA((RECV_X,)),
        pltpu.SemaphoreType.DMA((RECV_X + 9,)),
    ]
    grads, gas_out, parcels = pl.pallas_call(
        step_kernel,
        name="step",
        out_shape=(
            buf(640, 128),
            buf(3, 8, 128, 128),
            buf(3, 64, 1024),
        ),
        in_specs=[pl.BlockSpec(memory_space=pltpu.SMEM)]
        + [pl.BlockSpec(memory_space=pltpu.HBM)] * 8,
        out_specs=tuple([pl.BlockSpec(memory_space=pltpu.VMEM)] * 3),
        scratch_shapes=scratch,
        compiler_params=pltpu.CompilerParams(
            collective_id=0, has_side_effects=True, vmem_limit_bytes=VMEM_LIMIT
        ),
    )(
        *[
            pltpu.with_memory_space_constraint(array, pltpu.HBM)
            for array in (
                learner_ids, master_weights, sample_blocks.reshape(ROWS, 256), gas_velocity[0],
                parcel_velocity[0], parcel_cell[0], block_fill, relax_rate[0], parcel_mass[0],
            )
        ],
    )
    state = shape((640, 128), F32)
    master_out, first_out, second_out, gas_out, parcels = pl.pallas_call(
        finish_kernel,
        name="finish",
        out_shape=(state, state, state, shape(gas_out.shape, F32), shape(parcels.shape, F32)),
        in_specs=[pl.BlockSpec(memory_space=pltpu.VMEM)] * 6,
        out_specs=tuple(anywhere(5)),
        scratch_shapes=[buf(640, 128) for _ in range(3)] + [pltpu.SemaphoreType.DMA((5,))],
        compiler_params=pltpu.CompilerParams(vmem_limit_bytes=16 * 1024 * 1024),
    )(grads, master_weights, first_moment, second_moment, gas_out, parcels)
    return gas_out[None], parcels[None], master_out, first_out, second_out


def solution(mesh):
    placed = (
        P("grp", None, "dev", None, None),
        P("grp", None, None, "dev"),
        P("grp", None, "dev"),
        P("grp", "dev"),
        P("grp", None, "dev"),
        P("grp", None, "dev"),
        P(("grp", "dev"), None, None),
        P(("grp", "dev")),
        P("dev", None),
        P("dev", None),
        P("dev", None),
    )
    return jax.shard_map(
        shards,
        mesh=mesh,
        in_specs=placed,
        out_specs=(
            P("grp", None, "dev", None, None),
            P("grp", None, None, "dev"),
            P("dev", None),
            P("dev", None),
            P("dev", None),
        ),
        check_vma=False,
    )
```

```python
import jax
import jax.numpy as jnp
from jax import lax
from jax.experimental import pallas as pl
from jax.experimental.pallas import tpu as pltpu
from jax.sharding import PartitionSpec as P

MESH = pl.DeviceIdType.MESH
F32 = jnp.float32
BF16 = jnp.bfloat16

KAPPA = 0.15
BETA_ONE = 0.9
BETA_TWO = 0.95
ADAM_EPS = 1e-08
LEARN_RATE = 0.001
ADAM_STEP = 10

BLK = 44
ROWS = 704
PIECE = 80
VMEM_LIMIT = 46 * 1024 * 1024
RECV_X = 150


def coords():
    g = lax.axis_index("grp")
    d = lax.axis_index("dev")
    z = (g // 4) * 2 + (d // 2) % 2
    return d // 4, g % 4, z, d % 2


def device(x, y, z, core):
    return ((z // 2) * 4 + y, x * 4 + (z % 2) * 2 + core)


def on_axis(axis, x, y, z, k):
    return (
        (x + k) % 4 if axis == "x" else x,
        (y + k) % 4 if axis == "y" else y,
        (z + k) % 4 if axis == "z" else z,
    )


def evolves():
    g = lax.axis_index("grp")
    return jnp.logical_not((g == 0) | (g == 4) | (g == 2))


class Copies:
    def __init__(self, send_sem, recv_sem):
        self.send_sem, self.recv_sem = send_sem, recv_sem
        self.count = 0

    def make(self, src, dst, where):
        n = self.count
        self.count += 1
        return pltpu.make_async_remote_copy(
            src_ref=src,
            dst_ref=dst,
            send_sem=self.send_sem.at[n],
            recv_sem=self.recv_sem.at[n],
            device_id=where,
            device_id_type=MESH,
        )

    def start(self, src, dst, where):
        copy = self.make(src, dst, where)
        copy.start()
        return copy


def slab_device(step):
    d = lax.axis_index("dev")
    return (lax.axis_index("grp"), (d + step + 16) % 16)


def all_partners():
    x, y, z, core = coords()
    found = [device(x, y, z, 1 - core)]
    for axis in ("x", "y", "z"):
        for k in (1, 2, 3):
            found.append(device(*on_axis(axis, x, y, z, k), core))
    g, d = lax.axis_index("grp"), lax.axis_index("dev")
    found.append((g, (d + 15 + 2 * core) % 16))
    found += [device(x, (y + k) % 4, (z + 2) % 4, core) for k in (1, 2, 3)]
    return found


def dot(left, right, dims=((1,), (0,))):
    return lax.dot_general(left, right, (dims, ((), ())), preferred_element_type=F32)


def smooth(gas_ref, halo_ref, sm, layers):
    for k in range(3):
        for i in layers:
            lower = halo_ref[k, 1] if i == 0 else gas_ref[k, i - 1]
            upper = halo_ref[k, 2] if i == 7 else gas_ref[k, i + 1]
            sm[k, pl.ds(i * 128, 128), :] = 0.5 * gas_ref[k, i] + 0.25 * (lower + upper)


def drag(t, pv_ref, cell_ref, fill_ref, rate_ref, mass_ref, pout_ref, sm, cpair, hs):
    lane = lax.broadcasted_iota(jnp.int32, (128, 128), 1)
    slots = lax.broadcasted_iota(jnp.int32, (64, 128), 0)
    left_lanes = lane < 64
    cols = (pl.ds(t * 128, 128), pl.ds(t * 128 + 512, 128))
    index = jnp.concatenate([cell_ref[:, c] for c in cols], axis=0).T
    cpair[cols[0], :] = index
    for k in range(3):
        found = [
            jnp.take_along_axis(sm[k, c, :], index, axis=1, mode="promise_in_bounds") for c in cols
        ]
        gas_at = jnp.where(left_lanes, found[0], found[1]).T
        hands = []
        for side, c in enumerate(cols):
            velocity, rate = pv_ref[k, :, c], rate_ref[:, c]
            live = slots < fill_ref[:, c]
            relaxed = (velocity + rate * gas_at[64 * side : 64 * side + 64]) / (1.0 + rate)
            pout_ref[k, :, c] = jnp.where(live, relaxed, velocity)
            hands.append(jnp.where(live, mass_ref[:, c] * (velocity - relaxed), 0.0))
        handed = jnp.concatenate(hands, axis=0).T
        coarse = handed.astype(BF16).astype(F32)
        fine = handed - coarse
        base = t * 2048
        for first, part in ((0, coarse), (8, fine)):
            hs[pl.ds(base + first + k, 128, stride=16), :] = jnp.where(left_lanes, part, 0.0)
            hs[pl.ds(base + first + 3 + k, 128, stride=16), :] = jnp.where(left_lanes, 0.0, part)
    zero = jnp.zeros((128, 128), F32)
    for row in (6, 7, 14, 15):
        hs[pl.ds(t * 2048 + row, 128, stride=16), :] = zero


def deposit(t, cpair, hs, ob, dep):
    cells = lax.broadcasted_iota(jnp.int32, (128, 128), 0)
    upper_rows = lax.broadcasted_iota(jnp.int32, (32, 128), 0) < 16

    def several(step, carry):
        for u in range(32):
            b = t * 64 + step * 32 + u
            values = hs[pl.ds(pl.multiple_of(b * 32, 32), 32), :]
            left = jnp.concatenate(
                [jnp.where(upper_rows, values, 0.0), jnp.where(upper_rows, 0.0, values)], axis=1
            ).astype(BF16)
            hot = jnp.concatenate(
                [
                    (cells == cpair[pl.ds(2 * b + i, 1), :]).astype(F32).astype(BF16)
                    for i in range(2)
                ],
                axis=1,
            )
            out = dot(left, hot, ((1,), (1,)))
            ob[pl.ds(pl.multiple_of(b * 16, 16), 16), :] = jnp.concatenate(
                [out[0:8] + out[8:16], out[16:24] + out[24:32]], axis=0
            )
        return carry

    lax.fori_loop(0, 2, several, 0)
    for k in range(3):
        for side in range(2):
            dep[k, pl.ds(512 * side + 128 * t, 128), :] = ob[
                pl.ds(1024 * t + 3 * side + k, 128, stride=8), :
            ]


def gas_second(gas_ref, halo_ref, dep_ref, dep_halo, gout_ref, mid):
    row = lax.broadcasted_iota(jnp.int32, (128, 128), 0)
    col = lax.broadcasted_iota(jnp.int32, (128, 128), 1)

    def walls(f):
        return (
            jnp.where(row == 0, 0.0, pltpu.roll(f, 1, 0))
            + jnp.where(row == 127, 0.0, pltpu.roll(f, 127, 0))
            + jnp.where(col == 0, 0.0, pltpu.roll(f, 1, 1))
            + jnp.where(col == 127, 0.0, pltpu.roll(f, 127, 1))
        )

    def component(k, c):
        def gas(i):
            if i < 0:
                return halo_ref[k, i + 2]
            return gas_ref[k, i] if i < 8 else halo_ref[k, i - 6]

        def dep(i):
            if i < 0:
                return dep_halo[0, k, i + 2].astype(F32)
            if i < 8:
                return dep_ref[k, pl.ds(i * 128, 128), :]
            return dep_halo[1, k, i - 8].astype(F32)

        for i in range(-1, 9):
            f = gas(i)
            step = f + KAPPA * (gas(i - 1) + gas(i + 1) + walls(f) - 6.0 * f)
            mid[i + 1] = step + 0.5 * dep(i) + 0.25 * (dep(i - 1) + dep(i + 1))
        for i in range(8):
            f = mid[i + 1]
            gout_ref[k, i] = f + KAPPA * (mid[i] + mid[i + 2] + walls(f) - 6.0 * f)
        return c

    lax.fori_loop(0, 3, component, 0)


def step_kernel(
    ids_ref, w_in, xy_in, gas_in, pv_in, cell_in, fill_in, rate_in, mass_in,
    flat, gout_ref, pout_ref,
    ids, w_ref, xy_ref, gas_ref, pv_ref, cell_ref, fill_ref, rate_ref, mass_ref,
    in_sem, out_sem,
    wall, halo, cnt, cnt_in, sm, cpair, hs, ob, dep, dep_out, dep_halo, mid,
    a1, s1, a2, s2, b2, b1, err, w3f, w3, scale,
    grad, pair_sum, in1_x, in1_y, in1_z, sum1_x, sum1_y, sum1_z, in2_x, in2_y, in2_z,
    sum1_v, in2_v,
    sum2_x, sum2_y, sum2_z, in3_x, in3_y, in3_z, fin, send_sem, recv_sem,
):
    x, y, z, core = coords()
    zh, zl = z // 2, z % 2
    g, d = lax.axis_index("grp"), lax.axis_index("dev")
    sibling = device(x, y, z, 1 - core)
    evo = evolves()
    net = Copies(send_sem, recv_sem)
    sent = []

    def push(src, dst, where):
        copy = net.start(src, dst, where)
        sent.append(copy)
        return copy

    def when_evolving(*steps):
        @pl.when(evo)
        def _():
            for step in steps:
                step()

    partners = all_partners()
    barrier = pltpu.get_barrier_semaphore()
    for partner in partners:
        pl.semaphore_signal(barrier, inc=1, device_id=partner, device_id_type=MESH)
    pairs_in = (
        (w_in, w_ref), (gas_in, gas_ref), (cell_in, cell_ref), (pv_in, pv_ref), (rate_in, rate_ref),
        (mass_in, mass_ref), (fill_in, fill_ref), (xy_in, xy_ref),
    )
    loads = [
        pltpu.make_async_copy(src, dst, in_sem.at[i]) for i, (src, dst) in enumerate(pairs_in)
    ]
    for load in loads:
        load.start()
    for n in range(BLK):
        ids[pl.ds(n, 1), :] = jnp.full((1, 128), ids_ref[n], jnp.int32)
    gas_same = pltpu.make_async_copy(gas_ref, gout_ref, out_sem.at[0])
    parcel_same = pltpu.make_async_copy(pv_ref, pout_ref, out_sem.at[1])

    loads[0].wait()
    for j in range(8):
        spread = w_ref[pl.ds(j, PIECE, stride=8), :]
        mixed = jnp.concatenate([spread[:32], w_ref[pl.ds(256 + 48 * j, 48), :]], axis=0)
        last = w_ref[pl.ds(PIECE * j, PIECE), :]
        mine_j = jnp.where(d == 15, last, jnp.where(d == 14, mixed, spread))
        wall[j, pl.ds(pl.multiple_of(d * PIECE, 16), PIECE), :] = mine_j.astype(BF16)
    lanes = lax.broadcasted_iota(jnp.int32, (BLK, 128), 1)
    mine = (ids[...] == lanes).astype(F32)
    cnt[0] = jnp.broadcast_to(jnp.sum(mine, axis=0, keepdims=True), (8, 128))
    pl.semaphore_wait(barrier, len(partners))

    def shard(px, pz, pc, j0, jn):
        first = pl.multiple_of((px * 4 + (pz % 2) * 2 + pc) * PIECE, 16)
        return wall.at[pl.ds(j0, jn), pl.ds(first, PIECE)]

    def give(px, pz, j0, jn, where):
        piece = shard(px, pz, core, j0, jn)
        return push(piece, piece, where)

    half = (y % 2) * 4
    zm = z + 1 - 2 * zl
    count_copy = push(cnt.at[0], cnt_in.at[0], sibling)
    from_z = [
        give(x, z, 0, 4, device(x, y, (z + 1) % 4, core)),
        give(x, z, 4, 4, device(x, y, (z + 3) % 4, core)),
    ]
    near_x = [give(x, z, half, 4, device((x + k) % 4, y, z, core)) for k in (1, 2, 3)]
    over = [give(x, z, 0, 8, sibling)]
    low = net.make(gas_ref.at[:, pl.ds(6, 2)], halo.at[:, pl.ds(0, 2)], slab_device(1))
    high = net.make(gas_ref.at[:, pl.ds(0, 2)], halo.at[:, pl.ds(2, 2)], slab_device(-1))

    def parcels(t):
        drag(t, pv_ref, cell_ref, fill_ref, rate_ref, mass_ref, pout_ref, sm, cpair, hs)

    for load in loads[1:]:
        load.wait()

    @pl.when(jnp.logical_not(evo))
    def _():
        gas_same.start()
        parcel_same.start()

    when_evolving(
        lambda: smooth(gas_ref, halo, sm, range(1, 7)),
        lambda: parcels(1),
        lambda: parcels(2),
    )
    count_copy.wait_recv()
    cnt[1] = cnt[0] + cnt_in[0]

    def count_send(axis, at, slot):
        return [
            push(cnt.at[at], cnt_in.at[slot + k], device(*on_axis(axis, x, y, z, k + 1), core))
            for k in range(3)
        ]

    def count_add(copies, at, slot):
        for copy in copies:
            copy.wait_recv()
        cnt[at + 1] = cnt[at] + cnt_in[slot] + cnt_in[slot + 1] + cnt_in[slot + 2]

    counting = count_send("y", 1, 1)
    for copy in from_z:
        copy.wait_recv()
    far_x = [give(x, zm, half, 4, device((x + k) % 4, y, z, core)) for k in (1, 2, 3)]
    over.append(give(x, zm, 0, 8, sibling))
    when_evolving(lambda: deposit(1, cpair, hs, ob, dep))

    up, down = device(x, (y + 1) % 4, z, core), device(x, (y + 3) % 4, z, core)
    from_y = []
    for pz, copies in ((z, near_x), (zm, far_x)):
        for k, copy in zip((1, 2, 3), copies):
            copy.wait_recv()
            px = (x + 4 - k) % 4
            from_y.append((px, pz, 0, give(px, pz, half, 2, up)))
            from_y.append((px, pz, 2, give(px, pz, half + 2, 2, down)))
            over.append(give(px, pz, half, 4, sibling))
        if pz is z:
            count_add(counting, 1, 1)
            counting = count_send("z", 2, 4)
            when_evolving(lambda: deposit(2, cpair, hs, ob, dep))
    count_add(counting, 2, 4)
    counting = count_send("x", 3, 7)
    other = 4 - half
    for px, pz, q, copy in from_y:
        copy.wait_recv()
        over.append(give(px, pz, other + q, 2, sibling))
    for copy in over:
        copy.wait_recv()

    when_evolving(low.start, high.start)
    count_add(counting, 3, 7)

    inverse = 1.0 / jnp.maximum(cnt[4, 0:1, :], 1.0)
    picked = jnp.where(ids[...] == lanes, inverse, 0.0)
    per_block = jnp.broadcast_to(jnp.sum(picked, axis=1, keepdims=True), (BLK, 128))
    for n in range(BLK):
        scale[pl.ds(16 * n, 16), :] = jnp.broadcast_to(per_block[n : n + 1], (16, 128))
    for j in range(8):
        w3[pl.ds(48 * j, 48), :] = wall[j, pl.ds(1152, 48), :]
        w3[pl.ds(384 + PIECE * j, PIECE), :] = wall[j, pl.ds(1200, PIECE), :]

    def columns(j, first, rows):
        return jnp.concatenate([wall[2 * j + i, pl.ds(first, rows), :] for i in range(2)], axis=1)

    def activate(pre, act, slope, j):
        s = 0.5 * jnp.tanh(0.5 * pre) + 0.5
        value = pre * s
        act[j] = value.astype(BF16)
        slope[j] = s + value * (1.0 - s)

    for j in range(4):
        activate(dot(xy_ref[:, 0:128], columns(j, 0, 128)), a1, s1, j)
    acts = jnp.concatenate([a1[i] for i in range(4)], axis=1)
    for j in range(4):
        activate(dot(acts, columns(j, 128, 1024)), a2, s2, j)
    acts = jnp.concatenate([a2[i] for i in range(4)], axis=1)
    predicted = dot(acts, w3[...])
    err[...] = ((predicted - xy_ref[:, 128:256].astype(F32)) * scale[...]).astype(BF16)

    for j in range(4):
        part = pl.ds(256 * j, 256)
        b2[j] = (dot(err[...], w3[part, :], ((1,), (1,))) * s2[j]).astype(BF16)
    for j in range(4):
        w3f[pl.ds(256 * j, 256), :] = dot(a2[j], err[...], ((0,), (0,)))
    for j in range(8):
        grad[j // 4, j % 4, pl.ds(1152, 48), :] = w3f[pl.ds(48 * j, 48), :]
        grad[j // 4, j % 4, pl.ds(1200, PIECE), :] = w3f[pl.ds(384 + PIECE * j, PIECE), :]

    def grad_second(i):
        for j in range(4):
            piece = dot(a1[i], b2[j], ((0,), (0,)))
            for e in range(2):
                n = 2 * j + e
                grad[n // 4, n % 4, pl.ds(128 + 256 * i, 256), :] = piece[:, 128 * e : 128 * e + 128]

    def back_first():
        backs = jnp.concatenate([b2[j] for j in range(4)], axis=1)
        for i in range(4):
            h0 = 128 + 256 * i
            rows = jnp.concatenate([wall[j, pl.ds(h0, 256), :] for j in range(8)], axis=1)
            b1[i] = (dot(backs, rows, ((1,), (1,))) * s1[i]).astype(BF16)

    def y_rows(px):
        return pl.ds(48, 32) if px % 2 else pl.ds(56, 24)

    def z_rows(px):
        return pl.ds(24, 24 if px % 2 else 32)

    pairs = {}

    def pair_start(px):
        pairs[px] = [
            push(
                grad.at[:, :, pl.ds(pl.multiple_of((px * 4 + q * 2 + 1 - core) * PIECE, 8), PIECE)],
                pair_sum.at[px, q],
                sibling,
            )
            for q in range(2)
        ]

    first_x = {}
    first_y, first_z = {}, {}

    def to_x(px, src, slots, sems):
        k = (px - x + 4) % 4
        slot = jnp.maximum(k - 1, 0)
        n = net.count
        net.count += 1
        copy = pltpu.make_async_remote_copy(
            src_ref=src,
            dst_ref=slots.at[slot],
            send_sem=send_sem.at[n],
            recv_sem=sems.at[slot],
            device_id=device(px, y, z, core),
            device_id_type=MESH,
        )

        @pl.when(k > 0)
        def _():
            copy.start()

        return copy

    def from_x(slots, sems):
        for k in range(3):
            pltpu.make_async_remote_copy(
                src_ref=slots.at[k],
                dst_ref=slots.at[k],
                send_sem=send_sem.at[0],
                recv_sem=sems.at[k],
                device_id=sibling,
                device_id_type=MESH,
            ).wait_recv()

    def pair_done(px):
        for q, copy in enumerate(pairs[px]):
            copy.wait_recv()
            own = pl.ds(pl.multiple_of((px * 4 + q * 2 + core) * PIECE, 8), PIECE)
            pair_sum[px, q] = pair_sum[px, q] + grad[:, :, own, :]
        first_x[px] = to_x(px, pair_sum.at[px, :, :, :, pl.ds(0, 24)], in1_x, recv_x)

        for k in (1, 2, 3):
            ny = (y + k) % 4
            first_y.setdefault(px, []).append(
                push(
                    pair_sum.at[px, :, :, ny, y_rows(px)],
                    in1_y.at[k - 1, px, :, :, pl.ds(0, y_rows(px).size)],
                    device(x, ny, z, core),
                )
            )
        for k in (1, 2, 3):
            nz = (z + k) % 4
            first_z.setdefault(px, []).append(
                push(
                    pair_sum.at[px, nz % 2, nz // 2, :, z_rows(px)],
                    in1_z.at[k - 1, px, :, pl.ds(0, z_rows(px).size)],
                    device(x, y, nz, core),
                )
            )

    second_y, second_v, sent_z = {}, {}, {}

    def second_phase(px):
        for copy in first_z[px]:
            copy.wait_recv()
        zn = z_rows(px).size
        total = pair_sum[px, zl, zh, :, z_rows(px), :]
        for k in range(3):
            total = total + in1_z[k, px, :, pl.ds(0, zn), :]
        sum1_z[px] = total[:, :24]
        sent_z[px] = to_x(px, sum1_z.at[px], in2_z, recv_z)
        if zn > 24:
            sum1_v[px // 2] = total[:, 24:]
            second_v[px] = [
                push(
                    sum1_v.at[px // 2, (y + k) % 4],
                    in2_v.at[k - 1, px // 2],
                    device(x, (y + k) % 4, z, core),
                )
                for k in (1, 2, 3)
            ]
        for copy in first_y[px]:
            copy.wait_recv()
        yn = y_rows(px).size
        total = pair_sum[px, :, :, y, y_rows(px), :]
        for k in range(3):
            total = total + in1_y[k, px, :, :, pl.ds(0, yn), :]
        sum1_y[px, :, :, pl.ds(0, yn), :] = total
        second_y[px] = []
        for k in (1, 2, 3):
            nz = (z + k) % 4
            second_y[px].append(
                push(
                    sum1_y.at[px, nz % 2, nz // 2, pl.ds(0, yn)],
                    in2_y.at[k - 1, px, pl.ds(0, yn)],
                    device(x, y, nz, core),
                )
            )

    def third_phase(px):
        for copy in second_y[px] + second_v.get(px, []):
            copy.wait_recv()
        yn = y_rows(px).size
        rows = pl.ds(0, yn)
        sum2_y[px, pl.ds(32 - yn, yn), :] = (
            sum1_y[px, zl, zh, rows, :]
            + in2_y[0, px, rows, :] + in2_y[1, px, rows, :] + in2_y[2, px, rows, :]
        )
        if yn == 24:
            e = px // 2
            sum2_y[px, pl.ds(0, 8), :] = sum1_v[e, y] + in2_v[0, e] + in2_v[1, e] + in2_v[2, e]
        sent_y[px] = to_x(px, sum2_y.at[px], in3_y, recv_y)

    sent_y = {}
    recv_x = recv_sem.at[pl.ds(RECV_X, 3)]
    recv_z = recv_sem.at[pl.ds(RECV_X + 3, 3)]
    recv_y = recv_sem.at[pl.ds(RECV_X + 6, 3)]
    grad_second(3)
    pair_start(3)
    grad_second(2)
    pair_start(2)
    grad_second(1)
    pair_done(3)
    grad_second(0)
    pair_start(1)
    pair_done(2)
    back_first()
    pair_done(1)
    for j in range(4):
        piece = dot(xy_ref[:, 0:128], b1[j], ((0,), (0,)))
        for e in range(2):
            n = 2 * j + e
            grad[n // 4, n % 4, pl.ds(0, 128), :] = piece[:, 128 * e : 128 * e + 128]
    pair_start(0)
    pair_done(0)

    def send_deposit():
        for k in range(3):
            for i in range(2):
                dep_out[0, k, i] = dep[k, pl.ds(128 * (6 + i), 128), :].astype(BF16)
                dep_out[1, k, i] = dep[k, pl.ds(128 * i, 128), :].astype(BF16)
        dep_low.start()
        dep_high.start()

    dep_low = net.make(dep_out.at[0], dep_halo.at[0], slab_device(1))
    dep_high = net.make(dep_out.at[1], dep_halo.at[1], slab_device(-1))
    when_evolving(
        low.wait,
        high.wait,
        lambda: smooth(gas_ref, halo, sm, (0, 7)),
        lambda: parcels(0),
        lambda: parcels(3),
        lambda: deposit(0, cpair, hs, ob, dep),
    )
    second_phase(3)
    second_phase(2)
    when_evolving(lambda: deposit(3, cpair, hs, ob, dep), send_deposit)
    second_phase(1)


    from_x(in1_x, recv_x)
    sum1_x[...] = pair_sum[x, :, :, :, pl.ds(0, 24), :] + in1_x[0] + in1_x[1] + in1_x[2]
    second_x = [
        push(sum1_x.at[:, :, (y + k) % 4], in2_x.at[k - 1], device(x, (y + k) % 4, z, core))
        for k in (1, 2, 3)
    ]
    second_phase(0)
    for copy in second_x:
        copy.wait_recv()
    sum2_x[...] = sum1_x[:, :, y] + in2_x[0] + in2_x[1] + in2_x[2]
    third_x = []
    for k in (1, 2, 3):
        nz = (z + k) % 4
        third_x.append(push(sum2_x.at[nz % 2, nz // 2], in3_x.at[k - 1], device(x, y, nz, core)))
    from_x(in2_z, recv_z)
    sum2_z[...] = sum1_z[x] + in2_z[0] + in2_z[1] + in2_z[2]
    third_z = [
        push(sum2_z.at[(y + k) % 4], in3_z.at[k - 1], device(x, (y + k) % 4, z, core))
        for k in (1, 2, 3)
    ]
    for px in (3, 2, 1, 0):
        third_phase(px)
    for copy in third_x + third_z:
        copy.wait_recv()
    fin[g, pl.ds(0, 24), :] = sum2_x[zl, zh] + in3_x[0] + in3_x[1] + in3_x[2]
    fin[g, pl.ds(24, 24), :] = sum2_z[y] + in3_z[0] + in3_z[1] + in3_z[2]

    def across_groups(rows):
        return [
            push(fin.at[g, rows], fin.at[g, rows], ((g + k) % 8, d)) for k in range(1, 8)
        ]

    from_x(in3_y, recv_y)
    fin[g, pl.ds(48, 32), :] = sum2_y[x] + in3_y[0] + in3_y[1] + in3_y[2]
    across = across_groups(pl.ds(0, 80))
    when_evolving(
        dep_low.wait,
        dep_high.wait,
        lambda: gas_second(gas_ref, halo, dep, dep_halo, gout_ref, mid),
    )

    for copy in across:
        copy.wait_recv()

    @pl.when(d < 14)
    def _():
        for j in range(8):
            flat[pl.ds(j, PIECE, stride=8), :] = fin[j]

    @pl.when(d == 14)
    def _():
        for j in range(8):
            flat[pl.ds(j, 32, stride=8), :] = fin[j, :32]
            flat[pl.ds(256 + 48 * j, 48), :] = fin[j, 32:]

    @pl.when(d == 15)
    def _():
        for j in range(8):
            flat[pl.ds(PIECE * j, PIECE), :] = fin[j]

    @pl.when(jnp.logical_not(evo))
    def _():
        gas_same.wait()
        parcel_same.wait()

    for copy in sent:
        copy.wait_send()
    for px in range(4):

        @pl.when(px != x)
        def _():
            first_x[px].wait_send()
            sent_z[px].wait_send()
            sent_y[px].wait_send()


def finish_kernel(
    grad, w, m, v, gas, parcels,
    w_out, m_out, v_out, gas_out, parcel_out,
    w_new, m_new, v_new, out_sem,
):
    results = (
        (gas, gas_out), (parcels, parcel_out), (m_new, m_out), (v_new, v_out), (w_new, w_out),
    )
    stores = [pltpu.make_async_copy(a, b, out_sem.at[i]) for i, (a, b) in enumerate(results)]
    for store in stores[:2]:
        store.start()
    gradient = grad[...]
    first_new = BETA_ONE * m[...] + (1.0 - BETA_ONE) * gradient
    second_new = BETA_TWO * v[...] + (1.0 - BETA_TWO) * gradient * gradient
    m_new[...] = first_new
    v_new[...] = second_new
    first_hat = first_new / (1.0 - BETA_ONE**ADAM_STEP)
    second_hat = second_new / (1.0 - BETA_TWO**ADAM_STEP)
    w_new[...] = w[...] - LEARN_RATE * first_hat / (jnp.sqrt(second_hat) + ADAM_EPS)
    for store in stores[2:]:
        store.start()
    for store in stores:
        store.wait()


def anywhere(count):
    return [pl.BlockSpec(memory_space=pl.ANY)] * count


def shards(
    gas_velocity, parcel_velocity, parcel_cell, block_fill, relax_rate, parcel_mass,
    sample_blocks, learner_ids, master_weights, first_moment, second_moment,
):
    shape = jax.ShapeDtypeStruct

    def buf(*dims, dtype=F32):
        return pltpu.VMEM(dims, dtype)

    scratch = [
        buf(BLK, 128, dtype=jnp.int32),
        buf(640, 128),
        buf(ROWS, 256, dtype=BF16),
        buf(3, 8, 128, 128),
        buf(3, 64, 1024),
        buf(64, 1024, dtype=jnp.int32),
        buf(1, 1024, dtype=jnp.int32),
        buf(64, 1024),
        buf(64, 1024),
        pltpu.SemaphoreType.DMA((8,)),
        pltpu.SemaphoreType.DMA((2,)),
        buf(8, 1280, 128, dtype=BF16),
        buf(3, 4, 128, 128),
        buf(5, 8, 128),
        buf(10, 8, 128),
        buf(3, 1024, 128),
        buf(512, 128, dtype=jnp.int32),
        buf(8192, 128),
        buf(4096, 128),
        buf(3, 1024, 128),
        buf(2, 3, 2, 128, 128, dtype=BF16),
        buf(2, 3, 2, 128, 128, dtype=BF16),
        buf(10, 128, 128),
        buf(4, ROWS, 256, dtype=BF16),
        buf(4, ROWS, 256),
        buf(4, ROWS, 256, dtype=BF16),
        buf(4, ROWS, 256),
        buf(4, ROWS, 256, dtype=BF16),
        buf(4, ROWS, 256, dtype=BF16),
        buf(ROWS, 128, dtype=BF16),
        buf(1024, 128),
        buf(1024, 128, dtype=BF16),
        buf(ROWS, 128),
        buf(2, 4, 1280, 128),
        buf(4, 2, 2, 4, PIECE, 128),
        buf(3, 2, 2, 4, 24, 128),
        buf(3, 4, 2, 2, 32, 128),
        buf(3, 4, 4, 32, 128),
        buf(2, 2, 4, 24, 128),
        buf(4, 2, 2, 32, 128),
        buf(4, 4, 24, 128),
        buf(3, 2, 2, 24, 128),
        buf(3, 4, 32, 128),
        buf(3, 4, 24, 128),
        buf(2, 4, 8, 128),
        buf(3, 2, 8, 128),
        buf(2, 2, 24, 128),
        buf(4, 32, 128),
        buf(4, 24, 128),
        buf(3, 24, 128),
        buf(3, 32, 128),
        buf(3, 24, 128),
        buf(8, PIECE, 128),
        pltpu.SemaphoreType.DMA((RECV_X,)),
        pltpu.SemaphoreType.DMA((RECV_X + 9,)),
    ]
    grads, gas_out, parcels = pl.pallas_call(
        step_kernel,
        name="step",
        out_shape=(
            buf(640, 128),
            buf(3, 8, 128, 128),
            buf(3, 64, 1024),
        ),
        in_specs=[pl.BlockSpec(memory_space=pltpu.SMEM)]
        + [pl.BlockSpec(memory_space=pltpu.HBM)] * 8,
        out_specs=tuple([pl.BlockSpec(memory_space=pltpu.VMEM)] * 3),
        scratch_shapes=scratch,
        compiler_params=pltpu.CompilerParams(
            collective_id=0, has_side_effects=True, vmem_limit_bytes=VMEM_LIMIT
        ),
    )(
        *[
            pltpu.with_memory_space_constraint(array, pltpu.HBM)
            for array in (
                learner_ids, master_weights, sample_blocks.reshape(ROWS, 256), gas_velocity[0],
                parcel_velocity[0], parcel_cell[0], block_fill, relax_rate[0], parcel_mass[0],
            )
        ],
    )
    state = shape((640, 128), F32)
    master_out, first_out, second_out, gas_out, parcels = pl.pallas_call(
        finish_kernel,
        name="finish",
        out_shape=(state, state, state, shape(gas_out.shape, F32), shape(parcels.shape, F32)),
        in_specs=[pl.BlockSpec(memory_space=pltpu.VMEM)] * 6,
        out_specs=tuple(anywhere(5)),
        scratch_shapes=[buf(640, 128) for _ in range(3)] + [pltpu.SemaphoreType.DMA((5,))],
        compiler_params=pltpu.CompilerParams(vmem_limit_bytes=16 * 1024 * 1024),
    )(grads, master_weights, first_moment, second_moment, gas_out, parcels)
    return gas_out[None], parcels[None], master_out, first_out, second_out


def solution(mesh):
    placed = (
        P("grp", None, "dev", None, None),
        P("grp", None, None, "dev"),
        P("grp", None, "dev"),
        P("grp", "dev"),
        P("grp", None, "dev"),
        P("grp", None, "dev"),
        P(("grp", "dev"), None, None),
        P(("grp", "dev")),
        P("dev", None),
        P("dev", None),
        P("dev", None),
    )
    return jax.shard_map(
        shards,
        mesh=mesh,
        in_specs=placed,
        out_specs=(
            P("grp", None, "dev", None, None),
            P("grp", None, None, "dev"),
            P("dev", None),
            P("dev", None),
            P("dev", None),
        ),
        check_vma=False,
    )
```

```python
import jax
import jax.numpy as jnp
from jax import lax
from jax.experimental import pallas as pl
from jax.experimental.pallas import tpu as pltpu
from jax.sharding import PartitionSpec as P

MESH = pl.DeviceIdType.MESH
F32 = jnp.float32
BF16 = jnp.bfloat16

KAPPA = 0.15
BETA_ONE = 0.9
BETA_TWO = 0.95
ADAM_EPS = 1e-08
LEARN_RATE = 0.001
ADAM_STEP = 10

BLK = 44
ROWS = 704
PIECE = 80
VMEM_LIMIT = 46 * 1024 * 1024
RECV_X = 150


def coords():
    g = lax.axis_index("grp")
    d = lax.axis_index("dev")
    z = (g // 4) * 2 + (d // 2) % 2
    return d // 4, g % 4, z, d % 2


def device(x, y, z, core):
    return ((z // 2) * 4 + y, x * 4 + (z % 2) * 2 + core)


def on_axis(axis, x, y, z, k):
    return (
        (x + k) % 4 if axis == "x" else x,
        (y + k) % 4 if axis == "y" else y,
        (z + k) % 4 if axis == "z" else z,
    )


def evolves():
    g = lax.axis_index("grp")
    return jnp.logical_not((g == 0) | (g == 4) | (g == 2))


class Copies:
    def __init__(self, send_sem, recv_sem):
        self.send_sem, self.recv_sem = send_sem, recv_sem
        self.count = 0

    def make(self, src, dst, where):
        n = self.count
        self.count += 1
        return pltpu.make_async_remote_copy(
            src_ref=src,
            dst_ref=dst,
            send_sem=self.send_sem.at[n],
            recv_sem=self.recv_sem.at[n],
            device_id=where,
            device_id_type=MESH,
        )

    def start(self, src, dst, where):
        copy = self.make(src, dst, where)
        copy.start()
        return copy


def slab_device(step):
    d = lax.axis_index("dev")
    return (lax.axis_index("grp"), (d + step + 16) % 16)


def all_partners():
    x, y, z, core = coords()
    found = [device(x, y, z, 1 - core)]
    for axis in ("x", "y", "z"):
        for k in (1, 2, 3):
            found.append(device(*on_axis(axis, x, y, z, k), core))
    g, d = lax.axis_index("grp"), lax.axis_index("dev")
    found.append((g, (d + 15 + 2 * core) % 16))
    found += [device(x, (y + k) % 4, (z + 2) % 4, core) for k in (1, 2, 3)]
    return found


def dot(left, right, dims=((1,), (0,))):
    return lax.dot_general(left, right, (dims, ((), ())), preferred_element_type=F32)


def smooth(gas_ref, halo_ref, sm, layers):
    for k in range(3):
        for i in layers:
            lower = halo_ref[k, 1] if i == 0 else gas_ref[k, i - 1]
            upper = halo_ref[k, 2] if i == 7 else gas_ref[k, i + 1]
            sm[k, pl.ds(i * 128, 128), :] = 0.5 * gas_ref[k, i] + 0.25 * (lower + upper)


def drag(t, pv_ref, cell_ref, fill_ref, rate_ref, mass_ref, pout_ref, sm, cpair, hs):
    lane = lax.broadcasted_iota(jnp.int32, (128, 128), 1)
    slots = lax.broadcasted_iota(jnp.int32, (64, 128), 0)
    left_lanes = lane < 64
    cols = (pl.ds(t * 128, 128), pl.ds(t * 128 + 512, 128))
    index = jnp.concatenate([cell_ref[:, c] for c in cols], axis=0).T
    cpair[cols[0], :] = index
    for k in range(3):
        found = [
            jnp.take_along_axis(sm[k, c, :], index, axis=1, mode="promise_in_bounds") for c in cols
        ]
        gas_at = jnp.where(left_lanes, found[0], found[1]).T
        hands = []
        for side, c in enumerate(cols):
            velocity, rate = pv_ref[k, :, c], rate_ref[:, c]
            live = slots < fill_ref[:, c]
            relaxed = (velocity + rate * gas_at[64 * side : 64 * side + 64]) / (1.0 + rate)
            pout_ref[k, :, c] = jnp.where(live, relaxed, velocity)
            hands.append(jnp.where(live, mass_ref[:, c] * (velocity - relaxed), 0.0))
        handed = jnp.concatenate(hands, axis=0).T
        coarse = handed.astype(BF16).astype(F32)
        fine = handed - coarse
        base = t * 2048
        for first, part in ((0, coarse), (8, fine)):
            hs[pl.ds(base + first + k, 128, stride=16), :] = jnp.where(left_lanes, part, 0.0)
            hs[pl.ds(base + first + 3 + k, 128, stride=16), :] = jnp.where(left_lanes, 0.0, part)
    zero = jnp.zeros((128, 128), F32)
    for row in (6, 7, 14, 15):
        hs[pl.ds(t * 2048 + row, 128, stride=16), :] = zero


def deposit(t, cpair, hs, ob, dep):
    cells = lax.broadcasted_iota(jnp.int32, (128, 128), 0)
    upper_rows = lax.broadcasted_iota(jnp.int32, (32, 128), 0) < 16

    def several(step, carry):
        for u in range(32):
            b = t * 64 + step * 32 + u
            values = hs[pl.ds(pl.multiple_of(b * 32, 32), 32), :]
            left = jnp.concatenate(
                [jnp.where(upper_rows, values, 0.0), jnp.where(upper_rows, 0.0, values)], axis=1
            ).astype(BF16)
            hot = jnp.concatenate(
                [
                    (cells == cpair[pl.ds(2 * b + i, 1), :]).astype(F32).astype(BF16)
                    for i in range(2)
                ],
                axis=1,
            )
            out = dot(left, hot, ((1,), (1,)))
            ob[pl.ds(pl.multiple_of(b * 16, 16), 16), :] = jnp.concatenate(
                [out[0:8] + out[8:16], out[16:24] + out[24:32]], axis=0
            )
        return carry

    lax.fori_loop(0, 2, several, 0)
    for k in range(3):
        for side in range(2):
            dep[k, pl.ds(512 * side + 128 * t, 128), :] = ob[
                pl.ds(1024 * t + 3 * side + k, 128, stride=8), :
            ]


def gas_second(gas_ref, halo_ref, dep_ref, dep_halo, gout_ref, mid):
    row = lax.broadcasted_iota(jnp.int32, (128, 128), 0)
    col = lax.broadcasted_iota(jnp.int32, (128, 128), 1)

    def walls(f):
        return (
            jnp.where(row == 0, 0.0, pltpu.roll(f, 1, 0))
            + jnp.where(row == 127, 0.0, pltpu.roll(f, 127, 0))
            + jnp.where(col == 0, 0.0, pltpu.roll(f, 1, 1))
            + jnp.where(col == 127, 0.0, pltpu.roll(f, 127, 1))
        )

    def component(k, c):
        def gas(i):
            if i < 0:
                return halo_ref[k, i + 2]
            return gas_ref[k, i] if i < 8 else halo_ref[k, i - 6]

        def dep(i):
            if i < 0:
                return dep_halo[0, k, i + 2].astype(F32)
            if i < 8:
                return dep_ref[k, pl.ds(i * 128, 128), :]
            return dep_halo[1, k, i - 8].astype(F32)

        for i in range(-1, 9):
            f = gas(i)
            step = f + KAPPA * (gas(i - 1) + gas(i + 1) + walls(f) - 6.0 * f)
            mid[i + 1] = step + 0.5 * dep(i) + 0.25 * (dep(i - 1) + dep(i + 1))
        for i in range(8):
            f = mid[i + 1]
            gout_ref[k, i] = f + KAPPA * (mid[i] + mid[i + 2] + walls(f) - 6.0 * f)
        return c

    lax.fori_loop(0, 3, component, 0)


def step_kernel(
    ids_ref, w_in, xy_in, gas_in, pv_in, cell_in, fill_in, rate_in, mass_in,
    flat, gout_ref, pout_ref,
    ids, w_ref, xy_ref, gas_ref, pv_ref, cell_ref, fill_ref, rate_ref, mass_ref,
    in_sem, out_sem,
    wall, halo, cnt, cnt_in, sm, cpair, hs, ob, dep, dep_out, dep_halo, mid,
    a1, s1, a2, s2, b2, b1, err, w3f, w3, scale,
    grad, pair_sum, in1_x, in1_y, in1_z, sum1_x, sum1_y, sum1_z, in2_x, in2_y, in2_z,
    sum1_v, in2_v,
    sum2_x, sum2_y, sum2_z, in3_x, in3_y, in3_z, fin, spread_out, send_sem, recv_sem,
):
    x, y, z, core = coords()
    zh, zl = z // 2, z % 2
    g, d = lax.axis_index("grp"), lax.axis_index("dev")
    sibling = device(x, y, z, 1 - core)
    evo = evolves()
    net = Copies(send_sem, recv_sem)
    sent = []

    def push(src, dst, where):
        copy = net.start(src, dst, where)
        sent.append(copy)
        return copy

    def when_evolving(*steps):
        @pl.when(evo)
        def _():
            for step in steps:
                step()

    partners = all_partners()
    barrier = pltpu.get_barrier_semaphore()
    for partner in partners:
        pl.semaphore_signal(barrier, inc=1, device_id=partner, device_id_type=MESH)
    pairs_in = (
        (w_in, w_ref.at[pl.ds(0, 640)]), (gas_in, gas_ref), (cell_in, cell_ref), (pv_in, pv_ref), (rate_in, rate_ref),
        (mass_in, mass_ref), (fill_in, fill_ref), (xy_in, xy_ref),
    )
    loads = [
        pltpu.make_async_copy(src, dst, in_sem.at[i]) for i, (src, dst) in enumerate(pairs_in)
    ]
    for load in loads:
        load.start()
    for n in range(BLK):
        ids[pl.ds(n, 1), :] = jnp.full((1, 128), ids_ref[n], jnp.int32)
    gas_same = pltpu.make_async_copy(gas_ref, gout_ref, out_sem.at[0])
    parcel_same = pltpu.make_async_copy(pv_ref, pout_ref, out_sem.at[1])

    loads[0].wait()
    for j in range(8):
        spread = w_ref[pl.ds(j, PIECE, stride=8), :]
        mixed = jnp.concatenate([spread[:32], w_ref[pl.ds(256 + 48 * j, 48), :]], axis=0)
        last = w_ref[pl.ds(PIECE * j, PIECE), :]
        mine_j = jnp.where(d == 15, last, jnp.where(d == 14, mixed, spread))
        wall[j, pl.ds(pl.multiple_of(d * PIECE, 16), PIECE), :] = mine_j.astype(BF16)
    lanes = lax.broadcasted_iota(jnp.int32, (BLK, 128), 1)
    mine = (ids[...] == lanes).astype(F32)
    cnt[0] = jnp.broadcast_to(jnp.sum(mine, axis=0, keepdims=True), (8, 128))
    pl.semaphore_wait(barrier, len(partners))

    def shard(px, pz, pc, j0, jn):
        first = pl.multiple_of((px * 4 + (pz % 2) * 2 + pc) * PIECE, 16)
        return wall.at[pl.ds(j0, jn), pl.ds(first, PIECE)]

    def give(px, pz, j0, jn, where):
        piece = shard(px, pz, core, j0, jn)
        return push(piece, piece, where)

    half = (y % 2) * 4
    zm = z + 1 - 2 * zl
    count_copy = push(cnt.at[0], cnt_in.at[0], sibling)
    from_z = [
        give(x, z, 0, 4, device(x, y, (z + 1) % 4, core)),
        give(x, z, 4, 4, device(x, y, (z + 3) % 4, core)),
    ]
    near_x = [give(x, z, half, 4, device((x + k) % 4, y, z, core)) for k in (1, 2, 3)]
    over = [give(x, z, 0, 8, sibling)]
    low = net.make(gas_ref.at[:, pl.ds(6, 2)], halo.at[:, pl.ds(0, 2)], slab_device(1))
    high = net.make(gas_ref.at[:, pl.ds(0, 2)], halo.at[:, pl.ds(2, 2)], slab_device(-1))

    def parcels(t):
        drag(t, pv_ref, cell_ref, fill_ref, rate_ref, mass_ref, pout_ref, sm, cpair, hs)

    for load in loads[1:]:
        load.wait()

    @pl.when(jnp.logical_not(evo))
    def _():
        gas_same.start()
        parcel_same.start()

    when_evolving(
        lambda: smooth(gas_ref, halo, sm, range(1, 7)),
        lambda: parcels(1),
        lambda: parcels(2),
    )
    count_copy.wait_recv()
    cnt[1] = cnt[0] + cnt_in[0]

    def count_send(axis, at, slot):
        return [
            push(cnt.at[at], cnt_in.at[slot + k], device(*on_axis(axis, x, y, z, k + 1), core))
            for k in range(3)
        ]

    def count_add(copies, at, slot):
        for copy in copies:
            copy.wait_recv()
        cnt[at + 1] = cnt[at] + cnt_in[slot] + cnt_in[slot + 1] + cnt_in[slot + 2]

    counting = count_send("y", 1, 1)
    for copy in from_z:
        copy.wait_recv()
    far_x = [give(x, zm, half, 4, device((x + k) % 4, y, z, core)) for k in (1, 2, 3)]
    over.append(give(x, zm, 0, 8, sibling))
    when_evolving(lambda: deposit(1, cpair, hs, ob, dep))

    up, down = device(x, (y + 1) % 4, z, core), device(x, (y + 3) % 4, z, core)
    from_y = []
    for pz, copies in ((z, near_x), (zm, far_x)):
        for k, copy in zip((1, 2, 3), copies):
            copy.wait_recv()
            px = (x + 4 - k) % 4
            from_y.append((px, pz, 0, give(px, pz, half, 2, up)))
            from_y.append((px, pz, 2, give(px, pz, half + 2, 2, down)))
            over.append(give(px, pz, half, 4, sibling))
        if pz is z:
            count_add(counting, 1, 1)
            counting = count_send("z", 2, 4)
            when_evolving(lambda: deposit(2, cpair, hs, ob, dep))
    count_add(counting, 2, 4)
    counting = count_send("x", 3, 7)
    other = 4 - half
    for px, pz, q, copy in from_y:
        copy.wait_recv()
        over.append(give(px, pz, other + q, 2, sibling))
    for copy in over:
        copy.wait_recv()

    when_evolving(low.start, high.start)
    count_add(counting, 3, 7)

    inverse = 1.0 / jnp.maximum(cnt[4, 0:1, :], 1.0)
    picked = jnp.where(ids[...] == lanes, inverse, 0.0)
    per_block = jnp.broadcast_to(jnp.sum(picked, axis=1, keepdims=True), (BLK, 128))
    for n in range(BLK):
        scale[pl.ds(16 * n, 16), :] = jnp.broadcast_to(per_block[n : n + 1], (16, 128))
    for j in range(8):
        w3[pl.ds(48 * j, 48), :] = wall[j, pl.ds(1152, 48), :]
        w3[pl.ds(384 + PIECE * j, PIECE), :] = wall[j, pl.ds(1200, PIECE), :]

    def columns(j, first, rows):
        return jnp.concatenate([wall[2 * j + i, pl.ds(first, rows), :] for i in range(2)], axis=1)

    def activate(pre, act, slope, j):
        s = 0.5 * jnp.tanh(0.5 * pre) + 0.5
        value = pre * s
        act[j] = value.astype(BF16)
        slope[j] = s + value * (1.0 - s)

    for j in range(4):
        activate(dot(xy_ref[:, 0:128], columns(j, 0, 128)), a1, s1, j)
    acts = jnp.concatenate([a1[i] for i in range(4)], axis=1)
    for j in range(4):
        activate(dot(acts, columns(j, 128, 1024)), a2, s2, j)
    acts = jnp.concatenate([a2[i] for i in range(4)], axis=1)
    predicted = dot(acts, w3[...])
    err[...] = ((predicted - xy_ref[:, 128:256].astype(F32)) * scale[...]).astype(BF16)

    for j in range(4):
        part = pl.ds(256 * j, 256)
        b2[j] = (dot(err[...], w3[part, :], ((1,), (1,))) * s2[j]).astype(BF16)
    for j in range(4):
        w3f[pl.ds(256 * j, 256), :] = dot(a2[j], err[...], ((0,), (0,)))
    for j in range(8):
        grad[j // 4, j % 4, pl.ds(1152, 48), :] = w3f[pl.ds(48 * j, 48), :]
        grad[j // 4, j % 4, pl.ds(1200, PIECE), :] = w3f[pl.ds(384 + PIECE * j, PIECE), :]

    def grad_second(i):
        for j in range(4):
            piece = dot(a1[i], b2[j], ((0,), (0,)))
            for e in range(2):
                n = 2 * j + e
                grad[n // 4, n % 4, pl.ds(128 + 256 * i, 256), :] = piece[:, 128 * e : 128 * e + 128]

    def back_first():
        backs = jnp.concatenate([b2[j] for j in range(4)], axis=1)
        for i in range(4):
            h0 = 128 + 256 * i
            rows = jnp.concatenate([wall[j, pl.ds(h0, 256), :] for j in range(8)], axis=1)
            b1[i] = (dot(backs, rows, ((1,), (1,))) * s1[i]).astype(BF16)

    def y_rows(px):
        return pl.ds(48, 32) if px % 2 else pl.ds(56, 24)

    def z_rows(px):
        return pl.ds(24, 24 if px % 2 else 32)

    pairs = {}

    def pair_start(px):
        pairs[px] = [
            push(
                grad.at[:, :, pl.ds(pl.multiple_of((px * 4 + q * 2 + 1 - core) * PIECE, 8), PIECE)],
                pair_sum.at[px, q],
                sibling,
            )
            for q in range(2)
        ]

    first_x = {}
    first_y, first_z = {}, {}

    def to_x(px, src, slots, sems):
        k = (px - x + 4) % 4
        slot = jnp.maximum(k - 1, 0)
        n = net.count
        net.count += 1
        copy = pltpu.make_async_remote_copy(
            src_ref=src,
            dst_ref=slots.at[slot],
            send_sem=send_sem.at[n],
            recv_sem=sems.at[slot],
            device_id=device(px, y, z, core),
            device_id_type=MESH,
        )

        @pl.when(k > 0)
        def _():
            copy.start()

        return copy

    def from_x(slots, sems):
        for k in range(3):
            pltpu.make_async_remote_copy(
                src_ref=slots.at[k],
                dst_ref=slots.at[k],
                send_sem=send_sem.at[0],
                recv_sem=sems.at[k],
                device_id=sibling,
                device_id_type=MESH,
            ).wait_recv()

    def pair_done(px):
        for q, copy in enumerate(pairs[px]):
            copy.wait_recv()
            own = pl.ds(pl.multiple_of((px * 4 + q * 2 + core) * PIECE, 8), PIECE)
            pair_sum[px, q] = pair_sum[px, q] + grad[:, :, own, :]
        first_x[px] = to_x(px, pair_sum.at[px, :, :, :, pl.ds(0, 24)], in1_x, recv_x)

        for k in (1, 2, 3):
            ny = (y + k) % 4
            first_y.setdefault(px, []).append(
                push(
                    pair_sum.at[px, :, :, ny, y_rows(px)],
                    in1_y.at[k - 1, px, :, :, pl.ds(0, y_rows(px).size)],
                    device(x, ny, z, core),
                )
            )
        for k in (1, 2, 3):
            nz = (z + k) % 4
            first_z.setdefault(px, []).append(
                push(
                    pair_sum.at[px, nz % 2, nz // 2, :, z_rows(px)],
                    in1_z.at[k - 1, px, :, pl.ds(0, z_rows(px).size)],
                    device(x, y, nz, core),
                )
            )

    second_y, second_v, sent_z = {}, {}, {}

    def second_phase(px):
        for copy in first_z[px]:
            copy.wait_recv()
        zn = z_rows(px).size
        total = pair_sum[px, zl, zh, :, z_rows(px), :]
        for k in range(3):
            total = total + in1_z[k, px, :, pl.ds(0, zn), :]
        sum1_z[px] = total[:, :24]
        sent_z[px] = to_x(px, sum1_z.at[px], in2_z, recv_z)
        if zn > 24:
            sum1_v[px // 2] = total[:, 24:]
            second_v[px] = [
                push(
                    sum1_v.at[px // 2, (y + k) % 4],
                    in2_v.at[k - 1, px // 2],
                    device(x, (y + k) % 4, z, core),
                )
                for k in (1, 2, 3)
            ]
        for copy in first_y[px]:
            copy.wait_recv()
        yn = y_rows(px).size
        total = pair_sum[px, :, :, y, y_rows(px), :]
        for k in range(3):
            total = total + in1_y[k, px, :, :, pl.ds(0, yn), :]
        sum1_y[px, :, :, pl.ds(0, yn), :] = total
        second_y[px] = []
        for k in (1, 2, 3):
            nz = (z + k) % 4
            second_y[px].append(
                push(
                    sum1_y.at[px, nz % 2, nz // 2, pl.ds(0, yn)],
                    in2_y.at[k - 1, px, pl.ds(0, yn)],
                    device(x, y, nz, core),
                )
            )

    def third_phase(px):
        for copy in second_y[px] + second_v.get(px, []):
            copy.wait_recv()
        yn = y_rows(px).size
        rows = pl.ds(0, yn)
        sum2_y[px, pl.ds(32 - yn, yn), :] = (
            sum1_y[px, zl, zh, rows, :]
            + in2_y[0, px, rows, :] + in2_y[1, px, rows, :] + in2_y[2, px, rows, :]
        )
        if yn == 24:
            e = px // 2
            sum2_y[px, pl.ds(0, 8), :] = sum1_v[e, y] + in2_v[0, e] + in2_v[1, e] + in2_v[2, e]
        sent_y[px] = to_x(px, sum2_y.at[px], in3_y, recv_y)

    sent_y = {}
    recv_x = recv_sem.at[pl.ds(RECV_X, 3)]
    recv_z = recv_sem.at[pl.ds(RECV_X + 3, 3)]
    recv_y = recv_sem.at[pl.ds(RECV_X + 6, 3)]
    grad_second(3)
    pair_start(3)
    grad_second(2)
    pair_start(2)
    grad_second(1)
    pair_done(3)
    grad_second(0)
    pair_start(1)
    pair_done(2)
    back_first()
    pair_done(1)
    for j in range(4):
        piece = dot(xy_ref[:, 0:128], b1[j], ((0,), (0,)))
        for e in range(2):
            n = 2 * j + e
            grad[n // 4, n % 4, pl.ds(0, 128), :] = piece[:, 128 * e : 128 * e + 128]
    pair_start(0)
    pair_done(0)

    def send_deposit():
        for k in range(3):
            for i in range(2):
                dep_out[0, k, i] = dep[k, pl.ds(128 * (6 + i), 128), :].astype(BF16)
                dep_out[1, k, i] = dep[k, pl.ds(128 * i, 128), :].astype(BF16)
        dep_low.start()
        dep_high.start()

    dep_low = net.make(dep_out.at[0], dep_halo.at[0], slab_device(1))
    dep_high = net.make(dep_out.at[1], dep_halo.at[1], slab_device(-1))
    when_evolving(
        low.wait,
        high.wait,
        lambda: smooth(gas_ref, halo, sm, (0, 7)),
        lambda: parcels(0),
        lambda: parcels(3),
        lambda: deposit(0, cpair, hs, ob, dep),
    )
    second_phase(3)
    second_phase(2)
    when_evolving(lambda: deposit(3, cpair, hs, ob, dep), send_deposit)
    second_phase(1)


    from_x(in1_x, recv_x)
    sum1_x[...] = pair_sum[x, :, :, :, pl.ds(0, 24), :] + in1_x[0] + in1_x[1] + in1_x[2]
    second_x = [
        push(sum1_x.at[:, :, (y + k) % 4], in2_x.at[k - 1], device(x, (y + k) % 4, z, core))
        for k in (1, 2, 3)
    ]
    second_phase(0)
    for copy in second_x:
        copy.wait_recv()
    sum2_x[...] = sum1_x[:, :, y] + in2_x[0] + in2_x[1] + in2_x[2]
    third_x = []
    for k in (1, 2, 3):
        nz = (z + k) % 4
        third_x.append(push(sum2_x.at[nz % 2, nz // 2], in3_x.at[k - 1], device(x, y, nz, core)))
    from_x(in2_z, recv_z)
    sum2_z[...] = sum1_z[x] + in2_z[0] + in2_z[1] + in2_z[2]
    third_z = [
        push(sum2_z.at[(y + k) % 4], in3_z.at[k - 1], device(x, (y + k) % 4, z, core))
        for k in (1, 2, 3)
    ]
    for px in (3, 2, 1, 0):
        third_phase(px)
    for copy in third_x + third_z:
        copy.wait_recv()
    fin[g, pl.ds(0, 24), :] = sum2_x[zl, zh] + in3_x[0] + in3_x[1] + in3_x[2]
    fin[g, pl.ds(24, 24), :] = sum2_z[y] + in3_z[0] + in3_z[1] + in3_z[2]

    def across_groups(rows):
        return [
            push(fin.at[g, rows], fin.at[g, rows], ((g + k) % 8, d)) for k in range(1, 8)
        ]

    from_x(in3_y, recv_y)
    fin[g, pl.ds(48, 32), :] = sum2_y[x] + in3_y[0] + in3_y[1] + in3_y[2]
    across = across_groups(pl.ds(0, 80))
    when_evolving(
        dep_low.wait,
        dep_high.wait,
        lambda: gas_second(gas_ref, halo, dep, dep_halo, gout_ref, mid),
    )

    for copy in across:
        copy.wait_recv()

    @pl.when(d < 14)
    def _():
        for j in range(8):
            spread_out[pl.ds(j, PIECE, stride=8), :] = fin[j]
        flat[...] = spread_out[pl.ds(0, 640), :]

    @pl.when(d == 14)
    def _():
        for j in range(8):
            flat[pl.ds(j, 32, stride=8), :] = fin[j, :32]
            flat[pl.ds(256 + 48 * j, 48), :] = fin[j, 32:]

    @pl.when(d == 15)
    def _():
        for j in range(8):
            flat[pl.ds(PIECE * j, PIECE), :] = fin[j]

    @pl.when(jnp.logical_not(evo))
    def _():
        gas_same.wait()
        parcel_same.wait()

    for copy in sent:
        copy.wait_send()
    for px in range(4):

        @pl.when(px != x)
        def _():
            first_x[px].wait_send()
            sent_z[px].wait_send()
            sent_y[px].wait_send()


def finish_kernel(
    grad, w, m, v, gas, parcels,
    w_out, m_out, v_out, gas_out, parcel_out,
    w_new, m_new, v_new, out_sem,
):
    results = (
        (gas, gas_out), (parcels, parcel_out), (m_new, m_out), (v_new, v_out), (w_new, w_out),
    )
    stores = [pltpu.make_async_copy(a, b, out_sem.at[i]) for i, (a, b) in enumerate(results)]
    for store in stores[:2]:
        store.start()
    gradient = grad[...]
    first_new = BETA_ONE * m[...] + (1.0 - BETA_ONE) * gradient
    second_new = BETA_TWO * v[...] + (1.0 - BETA_TWO) * gradient * gradient
    m_new[...] = first_new
    v_new[...] = second_new
    first_hat = first_new / (1.0 - BETA_ONE**ADAM_STEP)
    second_hat = second_new / (1.0 - BETA_TWO**ADAM_STEP)
    w_new[...] = w[...] - LEARN_RATE * first_hat / (jnp.sqrt(second_hat) + ADAM_EPS)
    for store in stores[2:]:
        store.start()
    for store in stores:
        store.wait()


def anywhere(count):
    return [pl.BlockSpec(memory_space=pl.ANY)] * count


def shards(
    gas_velocity, parcel_velocity, parcel_cell, block_fill, relax_rate, parcel_mass,
    sample_blocks, learner_ids, master_weights, first_moment, second_moment,
):
    shape = jax.ShapeDtypeStruct

    def buf(*dims, dtype=F32):
        return pltpu.VMEM(dims, dtype)

    scratch = [
        buf(BLK, 128, dtype=jnp.int32),
        buf(648, 128),
        buf(ROWS, 256, dtype=BF16),
        buf(3, 8, 128, 128),
        buf(3, 64, 1024),
        buf(64, 1024, dtype=jnp.int32),
        buf(1, 1024, dtype=jnp.int32),
        buf(64, 1024),
        buf(64, 1024),
        pltpu.SemaphoreType.DMA((8,)),
        pltpu.SemaphoreType.DMA((2,)),
        buf(8, 1280, 128, dtype=BF16),
        buf(3, 4, 128, 128),
        buf(5, 8, 128),
        buf(10, 8, 128),
        buf(3, 1024, 128),
        buf(512, 128, dtype=jnp.int32),
        buf(8208, 128),
        buf(4112, 128),
        buf(3, 1024, 128),
        buf(2, 3, 2, 128, 128, dtype=BF16),
        buf(2, 3, 2, 128, 128, dtype=BF16),
        buf(10, 128, 128),
        buf(4, ROWS, 256, dtype=BF16),
        buf(4, ROWS, 256),
        buf(4, ROWS, 256, dtype=BF16),
        buf(4, ROWS, 256),
        buf(4, ROWS, 256, dtype=BF16),
        buf(4, ROWS, 256, dtype=BF16),
        buf(ROWS, 128, dtype=BF16),
        buf(1024, 128),
        buf(1024, 128, dtype=BF16),
        buf(ROWS, 128),
        buf(2, 4, 1280, 128),
        buf(4, 2, 2, 4, PIECE, 128),
        buf(3, 2, 2, 4, 24, 128),
        buf(3, 4, 2, 2, 32, 128),
        buf(3, 4, 4, 32, 128),
        buf(2, 2, 4, 24, 128),
        buf(4, 2, 2, 32, 128),
        buf(4, 4, 24, 128),
        buf(3, 2, 2, 24, 128),
        buf(3, 4, 32, 128),
        buf(3, 4, 24, 128),
        buf(2, 4, 8, 128),
        buf(3, 2, 8, 128),
        buf(2, 2, 24, 128),
        buf(4, 32, 128),
        buf(4, 24, 128),
        buf(3, 24, 128),
        buf(3, 32, 128),
        buf(3, 24, 128),
        buf(8, PIECE, 128),
        buf(648, 128),
        pltpu.SemaphoreType.DMA((RECV_X,)),
        pltpu.SemaphoreType.DMA((RECV_X + 9,)),
    ]
    grads, gas_out, parcels = pl.pallas_call(
        step_kernel,
        name="step",
        out_shape=(
            buf(640, 128),
            buf(3, 8, 128, 128),
            buf(3, 64, 1024),
        ),
        in_specs=[pl.BlockSpec(memory_space=pltpu.SMEM)]
        + [pl.BlockSpec(memory_space=pltpu.HBM)] * 8,
        out_specs=tuple([pl.BlockSpec(memory_space=pltpu.VMEM)] * 3),
        scratch_shapes=scratch,
        compiler_params=pltpu.CompilerParams(
            collective_id=0, has_side_effects=True, vmem_limit_bytes=VMEM_LIMIT
        ),
    )(
        *[
            pltpu.with_memory_space_constraint(array, pltpu.HBM)
            for array in (
                learner_ids, master_weights, sample_blocks.reshape(ROWS, 256), gas_velocity[0],
                parcel_velocity[0], parcel_cell[0], block_fill, relax_rate[0], parcel_mass[0],
            )
        ],
    )
    state = shape((640, 128), F32)
    master_out, first_out, second_out, gas_out, parcels = pl.pallas_call(
        finish_kernel,
        name="finish",
        out_shape=(state, state, state, shape(gas_out.shape, F32), shape(parcels.shape, F32)),
        in_specs=[pl.BlockSpec(memory_space=pltpu.VMEM)] * 6,
        out_specs=tuple(anywhere(5)),
        scratch_shapes=[buf(640, 128) for _ in range(3)] + [pltpu.SemaphoreType.DMA((5,))],
        compiler_params=pltpu.CompilerParams(vmem_limit_bytes=16 * 1024 * 1024),
    )(grads, master_weights, first_moment, second_moment, gas_out, parcels)
    return gas_out[None], parcels[None], master_out, first_out, second_out


def solution(mesh):
    placed = (
        P("grp", None, "dev", None, None),
        P("grp", None, None, "dev"),
        P("grp", None, "dev"),
        P("grp", "dev"),
        P("grp", None, "dev"),
        P("grp", None, "dev"),
        P(("grp", "dev"), None, None),
        P(("grp", "dev")),
        P("dev", None),
        P("dev", None),
        P("dev", None),
    )
    return jax.shard_map(
        shards,
        mesh=mesh,
        in_specs=placed,
        out_specs=(
            P("grp", None, "dev", None, None),
            P("grp", None, None, "dev"),
            P("dev", None),
            P("dev", None),
            P("dev", None),
        ),
        check_vma=False,
    )
```

```python
import jax
import jax.numpy as jnp
from jax import lax
from jax.experimental import pallas as pl
from jax.experimental.pallas import tpu as pltpu
from jax.sharding import PartitionSpec as P

MESH = pl.DeviceIdType.MESH
F32 = jnp.float32
BF16 = jnp.bfloat16

KAPPA = 0.15
BETA_ONE = 0.9
BETA_TWO = 0.95
ADAM_EPS = 1e-08
LEARN_RATE = 0.001
ADAM_STEP = 10

BLK = 44
ROWS = 704
PIECE = 80
VMEM_LIMIT = 46 * 1024 * 1024
RECV_X = 150


def coords():
    g = lax.axis_index("grp")
    d = lax.axis_index("dev")
    z = (g // 4) * 2 + (d // 2) % 2
    return d // 4, g % 4, z, d % 2


def device(x, y, z, core):
    return ((z // 2) * 4 + y, x * 4 + (z % 2) * 2 + core)


def on_axis(axis, x, y, z, k):
    return (
        (x + k) % 4 if axis == "x" else x,
        (y + k) % 4 if axis == "y" else y,
        (z + k) % 4 if axis == "z" else z,
    )


def evolves():
    g = lax.axis_index("grp")
    return jnp.logical_not((g == 0) | (g == 4) | (g == 2))


class Copies:
    def __init__(self, send_sem, recv_sem):
        self.send_sem, self.recv_sem = send_sem, recv_sem
        self.count = 0

    def make(self, src, dst, where):
        n = self.count
        self.count += 1
        return pltpu.make_async_remote_copy(
            src_ref=src,
            dst_ref=dst,
            send_sem=self.send_sem.at[n],
            recv_sem=self.recv_sem.at[n],
            device_id=where,
            device_id_type=MESH,
        )

    def start(self, src, dst, where):
        copy = self.make(src, dst, where)
        copy.start()
        return copy


def slab_device(step):
    d = lax.axis_index("dev")
    return (lax.axis_index("grp"), (d + step + 16) % 16)


def all_partners():
    x, y, z, core = coords()
    found = [device(x, y, z, 1 - core)]
    for axis in ("x", "y", "z"):
        for k in (1, 2, 3):
            found.append(device(*on_axis(axis, x, y, z, k), core))
    g, d = lax.axis_index("grp"), lax.axis_index("dev")
    found.append((g, (d + 15 + 2 * core) % 16))
    found += [device(x, (y + k) % 4, (z + 2) % 4, core) for k in (1, 2, 3)]
    return found


def dot(left, right, dims=((1,), (0,))):
    return lax.dot_general(left, right, (dims, ((), ())), preferred_element_type=F32)


def smooth(gas_ref, halo_ref, sm, layers):
    for k in range(3):
        for i in layers:
            lower = halo_ref[k, 1] if i == 0 else gas_ref[k, i - 1]
            upper = halo_ref[k, 2] if i == 7 else gas_ref[k, i + 1]
            sm[k, pl.ds(i * 128, 128), :] = 0.5 * gas_ref[k, i] + 0.25 * (lower + upper)


def drag(t, pv_ref, cell_ref, fill_ref, rate_ref, mass_ref, pout_ref, sm, cpair, hs):
    lane = lax.broadcasted_iota(jnp.int32, (128, 128), 1)
    slots = lax.broadcasted_iota(jnp.int32, (64, 128), 0)
    left_lanes = lane < 64
    cols = (pl.ds(t * 128, 128), pl.ds(t * 128 + 512, 128))
    index = jnp.concatenate([cell_ref[:, c] for c in cols], axis=0).T
    cpair[cols[0], :] = index
    for k in range(3):
        found = [
            jnp.take_along_axis(sm[k, c, :], index, axis=1, mode="promise_in_bounds") for c in cols
        ]
        gas_at = jnp.where(left_lanes, found[0], found[1]).T
        hands = []
        for side, c in enumerate(cols):
            velocity, rate = pv_ref[k, :, c], rate_ref[:, c]
            live = slots < fill_ref[:, c]
            relaxed = (velocity + rate * gas_at[64 * side : 64 * side + 64]) / (1.0 + rate)
            pout_ref[k, :, c] = jnp.where(live, relaxed, velocity)
            hands.append(jnp.where(live, mass_ref[:, c] * (velocity - relaxed), 0.0))
        handed = jnp.concatenate(hands, axis=0).T
        coarse = handed.astype(BF16).astype(F32)
        fine = handed - coarse
        base = t * 2048
        for first, part in ((0, coarse), (8, fine)):
            hs[pl.ds(base + first + k, 128, stride=16), :] = jnp.where(left_lanes, part, 0.0)
            hs[pl.ds(base + first + 3 + k, 128, stride=16), :] = jnp.where(left_lanes, 0.0, part)
    zero = jnp.zeros((128, 128), F32)
    for row in (6, 7, 14, 15):
        hs[pl.ds(t * 2048 + row, 128, stride=16), :] = zero


def deposit(t, cpair, hs, ob, dep):
    cells = lax.broadcasted_iota(jnp.int32, (128, 128), 0)
    upper_rows = lax.broadcasted_iota(jnp.int32, (32, 128), 0) < 16

    def several(step, carry):
        for u in range(32):
            b = t * 64 + step * 32 + u
            values = hs[pl.ds(pl.multiple_of(b * 32, 32), 32), :]
            left = jnp.concatenate(
                [jnp.where(upper_rows, values, 0.0), jnp.where(upper_rows, 0.0, values)], axis=1
            ).astype(BF16)
            hot = jnp.concatenate(
                [
                    (cells == cpair[pl.ds(2 * b + i, 1), :]).astype(F32).astype(BF16)
                    for i in range(2)
                ],
                axis=1,
            )
            out = dot(left, hot, ((1,), (1,)))
            ob[pl.ds(pl.multiple_of(b * 16, 16), 16), :] = jnp.concatenate(
                [out[0:8] + out[8:16], out[16:24] + out[24:32]], axis=0
            )
        return carry

    lax.fori_loop(0, 2, several, 0)
    for k in range(3):
        for side in range(2):
            dep[k, pl.ds(512 * side + 128 * t, 128), :] = ob[
                pl.ds(1024 * t + 3 * side + k, 128, stride=8), :
            ]


def gas_second(gas_ref, halo_ref, dep_ref, dep_halo, gout_ref, mid):
    row = lax.broadcasted_iota(jnp.int32, (128, 128), 0)
    col = lax.broadcasted_iota(jnp.int32, (128, 128), 1)

    def walls(f):
        return (
            jnp.where(row == 0, 0.0, pltpu.roll(f, 1, 0))
            + jnp.where(row == 127, 0.0, pltpu.roll(f, 127, 0))
            + jnp.where(col == 0, 0.0, pltpu.roll(f, 1, 1))
            + jnp.where(col == 127, 0.0, pltpu.roll(f, 127, 1))
        )

    def component(k, c):
        def gas(i):
            if i < 0:
                return halo_ref[k, i + 2]
            return gas_ref[k, i] if i < 8 else halo_ref[k, i - 6]

        def dep(i):
            if i < 0:
                return dep_halo[0, k, i + 2].astype(F32)
            if i < 8:
                return dep_ref[k, pl.ds(i * 128, 128), :]
            return dep_halo[1, k, i - 8].astype(F32)

        for i in range(-1, 9):
            f = gas(i)
            step = f + KAPPA * (gas(i - 1) + gas(i + 1) + walls(f) - 6.0 * f)
            mid[i + 1] = step + 0.5 * dep(i) + 0.25 * (dep(i - 1) + dep(i + 1))
        for i in range(8):
            f = mid[i + 1]
            gout_ref[k, i] = f + KAPPA * (mid[i] + mid[i + 2] + walls(f) - 6.0 * f)
        return c

    lax.fori_loop(0, 3, component, 0)


def step_kernel(
    ids_ref, w_in, xy_in, gas_in, pv_in, cell_in, fill_in, rate_in, mass_in,
    flat, gout_ref, pout_ref,
    ids, w_ref, xy_ref, gas_ref, pv_ref, cell_ref, fill_ref, rate_ref, mass_ref,
    in_sem, out_sem,
    wall, halo, cnt, cnt_in, sm, cpair, hs, ob, dep, dep_out, dep_halo, mid,
    a1, s1, a2, s2, b2, b1, err, w3f, w3, scale,
    grad, pair_sum, in1_x, in1_y, in1_z, sum1_x, sum1_y, sum1_z, in2_x, in2_y, in2_z,
    sum1_v, in2_v,
    sum2_x, sum2_y, sum2_z, in3_x, in3_y, in3_z, fin, spread_out, send_sem, recv_sem,
):
    x, y, z, core = coords()
    zh, zl = z // 2, z % 2
    g, d = lax.axis_index("grp"), lax.axis_index("dev")
    sibling = device(x, y, z, 1 - core)
    evo = evolves()
    net = Copies(send_sem, recv_sem)
    sent = []

    def push(src, dst, where):
        copy = net.start(src, dst, where)
        sent.append(copy)
        return copy

    def when_evolving(*steps):
        @pl.when(evo)
        def _():
            for step in steps:
                step()

    partners = all_partners()
    barrier = pltpu.get_barrier_semaphore()
    for partner in partners:
        pl.semaphore_signal(barrier, inc=1, device_id=partner, device_id_type=MESH)
    pairs_in = (
        (w_in, w_ref.at[pl.ds(0, 640)]), (gas_in, gas_ref), (cell_in, cell_ref), (pv_in, pv_ref), (rate_in, rate_ref),
        (mass_in, mass_ref), (fill_in, fill_ref), (xy_in, xy_ref),
    )
    loads = [
        pltpu.make_async_copy(src, dst, in_sem.at[i]) for i, (src, dst) in enumerate(pairs_in)
    ]
    for load in loads:
        load.start()
    for n in range(BLK):
        ids[pl.ds(n, 1), :] = jnp.full((1, 128), ids_ref[n], jnp.int32)
    gas_same = pltpu.make_async_copy(gas_ref, gout_ref, out_sem.at[0])
    parcel_same = pltpu.make_async_copy(pv_ref, pout_ref, out_sem.at[1])

    loads[0].wait()
    for j in range(8):
        spread = w_ref[pl.ds(j, PIECE, stride=8), :]
        mixed = jnp.concatenate([spread[:32], w_ref[pl.ds(256 + 48 * j, 48), :]], axis=0)
        last = w_ref[pl.ds(PIECE * j, PIECE), :]
        mine_j = jnp.where(d == 15, last, jnp.where(d == 14, mixed, spread))
        wall[j, pl.ds(pl.multiple_of(d * PIECE, 16), PIECE), :] = mine_j.astype(BF16)
    lanes = lax.broadcasted_iota(jnp.int32, (BLK, 128), 1)
    mine = (ids[...] == lanes).astype(F32)
    cnt[0] = jnp.broadcast_to(jnp.sum(mine, axis=0, keepdims=True), (8, 128))
    pl.semaphore_wait(barrier, len(partners))

    def shard(px, pz, pc, j0, jn):
        first = pl.multiple_of((px * 4 + (pz % 2) * 2 + pc) * PIECE, 16)
        return wall.at[pl.ds(j0, jn), pl.ds(first, PIECE)]

    def give(px, pz, j0, jn, where):
        piece = shard(px, pz, core, j0, jn)
        return push(piece, piece, where)

    half = (y % 2) * 4
    zm = z + 1 - 2 * zl
    count_copy = push(cnt.at[0], cnt_in.at[0], sibling)
    from_z = [
        give(x, z, 0, 4, device(x, y, (z + 1) % 4, core)),
        give(x, z, 4, 4, device(x, y, (z + 3) % 4, core)),
    ]
    near_x = [give(x, z, half, 4, device((x + k) % 4, y, z, core)) for k in (1, 2, 3)]
    over = [give(x, z, 0, 8, sibling)]
    low = net.make(gas_ref.at[:, pl.ds(6, 2)], halo.at[:, pl.ds(0, 2)], slab_device(1))
    high = net.make(gas_ref.at[:, pl.ds(0, 2)], halo.at[:, pl.ds(2, 2)], slab_device(-1))

    def parcels(t):
        drag(t, pv_ref, cell_ref, fill_ref, rate_ref, mass_ref, pout_ref, sm, cpair, hs)

    for load in loads[1:]:
        load.wait()

    @pl.when(jnp.logical_not(evo))
    def _():
        gas_same.start()
        parcel_same.start()

    when_evolving(
        lambda: smooth(gas_ref, halo, sm, range(1, 7)),
        lambda: parcels(1),
        lambda: parcels(2),
    )
    count_copy.wait_recv()
    cnt[1] = cnt[0] + cnt_in[0]

    def count_send(axis, at, slot):
        return [
            push(cnt.at[at], cnt_in.at[slot + k], device(*on_axis(axis, x, y, z, k + 1), core))
            for k in range(3)
        ]

    def count_add(copies, at, slot):
        for copy in copies:
            copy.wait_recv()
        cnt[at + 1] = cnt[at] + cnt_in[slot] + cnt_in[slot + 1] + cnt_in[slot + 2]

    counting = count_send("y", 1, 1)
    for copy in from_z:
        copy.wait_recv()
    far_x = [give(x, zm, half, 4, device((x + k) % 4, y, z, core)) for k in (1, 2, 3)]
    over.append(give(x, zm, 0, 8, sibling))
    when_evolving(lambda: deposit(1, cpair, hs, ob, dep))

    up, down = device(x, (y + 1) % 4, z, core), device(x, (y + 3) % 4, z, core)
    from_y = []
    for pz, copies in ((z, near_x), (zm, far_x)):
        for k, copy in zip((1, 2, 3), copies):
            copy.wait_recv()
            px = (x + 4 - k) % 4
            from_y.append((px, pz, 0, give(px, pz, half, 2, up)))
            from_y.append((px, pz, 2, give(px, pz, half + 2, 2, down)))
            over.append(give(px, pz, half, 4, sibling))
        if pz is z:
            count_add(counting, 1, 1)
            counting = count_send("z", 2, 4)
            when_evolving(lambda: deposit(2, cpair, hs, ob, dep))
    count_add(counting, 2, 4)
    counting = count_send("x", 3, 7)
    other = 4 - half
    for px, pz, q, copy in from_y:
        copy.wait_recv()
        over.append(give(px, pz, other + q, 2, sibling))
    for copy in over:
        copy.wait_recv()

    when_evolving(low.start, high.start)
    count_add(counting, 3, 7)

    inverse = 1.0 / jnp.maximum(cnt[4, 0:1, :], 1.0)
    picked = jnp.where(ids[...] == lanes, inverse, 0.0)
    per_block = jnp.broadcast_to(jnp.sum(picked, axis=1, keepdims=True), (BLK, 128))
    for n in range(BLK):
        scale[pl.ds(16 * n, 16), :] = jnp.broadcast_to(per_block[n : n + 1], (16, 128))
    for j in range(8):
        w3[pl.ds(48 * j, 48), :] = wall[j, pl.ds(1152, 48), :]
        w3[pl.ds(384 + PIECE * j, PIECE), :] = wall[j, pl.ds(1200, PIECE), :]

    def columns(j, first, rows):
        return jnp.concatenate([wall[2 * j + i, pl.ds(first, rows), :] for i in range(2)], axis=1)

    def activate(pre, act, slope, j):
        s = 0.5 * jnp.tanh(0.5 * pre) + 0.5
        value = pre * s
        act[j] = value.astype(BF16)
        slope[j] = s + value * (1.0 - s)

    for j in range(4):
        activate(dot(xy_ref[:, 0:128], columns(j, 0, 128)), a1, s1, j)
    acts = jnp.concatenate([a1[i] for i in range(4)], axis=1)
    for j in range(4):
        activate(dot(acts, columns(j, 128, 1024)), a2, s2, j)
    acts = jnp.concatenate([a2[i] for i in range(4)], axis=1)
    predicted = dot(acts, w3[...])
    err[...] = ((predicted - xy_ref[:, 128:256].astype(F32)) * scale[...]).astype(BF16)

    for j in range(4):
        part = pl.ds(256 * j, 256)
        b2[j] = (dot(err[...], w3[part, :], ((1,), (1,))) * s2[j]).astype(BF16)
    for j in range(4):
        w3f[pl.ds(256 * j, 256), :] = dot(a2[j], err[...], ((0,), (0,)))
    for j in range(8):
        grad[j // 4, j % 4, pl.ds(1152, 48), :] = w3f[pl.ds(48 * j, 48), :]
        grad[j // 4, j % 4, pl.ds(1200, PIECE), :] = w3f[pl.ds(384 + PIECE * j, PIECE), :]

    def grad_second(i):
        for j in range(4):
            piece = dot(a1[i], b2[j], ((0,), (0,)))
            for e in range(2):
                n = 2 * j + e
                grad[n // 4, n % 4, pl.ds(128 + 256 * i, 256), :] = piece[:, 128 * e : 128 * e + 128]

    def back_first():
        backs = jnp.concatenate([b2[j] for j in range(4)], axis=1)
        for i in range(4):
            h0 = 128 + 256 * i
            rows = jnp.concatenate([wall[j, pl.ds(h0, 256), :] for j in range(8)], axis=1)
            b1[i] = (dot(backs, rows, ((1,), (1,))) * s1[i]).astype(BF16)

    def y_rows(px):
        return pl.ds(48, 32) if px % 2 else pl.ds(56, 24)

    def z_rows(px):
        return pl.ds(24, 24 if px % 2 else 32)

    pairs = {}

    def pair_start(px):
        pairs[px] = [
            push(
                grad.at[:, :, pl.ds(pl.multiple_of((px * 4 + q * 2 + 1 - core) * PIECE, 8), PIECE)],
                pair_sum.at[px, q],
                sibling,
            )
            for q in range(2)
        ]

    first_x = {}
    first_y, first_z = {}, {}

    def to_x(px, src, slots, sems):
        k = (px - x + 4) % 4
        slot = jnp.maximum(k - 1, 0)
        n = net.count
        net.count += 1
        copy = pltpu.make_async_remote_copy(
            src_ref=src,
            dst_ref=slots.at[slot],
            send_sem=send_sem.at[n],
            recv_sem=sems.at[slot],
            device_id=device(px, y, z, core),
            device_id_type=MESH,
        )

        @pl.when(k > 0)
        def _():
            copy.start()

        return copy

    def from_x(slots, sems):
        for k in range(3):
            pltpu.make_async_remote_copy(
                src_ref=slots.at[k],
                dst_ref=slots.at[k],
                send_sem=send_sem.at[0],
                recv_sem=sems.at[k],
                device_id=sibling,
                device_id_type=MESH,
            ).wait_recv()

    def pair_done(px):
        for q, copy in enumerate(pairs[px]):
            copy.wait_recv()
            own = pl.ds(pl.multiple_of((px * 4 + q * 2 + core) * PIECE, 8), PIECE)
            pair_sum[px, q] = pair_sum[px, q] + grad[:, :, own, :]
        first_x[px] = to_x(px, pair_sum.at[px, :, :, :, pl.ds(0, 24)], in1_x, recv_x)

        for k in (1, 2, 3):
            ny = (y + k) % 4
            first_y.setdefault(px, []).append(
                push(
                    pair_sum.at[px, :, :, ny, y_rows(px)],
                    in1_y.at[k - 1, px, :, :, pl.ds(0, y_rows(px).size)],
                    device(x, ny, z, core),
                )
            )
        for k in (1, 2, 3):
            nz = (z + k) % 4
            first_z.setdefault(px, []).append(
                push(
                    pair_sum.at[px, nz % 2, nz // 2, :, z_rows(px)],
                    in1_z.at[k - 1, px, :, pl.ds(0, z_rows(px).size)],
                    device(x, y, nz, core),
                )
            )

    second_y, second_v, sent_z = {}, {}, {}

    def second_phase(px):
        for copy in first_z[px]:
            copy.wait_recv()
        zn = z_rows(px).size
        total = pair_sum[px, zl, zh, :, z_rows(px), :]
        for k in range(3):
            total = total + in1_z[k, px, :, pl.ds(0, zn), :]
        sum1_z[px] = total[:, :24]
        sent_z[px] = to_x(px, sum1_z.at[px], in2_z, recv_z)
        if zn > 24:
            sum1_v[px // 2] = total[:, 24:]
            second_v[px] = [
                push(
                    sum1_v.at[px // 2, (y + k) % 4],
                    in2_v.at[k - 1, px // 2],
                    device(x, (y + k) % 4, z, core),
                )
                for k in (1, 2, 3)
            ]
        for copy in first_y[px]:
            copy.wait_recv()
        yn = y_rows(px).size
        total = pair_sum[px, :, :, y, y_rows(px), :]
        for k in range(3):
            total = total + in1_y[k, px, :, :, pl.ds(0, yn), :]
        sum1_y[px, :, :, pl.ds(0, yn), :] = total
        second_y[px] = []
        for k in (1, 2, 3):
            nz = (z + k) % 4
            second_y[px].append(
                push(
                    sum1_y.at[px, nz % 2, nz // 2, pl.ds(0, yn)],
                    in2_y.at[k - 1, px, pl.ds(0, yn)],
                    device(x, y, nz, core),
                )
            )

    def third_phase(px):
        for copy in second_y[px] + second_v.get(px, []):
            copy.wait_recv()
        yn = y_rows(px).size
        rows = pl.ds(0, yn)
        sum2_y[px, pl.ds(32 - yn, yn), :] = (
            sum1_y[px, zl, zh, rows, :]
            + in2_y[0, px, rows, :] + in2_y[1, px, rows, :] + in2_y[2, px, rows, :]
        )
        if yn == 24:
            e = px // 2
            sum2_y[px, pl.ds(0, 8), :] = sum1_v[e, y] + in2_v[0, e] + in2_v[1, e] + in2_v[2, e]
        sent_y[px] = to_x(px, sum2_y.at[px], in3_y, recv_y)

    sent_y = {}
    recv_x = recv_sem.at[pl.ds(RECV_X, 3)]
    recv_z = recv_sem.at[pl.ds(RECV_X + 3, 3)]
    recv_y = recv_sem.at[pl.ds(RECV_X + 6, 3)]
    grad_second(3)
    pair_start(3)
    grad_second(2)
    pair_start(2)
    grad_second(1)
    grad_second(0)
    pair_start(1)
    pair_done(3)
    pair_done(2)
    back_first()
    pair_done(1)
    for j in range(4):
        piece = dot(xy_ref[:, 0:128], b1[j], ((0,), (0,)))
        for e in range(2):
            n = 2 * j + e
            grad[n // 4, n % 4, pl.ds(0, 128), :] = piece[:, 128 * e : 128 * e + 128]
    pair_start(0)
    pair_done(0)

    def send_deposit():
        for k in range(3):
            for i in range(2):
                dep_out[0, k, i] = dep[k, pl.ds(128 * (6 + i), 128), :].astype(BF16)
                dep_out[1, k, i] = dep[k, pl.ds(128 * i, 128), :].astype(BF16)
        dep_low.start()
        dep_high.start()

    dep_low = net.make(dep_out.at[0], dep_halo.at[0], slab_device(1))
    dep_high = net.make(dep_out.at[1], dep_halo.at[1], slab_device(-1))
    when_evolving(
        low.wait,
        high.wait,
        lambda: smooth(gas_ref, halo, sm, (0, 7)),
        lambda: parcels(0),
        lambda: parcels(3),
        lambda: deposit(0, cpair, hs, ob, dep),
    )
    second_phase(3)
    second_phase(2)
    when_evolving(lambda: deposit(3, cpair, hs, ob, dep), send_deposit)


    from_x(in1_x, recv_x)
    sum1_x[...] = pair_sum[x, :, :, :, pl.ds(0, 24), :] + in1_x[0] + in1_x[1] + in1_x[2]
    second_x = [
        push(sum1_x.at[:, :, (y + k) % 4], in2_x.at[k - 1], device(x, (y + k) % 4, z, core))
        for k in (1, 2, 3)
    ]
    second_phase(1)
    second_phase(0)
    for copy in second_x:
        copy.wait_recv()
    sum2_x[...] = sum1_x[:, :, y] + in2_x[0] + in2_x[1] + in2_x[2]
    third_x = []
    for k in (1, 2, 3):
        nz = (z + k) % 4
        third_x.append(push(sum2_x.at[nz % 2, nz // 2], in3_x.at[k - 1], device(x, y, nz, core)))
    from_x(in2_z, recv_z)
    sum2_z[...] = sum1_z[x] + in2_z[0] + in2_z[1] + in2_z[2]
    third_z = [
        push(sum2_z.at[(y + k) % 4], in3_z.at[k - 1], device(x, (y + k) % 4, z, core))
        for k in (1, 2, 3)
    ]
    for px in (3, 2, 1, 0):
        third_phase(px)
    for copy in third_x + third_z:
        copy.wait_recv()
    fin[g, pl.ds(0, 24), :] = sum2_x[zl, zh] + in3_x[0] + in3_x[1] + in3_x[2]
    fin[g, pl.ds(24, 24), :] = sum2_z[y] + in3_z[0] + in3_z[1] + in3_z[2]

    def across_groups(rows):
        return [
            push(fin.at[g, rows], fin.at[g, rows], ((g + k) % 8, d)) for k in range(1, 8)
        ]

    from_x(in3_y, recv_y)
    fin[g, pl.ds(48, 32), :] = sum2_y[x] + in3_y[0] + in3_y[1] + in3_y[2]
    across = across_groups(pl.ds(0, 80))
    when_evolving(
        dep_low.wait,
        dep_high.wait,
        lambda: gas_second(gas_ref, halo, dep, dep_halo, gout_ref, mid),
    )

    for copy in across:
        copy.wait_recv()

    @pl.when(d < 14)
    def _():
        for j in range(8):
            spread_out[pl.ds(j, PIECE, stride=8), :] = fin[j]
        flat[...] = spread_out[pl.ds(0, 640), :]

    @pl.when(d == 14)
    def _():
        for j in range(8):
            flat[pl.ds(j, 32, stride=8), :] = fin[j, :32]
            flat[pl.ds(256 + 48 * j, 48), :] = fin[j, 32:]

    @pl.when(d == 15)
    def _():
        for j in range(8):
            flat[pl.ds(PIECE * j, PIECE), :] = fin[j]

    @pl.when(jnp.logical_not(evo))
    def _():
        gas_same.wait()
        parcel_same.wait()

    for copy in sent:
        copy.wait_send()
    for px in range(4):

        @pl.when(px != x)
        def _():
            first_x[px].wait_send()
            sent_z[px].wait_send()
            sent_y[px].wait_send()


def finish_kernel(
    grad, w, m, v, gas, parcels,
    w_out, m_out, v_out, gas_out, parcel_out,
    w_new, m_new, v_new, out_sem,
):
    results = (
        (gas, gas_out), (parcels, parcel_out), (m_new, m_out), (v_new, v_out), (w_new, w_out),
    )
    stores = [pltpu.make_async_copy(a, b, out_sem.at[i]) for i, (a, b) in enumerate(results)]
    for store in stores[:2]:
        store.start()
    gradient = grad[...]
    first_new = BETA_ONE * m[...] + (1.0 - BETA_ONE) * gradient
    second_new = BETA_TWO * v[...] + (1.0 - BETA_TWO) * gradient * gradient
    m_new[...] = first_new
    v_new[...] = second_new
    first_hat = first_new / (1.0 - BETA_ONE**ADAM_STEP)
    second_hat = second_new / (1.0 - BETA_TWO**ADAM_STEP)
    w_new[...] = w[...] - LEARN_RATE * first_hat / (jnp.sqrt(second_hat) + ADAM_EPS)
    for store in stores[2:]:
        store.start()
    for store in stores:
        store.wait()


def anywhere(count):
    return [pl.BlockSpec(memory_space=pl.ANY)] * count


def shards(
    gas_velocity, parcel_velocity, parcel_cell, block_fill, relax_rate, parcel_mass,
    sample_blocks, learner_ids, master_weights, first_moment, second_moment,
):
    shape = jax.ShapeDtypeStruct

    def buf(*dims, dtype=F32):
        return pltpu.VMEM(dims, dtype)

    scratch = [
        buf(BLK, 128, dtype=jnp.int32),
        buf(648, 128),
        buf(ROWS, 256, dtype=BF16),
        buf(3, 8, 128, 128),
        buf(3, 64, 1024),
        buf(64, 1024, dtype=jnp.int32),
        buf(1, 1024, dtype=jnp.int32),
        buf(64, 1024),
        buf(64, 1024),
        pltpu.SemaphoreType.DMA((8,)),
        pltpu.SemaphoreType.DMA((2,)),
        buf(8, 1280, 128, dtype=BF16),
        buf(3, 4, 128, 128),
        buf(5, 8, 128),
        buf(10, 8, 128),
        buf(3, 1024, 128),
        buf(512, 128, dtype=jnp.int32),
        buf(8208, 128),
        buf(4112, 128),
        buf(3, 1024, 128),
        buf(2, 3, 2, 128, 128, dtype=BF16),
        buf(2, 3, 2, 128, 128, dtype=BF16),
        buf(10, 128, 128),
        buf(4, ROWS, 256, dtype=BF16),
        buf(4, ROWS, 256),
        buf(4, ROWS, 256, dtype=BF16),
        buf(4, ROWS, 256),
        buf(4, ROWS, 256, dtype=BF16),
        buf(4, ROWS, 256, dtype=BF16),
        buf(ROWS, 128, dtype=BF16),
        buf(1024, 128),
        buf(1024, 128, dtype=BF16),
        buf(ROWS, 128),
        buf(2, 4, 1280, 128),
        buf(4, 2, 2, 4, PIECE, 128),
        buf(3, 2, 2, 4, 24, 128),
        buf(3, 4, 2, 2, 32, 128),
        buf(3, 4, 4, 32, 128),
        buf(2, 2, 4, 24, 128),
        buf(4, 2, 2, 32, 128),
        buf(4, 4, 24, 128),
        buf(3, 2, 2, 24, 128),
        buf(3, 4, 32, 128),
        buf(3, 4, 24, 128),
        buf(2, 4, 8, 128),
        buf(3, 2, 8, 128),
        buf(2, 2, 24, 128),
        buf(4, 32, 128),
        buf(4, 24, 128),
        buf(3, 24, 128),
        buf(3, 32, 128),
        buf(3, 24, 128),
        buf(8, PIECE, 128),
        buf(648, 128),
        pltpu.SemaphoreType.DMA((RECV_X,)),
        pltpu.SemaphoreType.DMA((RECV_X + 9,)),
    ]
    grads, gas_out, parcels = pl.pallas_call(
        step_kernel,
        name="step",
        out_shape=(
            buf(640, 128),
            buf(3, 8, 128, 128),
            buf(3, 64, 1024),
        ),
        in_specs=[pl.BlockSpec(memory_space=pltpu.SMEM)]
        + [pl.BlockSpec(memory_space=pltpu.HBM)] * 8,
        out_specs=tuple([pl.BlockSpec(memory_space=pltpu.VMEM)] * 3),
        scratch_shapes=scratch,
        compiler_params=pltpu.CompilerParams(
            collective_id=0, has_side_effects=True, vmem_limit_bytes=VMEM_LIMIT
        ),
    )(
        *[
            pltpu.with_memory_space_constraint(array, pltpu.HBM)
            for array in (
                learner_ids, master_weights, sample_blocks.reshape(ROWS, 256), gas_velocity[0],
                parcel_velocity[0], parcel_cell[0], block_fill, relax_rate[0], parcel_mass[0],
            )
        ],
    )
    state = shape((640, 128), F32)
    master_out, first_out, second_out, gas_out, parcels = pl.pallas_call(
        finish_kernel,
        name="finish",
        out_shape=(state, state, state, shape(gas_out.shape, F32), shape(parcels.shape, F32)),
        in_specs=[pl.BlockSpec(memory_space=pltpu.VMEM)] * 6,
        out_specs=tuple(anywhere(5)),
        scratch_shapes=[buf(640, 128) for _ in range(3)] + [pltpu.SemaphoreType.DMA((5,))],
        compiler_params=pltpu.CompilerParams(vmem_limit_bytes=16 * 1024 * 1024),
    )(grads, master_weights, first_moment, second_moment, gas_out, parcels)
    return gas_out[None], parcels[None], master_out, first_out, second_out


def solution(mesh):
    placed = (
        P("grp", None, "dev", None, None),
        P("grp", None, None, "dev"),
        P("grp", None, "dev"),
        P("grp", "dev"),
        P("grp", None, "dev"),
        P("grp", None, "dev"),
        P(("grp", "dev"), None, None),
        P(("grp", "dev")),
        P("dev", None),
        P("dev", None),
        P("dev", None),
    )
    return jax.shard_map(
        shards,
        mesh=mesh,
        in_specs=placed,
        out_specs=(
            P("grp", None, "dev", None, None),
            P("grp", None, None, "dev"),
            P("dev", None),
            P("dev", None),
            P("dev", None),
        ),
        check_vma=False,
    )
```
